32 devices in a mesh: leaf: 16 (over z, y, core), blk: 2 (over x).
Axes of the slice: x: 2, y: 2, z: 4, core: 2. Of those that a mesh axis runs over, the one named last changes fastest.
Arguments:
- sample: float32 [3, 28672, 512], P(None, ('leaf', 'blk')), may hold values from -6 to 6
- probes: float32 [3, 28672, 512], P(None, ('leaf', 'blk')), may hold values from -0.09375 to 0.09375
- skeleton_rows: int32 [14, 128], replicated, may hold values from 0 to 14335, as said below
Outputs:
- interpolants: float32 [3, 28672, 128], P(None, ('leaf', 'blk'))
- coupling: float32 [3, 16, 128, 128], P(None, 'leaf')
The draws below stay inside these ranges and needn't reach their ends.
Inputs may be any that keep to these rules, and one draw needn't show every extreme that they name: `skeleton_rows`: list 2^(l+1) - 2 + j belongs to node j of level l; it holds 128 distinct row indices counted from the node's first row, below 28672 / 2^(l+1); its first entry is always 0 and its last entry is always the node's last row.
All inputs are finite; a program needn't handle non-finite values.
Results may differ from the reference program's by a relative error of at most 0.0003.
Values sent between devices are 32-bit elements; how exact they have to be, the bound alone decides.
No kernel may reach another device: no remote copies, remote signals or barrier semaphores. Data moves between devices by JAX's collectives and lax.ppermute only.
A program may use at most 128 MiB of HBM per device.

```python
import jax
import jax.numpy as jnp
from jax import lax

SAMPLES = 512
SKEL = 128
LEVELS = 3
GROUPS = 16
NROWS = 28672


def draw_skeleton_rows(key, part):
    key = jax.random.fold_in(key, 7)
    listed = []
    for level_id in range(LEVELS):
        nodes = 2 ** (level_id + 1)
        node_rows = NROWS // nodes
        for node_id in range(nodes):
            sub_key = jax.random.fold_in(key, nodes - 2 + node_id)
            chosen = (jax.random.permutation(sub_key, node_rows - 2)[:SKEL - 2] + 1).astype(jnp.int32)
            listed.append(jnp.concatenate([jnp.zeros((1,), jnp.int32), chosen, jnp.full((1,), node_rows - 1, jnp.int32)]))
    return jnp.stack(listed)


def shard_levels(key, dims, pieces, least, top_value):
    def one(position, shards_of):
        steps = jax.random.uniform(jax.random.fold_in(jax.random.fold_in(key, 6), position), (shards_of,), jnp.float32, least / len(pieces), top_value / len(pieces))
        return jnp.repeat(jnp.exp(steps), dims[position] // shards_of).reshape((-1,) + (1,) * (len(dims) - position - 1))

    gain = one(*pieces[0])
    for cut in pieces[1:]:
        gain = gain * one(*cut)
    return gain


def gaussian(key, shape, deviation, bound, cuts=(), kind=jnp.bfloat16):
    factor_of = shard_levels(key, shape, cuts, -0.22, 0.18) if cuts else 1.0
    array = jax.random.normal(key, shape, jnp.float32) * deviation * factor_of
    return jnp.minimum(jnp.maximum(array, -bound), bound).astype(kind)


def setup_inputs(seed: int = 0) -> dict:
    key_of = jax.random.split(jax.random.key(seed), 4)
    sample = gaussian(key_of[0], (LEVELS, NROWS, SAMPLES), 1.0, 6.0, ((1, 32),), jnp.float32)
    probes = gaussian(key_of[1], (LEVELS, NROWS, SAMPLES), (NROWS // 8) ** -0.5, 0.09375, ((1, 32),), jnp.float32)
    skeleton_rows = draw_skeleton_rows(jax.random.fold_in(key_of[3], 71), 0)
    return {"sample": sample, "probes": probes, "skeleton_rows": skeleton_rows}


ridge_term = 0.05

def chol_solve(gram_matrix, right_side):
    factor = jnp.linalg.cholesky(gram_matrix)
    return jax.scipy.linalg.cho_solve((factor, True), right_side)

def exact_sum(form, left_side, right_side):
    return jnp.einsum(form, left_side, right_side, precision=lax.Precision.HIGHEST)

def pick_rows(block_rows, indices):
    return block_rows[indices]

def reference(sample, probes, skeleton_rows):
    row_total = sample.shape[1]
    identity = jnp.eye(SKEL, dtype=jnp.float32)
    bases = []
    couplings = []
    outputs = []
    for level_id in range(LEVELS):
        nodes = 2 ** (level_id + 1)
        node_rows = row_total // nodes
        corrected = sample[level_id].reshape(nodes, node_rows, SAMPLES)
        tests = probes[level_id].reshape(nodes, node_rows, SAMPLES)
        for coarse in range(level_id):
            coarse_nodes = 2 ** (coarse + 1)
            inner = nodes // coarse_nodes
            basis_here = bases[coarse].reshape(nodes, node_rows, SKEL)
            per_node = exact_sum('nrk,nrp->nkp', basis_here, tests)
            parity_slots = per_node.reshape(coarse_nodes, inner // 2, 2, SKEL, SAMPLES).sum(axis=1)
            swapped = parity_slots.reshape(coarse_nodes // 2, 2, 2, SKEL, SAMPLES)[:, ::-1]
            swapped = swapped.reshape(coarse_nodes, 2, SKEL, SAMPLES)
            owner = jnp.arange(nodes, dtype=jnp.int32) // inner
            parity = jnp.arange(nodes, dtype=jnp.int32) % 2
            chosen = swapped[owner, 1 - parity]
            mapped = exact_sum('nkj,njp->nkp', couplings[coarse][owner], chosen)
            corrected = corrected - exact_sum('nrk,nkp->nrp', basis_here, mapped)
        picked = skeleton_rows[nodes - 2:2 * nodes - 2]
        skeleton = jax.vmap(pick_rows)(corrected, picked)
        gram_matrix = exact_sum('nkp,njp->nkj', skeleton, skeleton) / SAMPLES + ridge_term * identity
        projected = exact_sum('nrp,nkp->nkr', corrected, skeleton) / SAMPLES
        basis_now = jnp.swapaxes(jax.vmap(chol_solve)(gram_matrix, projected), 1, 2)
        bases.append(basis_now.reshape(row_total, SKEL))
        moment = exact_sum('nrk,nrp->nkp', basis_now, tests)
        partner = moment.reshape(nodes // 2, 2, SKEL, SAMPLES)[:, ::-1].reshape(nodes, SKEL, SAMPLES)
        spread = exact_sum('nkp,njp->nkj', partner, partner) + ridge_term * identity
        cross = exact_sum('nkp,njp->nkj', partner, skeleton)
        coupled = jnp.swapaxes(jax.vmap(chol_solve)(spread, cross), 1, 2)
        couplings.append(coupled)
        outputs.append(jnp.repeat(coupled, GROUPS // nodes, axis=0))
    return (jnp.stack(bases), jnp.stack(outputs))
```

```python
import functools
import math

import jax
import jax.numpy as jnp
from jax import lax
from jax.experimental import pallas as pl
from jax.experimental.pallas import tpu as pltpu
from jax.sharding import PartitionSpec as P

ridge_term = 0.05
AXES = ("n0", "n1", "n2", "mid", "core", "blk")
TILE = 8
WIDTH = 128
VMEM = pl.BlockSpec(memory_space=pltpu.VMEM)
SMEM = pl.BlockSpec(memory_space=pltpu.SMEM)
ANY = pl.BlockSpec(memory_space=pltpu.HBM)
BIG = pltpu.CompilerParams(vmem_limit_bytes=49 * 1024 * 1024)


def arr(*shape):
    return jax.ShapeDtypeStruct(shape, jnp.float32)


def cost(flops, bytes_accessed):
    return pl.CostEstimate(flops=flops, bytes_accessed=bytes_accessed, transcendentals=0)


def split(block):
    high = block.astype(jnp.bfloat16)
    low = (block - high.astype(jnp.float32)).astype(jnp.bfloat16)
    return high, low


def plain_dot(left_side, right_side, left_dim, right_dim):
    return lax.dot_general(
        left_side, right_side, (((left_dim,), (right_dim,)), ((), ())), preferred_element_type=jnp.float32
    )


def dot3(left_side, right_side, left_dim=1, right_dim=0):
    left_high, left_low = split(left_side)
    right_high, right_low = split(right_side)
    return (
        plain_dot(left_high, right_high, left_dim, right_dim)
        + plain_dot(left_high, right_low, left_dim, right_dim)
        + plain_dot(left_low, right_high, left_dim, right_dim)
    )


def dot6(left_side, right_side, left_dim=1, right_dim=0):
    return lax.dot_general(
        left_side,
        right_side,
        (((left_dim,), (right_dim,)), ((), ())),
        precision=lax.Precision.HIGHEST,
        preferred_element_type=jnp.float32,
    )


def inverse_of(matrix):
    size = matrix.shape[0]
    count = size // TILE
    wide = 4
    shape = (TILE, size)
    lane = lax.broadcasted_iota(jnp.int32, shape, 1)
    sub = lax.broadcasted_iota(jnp.int32, shape, 0)

    def over_lanes(block, at):
        return jnp.broadcast_to(block[:, at:at + 1], shape)

    def over_subs(block, at):
        return jnp.broadcast_to(block[at:at + 1, :], shape)

    def swept(entry):
        for j in range(0, TILE, 2):
            k = j + 1
            a, b, c = entry[j, j], entry[j, k], entry[k, k]
            factor = 1.0 / (a * c - b * b)
            others = [m for m in range(TILE) if m not in (j, k)]
            top = {m: entry[min(j, m), max(j, m)] for m in others}
            bottom = {m: entry[min(k, m), max(k, m)] for m in others}
            new_top = {m: c * top[m] - b * bottom[m] for m in others}
            new_bottom = {m: a * bottom[m] - b * top[m] for m in others}
            for i in others:
                for m in others:
                    if i <= m:
                        change = top[i] * new_top[m] + bottom[i] * new_bottom[m]
                        entry[i, m] = entry[i, m] - change * factor
            for m in others:
                entry[min(j, m), max(j, m)] = new_top[m] * factor
                entry[min(k, m), max(k, m)] = new_bottom[m] * factor
            entry[j, j], entry[j, k], entry[k, k] = -c * factor, b * factor, -a * factor
        return entry

    rows = [matrix[TILE * i:TILE * (i + 1), :] for i in range(count)]
    diagonal = [jnp.where(lane - TILE * i == sub, rows[i], 0.0) for i in range(count)]
    along = jnp.broadcast_to(lax.rsqrt(sum(diagonal).sum(axis=0, keepdims=True)), shape)
    down = [jnp.broadcast_to(lax.rsqrt(block.sum(axis=1, keepdims=True)), shape) for block in diagonal]
    rows = [rows[i] * down[i] * along for i in range(count)]
    for panel_at in range(0, count, wide):
        inside = range(panel_at, panel_at + wide)
        for k in inside:
            first = TILE * k
            in_block = (lane >= first) & (lane < first + TILE)
            cols = [over_lanes(rows[k], first + j) for j in range(TILE)]
            entry = swept({(i, j): over_subs(cols[j], i) for j in range(TILE) for i in range(j + 1)})
            panel = jnp.where(in_block, jnp.where(lane - first == sub, -1.0, 0.0), -rows[k])
            old_rows = [over_subs(panel, j) for j in range(TILE)]
            spread_rows = []
            for i in range(TILE):
                parts = [entry[min(i, j), max(i, j)] * old_rows[j] for j in range(TILE)]
                while len(parts) > 1:
                    parts = [parts[p] + parts[p + 1] for p in range(0, len(parts), 2)]
                spread_rows.append(parts[0])
            for i in inside:
                if i != k:
                    block = rows[i]
                    parts = [over_lanes(block, first + j) * spread_rows[j] for j in range(TILE)]
                    while len(parts) > 1:
                        parts = [parts[p] + parts[p + 1] for p in range(0, len(parts), 2)]
                    rows[i] = jnp.where(in_block, 0.0, block) - parts[0]
            panel = spread_rows[0]
            for i in range(1, TILE):
                panel = jnp.where(sub == i, spread_rows[i], panel)
            rows[k] = panel
        first, last = TILE * panel_at, TILE * (panel_at + wide)
        in_panel = (lane >= first) & (lane < last)
        zero = jnp.zeros(shape, jnp.float32)
        factors = jnp.concatenate([zero if i in inside else jnp.where(in_panel, rows[i], 0.0) for i in range(count)], axis=0)
        solved = jnp.concatenate([rows[i] if i in inside else zero for i in range(count)], axis=0)
        change = dot6(factors, solved)
        for i in range(count):
            if i not in inside:
                rows[i] = jnp.where(in_panel, 0.0, rows[i]) - change[TILE * i:TILE * (i + 1), :]
    return jnp.concatenate([rows[i] * down[i] * along for i in range(count)], axis=0)


def invert_kernel(a_ref, o_ref):
    o_ref[...] = inverse_of(a_ref[...])


def invert(matrix):
    size = matrix.shape[0]
    return pl.pallas_call(
        invert_kernel,
        out_shape=arr(size, size),
        in_specs=[VMEM],
        out_specs=VMEM,
        cost_estimate=cost(4 * 10 ** 9, 8 * size ** 2),
    )(matrix)


def ridge(matrix):
    size = matrix.shape[0]
    row = lax.broadcasted_iota(jnp.int32, (size, size), 0)
    col = lax.broadcasted_iota(jnp.int32, (size, size), 1)
    return matrix + jnp.where(row == col, ridge_term, 0.0)


def split3(block):
    high = block.astype(jnp.bfloat16)
    rest = block - high.astype(jnp.float32)
    middle = rest.astype(jnp.bfloat16)
    return high, middle, (rest - middle.astype(jnp.float32)).astype(jnp.bfloat16)


def marks(list_ref, level, sizes, row_count):
    place = [lax.axis_index(axis) for axis in AXES]
    device = 0
    for index, size in zip(place, sizes):
        device = device * size + index
    node = 0
    for index in place[:level + 1]:
        node = node * 2 + index
    row_total = row_count * math.prod(sizes)
    shift = node * (row_total >> level + 1) - device * row_count
    listed = list_ref[pl.ds(node + (2 ** (level + 1) - 2), 1), :] + shift
    row_ids = lax.broadcasted_iota(jnp.int32, (row_count, listed.shape[1]), 0)
    return jnp.where(row_ids == listed, 1.0, 0.0).astype(jnp.bfloat16)


def taken(mark, parts):
    return sum(plain_dot(mark, part, 0, 0) for part in reversed(parts))


def pick_kernel(wanted, sizes, list_hbm, s_hbm, kept_ref, sent_ref, list_ref, s_buf, sems):
    levels = sorted({level for level, _ in wanted})
    sources = sorted({source for _, source in wanted})
    running = copies(
        [(list_hbm, list_ref)] + [(s_hbm.at[source], s_buf.at[at]) for at, source in enumerate(sources)], sems
    )
    half = kept_ref.shape[1]
    here = lax.axis_index("core") == 0
    running[0].wait()
    mark = {level: marks(list_ref, level, sizes, s_buf.shape[1]) for level in levels}
    for at, source in enumerate(sources):
        running[1 + at].wait()
        parts = split3(s_buf[at])
        for slot, (level, from_source) in enumerate(wanted):
            if from_source == source:
                rows = taken(mark[level], parts)
                kept_ref[slot] = jnp.where(here, rows[:half], rows[half:])
                sent_ref[slot] = jnp.where(here, rows[half:], rows[:half])


def pick(skeleton_rows, sample, wanted, sizes):
    _, row_count, samples = sample.shape
    skel = skeleton_rows.shape[1]
    count = len(wanted)
    sources = len({source for _, source in wanted})
    return pl.pallas_call(
        functools.partial(pick_kernel, wanted, sizes),
        out_shape=[arr(count, skel // 2, samples)] * 2,
        in_specs=[ANY, ANY],
        out_specs=[VMEM] * 2,
        scratch_shapes=[
            pltpu.VMEM(skeleton_rows.shape, jnp.int32),
            pltpu.VMEM((sources, row_count, samples), jnp.float32),
            pltpu.SemaphoreType.DMA((1 + sources,)),
        ],
        compiler_params=BIG,
        cost_estimate=cost(10 ** 9 * count, sources * row_count * samples * 4),
    )(skeleton_rows, sample)


def project(sample_block, skeleton, samples, earlier):
    high, low = split(sample_block)
    total = dot3_halves(high, low, skeleton, 1)
    for basis, tilt in earlier:
        total = total - dot3(basis, tilt)
    return total * (1.0 / samples)


def dot3_halves(high, low, skeleton, right_dim):
    width = skeleton.shape[0]
    right_high, right_low = split(skeleton)
    both = plain_dot(high, jnp.concatenate([right_high, right_low], axis=0), 1, right_dim)
    return both[:, :width] + both[:, width:] + plain_dot(low, right_high, 1, right_dim)


def store_terms(kept_ref, sent_ref, kind, term):
    here = lax.axis_index("core") == 0
    half, width = kept_ref.shape[0], term.shape[0]
    turned = term.T
    lanes = pl.ds(kind * width, width)
    kept_ref[:, lanes] = jnp.where(here, turned[:half], turned[half:])
    sent_ref[:, lanes] = jnp.where(here, turned[half:], turned[:half])


def moments(projected, tests):
    high, low = split(projected)
    test_high, test_low = split(tests)
    return plain_dot(high, test_high, 0, 0) + plain_dot(high, test_low, 0, 0) + plain_dot(low, test_high, 0, 0)


def copies(pairs, sems):
    started = []
    for at, (source, target) in enumerate(pairs):
        copy = pltpu.make_async_copy(source, target, sems.at[at])
        copy.start()
        started.append(copy)
    return started


def ordered(mine_ref, other_ref):
    here = lax.axis_index("core") == 0
    low = jnp.where(here, mine_ref[...], other_ref[...])
    high = jnp.where(here, other_ref[...], mine_ref[...])
    return low, high


def joined(low, high, kind):
    return jnp.concatenate([half[:, kind * WIDTH:(kind + 1) * WIDTH] for half in (low, high)], axis=0)


def whole(mine_ref, other_ref):
    return jnp.concatenate(ordered(mine_ref, other_ref), axis=0)


def whole_rows(low, high, slot):
    return jnp.concatenate([low[slot], high[slot]], axis=0)


def couple(skeleton, moment_t):
    spread = ridge(dot6(moment_t, moment_t, 0, 0))
    cross = dot3(skeleton, moment_t)
    return dot3(cross, inverse_of(spread))


def gram_of(skeleton, samples):
    return ridge(dot6(skeleton, skeleton, 1, 1) * (1.0 / samples))


def first_kernel(mine_ref, other_ref, s_hbm, t_hbm, skel_ref, gram_ref, p_ref, kept_ref, sent_ref, s_buf, t_buf, sems):
    samples = mine_ref.shape[1]
    levels = t_buf.shape[0]
    running = copies([(s_hbm.at[0], s_buf)] + [(t_hbm.at[l], t_buf.at[l]) for l in range(levels)], sems)
    skeleton = whole(mine_ref, other_ref)
    skel_ref[...] = skeleton
    gram_ref[...] = gram_of(skeleton, samples)
    running[0].wait()
    projected = project(s_buf[...], skeleton, samples, [])
    p_ref[...] = projected
    for level in range(levels):
        running[1 + level].wait()
        store_terms(kept_ref, sent_ref, level, moments(projected, t_buf[level]))


def second_kernel(mine_ref, other_ref, ours_ref, rows_mine, rows_other, skel0_ref, p0_ref, s_hbm, t_hbm,
                  c0_ref, e02_ref, skel_ref, tilt_ref, gram_ref, p_ref, kept_ref, sent_ref, s_buf, t_buf, sems):
    samples = skel0_ref.shape[1]
    running = copies([(s_hbm.at[1], s_buf), (t_hbm.at[1], t_buf.at[0]), (t_hbm.at[2], t_buf.at[1])], sems)
    low, high = ordered(mine_ref, other_ref)
    rows_low, rows_high = ordered(rows_mine, rows_other)
    skeleton_0 = skel0_ref[...]
    low_0 = dot3(whole_rows(rows_low, rows_high, 0), skeleton_0, 1, 1) * (1.0 / samples)
    coupling = couple(skeleton_0, joined(low, high, 0))
    c0_ref[...] = coupling
    back = dot3(ours_ref[...], coupling)
    e01 = dot3(back, joined(low, high, 1), 1, 1)
    e02_ref[...] = dot3(back, joined(low, high, 2), 1, 1)
    skeleton = whole_rows(rows_low, rows_high, 1) - dot3(low_0, e01)
    skel_ref[...] = skeleton
    gram_ref[...] = gram_of(skeleton, samples)
    tilt = dot3(e01, skeleton, 1, 1)
    tilt_ref[...] = tilt
    running[0].wait()
    projected = project(s_buf[...], skeleton, samples, [(p0_ref[...], tilt)])
    p_ref[...] = projected
    for kind in range(2):
        running[1 + kind].wait()
        store_terms(kept_ref, sent_ref, kind, moments(projected, t_buf[kind]))


def third_kernel(mine_ref, other_ref, ours_ref, rows_mine, rows_other, skel0_ref, skel1_ref, tilt_in_ref, e02_ref,
                 p0_ref, p1_ref, s_hbm, t_hbm, c1_ref, skel_ref, gram_ref, p_ref, kept_ref, sent_ref, s_buf, t_buf, sems):
    samples = skel1_ref.shape[1]
    share = 1.0 / samples
    running = copies([(s_hbm.at[2], s_buf), (t_hbm.at[2], t_buf)], sems)
    low, high = ordered(mine_ref, other_ref)
    rows_low, rows_high = ordered(rows_mine, rows_other)
    skeleton_1 = skel1_ref[...]
    e02 = e02_ref[...]
    low_0 = dot3(whole_rows(rows_low, rows_high, 0), skel0_ref[...], 1, 1) * share
    low_1 = (dot3(whole_rows(rows_low, rows_high, 1), skeleton_1, 1, 1) - dot3(low_0, tilt_in_ref[...])) * share
    rows = whole_rows(rows_low, rows_high, 2) - dot3(low_0, e02)
    coupling = couple(skeleton_1, joined(low, high, 0))
    c1_ref[...] = coupling
    e12 = dot3(dot3(ours_ref[...], coupling), joined(low, high, 1), 1, 1)
    skeleton = rows - dot3(low_1, e12)
    skel_ref[...] = skeleton
    gram_ref[...] = gram_of(skeleton, samples)
    tilt_0 = dot3(e02, skeleton, 1, 1)
    tilt_1 = dot3(e12, skeleton, 1, 1)
    running[0].wait()
    projected = project(s_buf[...], skeleton, samples, [(p0_ref[...], tilt_0), (p1_ref[...], tilt_1)])
    p_ref[...] = projected
    running[1].wait()
    store_terms(kept_ref, sent_ref, 0, moments(projected, t_buf[...]))


def bases_kernel(*refs):
    levels = len(refs) // 2
    for level in range(levels):
        refs[-1][level] = dot3(refs[level][...], refs[levels + level][...])


def last_kernel(mine_ref, other_ref, skel_ref, c0_ref, c1_ref, out_ref):
    low, high = ordered(mine_ref, other_ref)
    out_ref[0, 0] = c0_ref[...]
    out_ref[1, 0] = c1_ref[...]
    out_ref[2, 0] = couple(skel_ref[...], joined(low, high, 0))


def level_call(kernel, specs, outs, scratch, flops, operands):
    return pl.pallas_call(
        kernel,
        out_shape=outs,
        in_specs=specs,
        out_specs=[VMEM] * len(outs),
        scratch_shapes=scratch,
        compiler_params=BIG,
        cost_estimate=cost(flops, 4 * 10 ** 6),
    )(*operands)


def swap(block, axis):
    return lax.ppermute(block, axis, [(0, 1), (1, 0)])


def chips_of(axes):
    return math.prod(lax.axis_size(axis) for axis in axes)


def to_chunks(stack, count):
    rows, width = stack.shape
    return stack.reshape(count, rows // count, width)


def exchange(pieces, axes):
    return lax.all_to_all(pieces, axes, 0, 0, tiled=True)


def total_over(stack, axes):
    for axis in axes:
        count = lax.axis_size(axis)
        if count == 2:
            stack = stack + swap(stack, axis)
        elif count > 2:
            stack = lax.psum(stack, axis)
    return stack


def held(first, *others):
    return lax.optimization_barrier((first,) + others)


def by_inverse(sums, inverse):
    rows, width = sums[0].shape
    stacked = jnp.concatenate(sums, axis=0)
    solved = jnp.dot(stacked, inverse, precision=lax.Precision.HIGH, preferred_element_type=jnp.float32)
    return solved.reshape(len(sums), rows, width)


def local(sample, probes, skeleton_rows):
    levels, row_count, samples = sample.shape
    skel = skeleton_rows.shape[1]
    sizes = [lax.axis_size(axis) for axis in AXES]
    s_buf = pltpu.VMEM((row_count, samples), jnp.float32)
    square, wide, tall = arr(skel, skel), arr(skel, samples), arr(row_count, skel)

    def t_buf(count):
        return pltpu.VMEM((count, row_count, samples), jnp.float32)

    def sems(count):
        return pltpu.SemaphoreType.DMA((count,))

    def outgoing(kinds):
        return [arr(samples // 2, kinds * skel)] * 2

    chips = [("n1", "n2", "mid", "blk"), ("n2", "mid", "blk"), ("mid", "blk")]
    kept, sent = pick(skeleton_rows, sample, ((0, 0),), sizes)
    half = kept[0] + swap(sent[0], "core")
    half, lists = held(half, skeleton_rows)
    half = total_over(half, ("mid", "blk"))
    rest_kept, rest_sent = pick(lists, sample, ((1, 0), (1, 1)), sizes)
    half = total_over(half, ("n2", "n1"))
    rest = rest_kept + swap(rest_sent, "core")
    half, rest = held(half, rest)
    rest = total_over(rest, ("mid", "blk"))

    skeleton_0, gram, projected_0, kept, sent = level_call(
        first_kernel,
        [VMEM] * 2 + [ANY, ANY],
        [wide, square, tall] + outgoing(levels),
        [s_buf, t_buf(levels), sems(1 + levels)],
        3 * 10 ** 9,
        (half, swap(half, "core"), sample, probes),
    )
    sent, rest = held(sent, rest)
    terms = kept + swap(sent, "core")
    inverse_0 = invert(gram)
    rows_one = total_over(rest, ("n2",))
    pieces = exchange(to_chunks(terms, chips_of(chips[0])), chips[0])
    pieces, inverse_0, rows_one = held(pieces, inverse_0, rows_one)
    by_place = pieces.reshape((2, 2, -1) + pieces.shape[1:])
    n0, n01, n02 = [by_place[..., kind * skel:(kind + 1) * skel] for kind in range(3)]
    n01, n02 = n01.sum(axis=(1, 2)), n02.sum(axis=(0, 2))
    sums = by_inverse([n0.sum(axis=(0, 1, 2)), n01[0], n01[1], n02[0], n02[1]], inverse_0)
    sums = swap(sums, "n0")
    sums, lists = held(sums, skeleton_rows)
    rest_kept, rest_sent = pick(lists, sample, ((2, 0), (2, 1), (2, 2)), sizes)
    sendable = jnp.stack([
        jnp.concatenate([sums[0], sums[1 + (1 - one)], sums[3 + (1 - two)]], axis=-1)
        for one in range(2) for two in range(2)
    ])
    inner = chips_of(chips[2])
    sendable = jnp.broadcast_to(sendable[:, None], (4, inner) + sendable.shape[1:])
    mine = exchange(sendable.reshape((4 * inner,) + sendable.shape[2:]), chips[0])
    mine = mine.reshape(samples // 2, levels * skel)
    mine, rest_kept, rest_sent = held(mine, rest_kept, rest_sent)
    other = swap(mine, "core")
    rest = rest_kept + swap(rest_sent, "core")

    coupling_0, e02, skeleton_1, tilt, gram, projected_1, kept, sent = level_call(
        second_kernel,
        [VMEM] * 7 + [ANY, ANY],
        [square, wide, wide, square, square, tall] + outgoing(2),
        [s_buf, t_buf(2), sems(3)],
        8 * 10 ** 9,
        (mine, other, inverse_0, rows_one, swap(rows_one, "core"), skeleton_0, projected_0, sample, probes),
    )
    sent, rest = held(sent, rest)
    terms = kept + swap(sent, "core")
    inverse_1 = invert(gram)
    pieces = exchange(to_chunks(terms, chips_of(chips[1])), chips[1])
    rows_two = total_over(rest, ("mid", "blk"))
    pieces, inverse_1, rows_two = held(pieces, inverse_1, rows_two)
    by_place = pieces.reshape((2, -1) + pieces.shape[1:])
    n1, n12 = by_place[..., :skel], by_place[..., skel:].sum(axis=1)
    sums = by_inverse([n1.sum(axis=(0, 1)), n12[0], n12[1]], inverse_1)
    sums = swap(sums, "n1")
    sendable = jnp.stack([jnp.concatenate([sums[0], sums[1 + (1 - two)]], axis=-1) for two in range(2)])
    sendable = jnp.broadcast_to(sendable[:, None], (2, inner) + sendable.shape[1:])
    mine = exchange(sendable.reshape((2 * inner,) + sendable.shape[2:]), chips[1])
    mine = mine.reshape(samples // 2, 2 * skel)
    other = swap(mine, "core")

    coupling_1, skeleton_2, gram, projected_2, kept, sent = level_call(
        third_kernel,
        [VMEM] * 11 + [ANY, ANY],
        [square, wide, square, tall] + outgoing(1),
        [s_buf, pltpu.VMEM((row_count, samples), jnp.float32), sems(2)],
        8 * 10 ** 9,
        (mine, other, inverse_1, rows_two, swap(rows_two, "core"), skeleton_0, skeleton_1, tilt, e02,
         projected_0, projected_1, sample, probes),
    )
    terms = kept + swap(sent, "core")
    terms = total_over(terms, chips[2])
    inverse_2 = invert(gram)
    terms, inverse_2 = held(terms, inverse_2)
    mine = swap(by_inverse([terms], inverse_2)[0], "n2")
    bases, = level_call(
        bases_kernel, [VMEM] * 6, [arr(levels, row_count, skel)], [], 10 ** 9,
        (projected_0, projected_1, projected_2, inverse_0, inverse_1, inverse_2),
    )
    other = swap(mine, "core")
    other, bases = held(other, bases)
    couplings, = level_call(
        last_kernel, [VMEM] * 5, [arr(levels, 1, skel, skel)], [], 5 * 10 ** 9,
        (mine, other, skeleton_2, coupling_0, coupling_1),
    )
    return bases, couplings


def solution(mesh):
    leaves, blocks = mesh.shape["leaf"], mesh.shape["blk"]
    fine = jax.sharding.Mesh(mesh.devices.reshape(2, 2, 2, leaves // 16, 2, blocks), AXES)
    rows = P(None, AXES, None)
    return jax.shard_map(
        local,
        mesh=fine,
        in_specs=(rows, rows, P()),
        out_specs=(rows, P(None, AXES[:-1], None, None)),
        check_vma=False,
    )
```

```python
import functools
import math

import jax
import jax.numpy as jnp
from jax import lax
from jax.experimental import pallas as pl
from jax.experimental.pallas import tpu as pltpu
from jax.sharding import PartitionSpec as P

ridge_term = 0.05
AXES = ("n0", "n1", "n2", "mid", "core", "blk")
TILE = 8
WIDTH = 128
VMEM = pl.BlockSpec(memory_space=pltpu.VMEM)
SMEM = pl.BlockSpec(memory_space=pltpu.SMEM)
ANY = pl.BlockSpec(memory_space=pltpu.HBM)
BIG = pltpu.CompilerParams(vmem_limit_bytes=49 * 1024 * 1024)


def arr(*shape):
    return jax.ShapeDtypeStruct(shape, jnp.float32)


def cost(flops, bytes_accessed):
    return pl.CostEstimate(flops=flops, bytes_accessed=bytes_accessed, transcendentals=0)


def split(block):
    high = block.astype(jnp.bfloat16)
    low = (block - high.astype(jnp.float32)).astype(jnp.bfloat16)
    return high, low


def plain_dot(left_side, right_side, left_dim, right_dim):
    return lax.dot_general(
        left_side, right_side, (((left_dim,), (right_dim,)), ((), ())), preferred_element_type=jnp.float32
    )


def dot3(left_side, right_side, left_dim=1, right_dim=0):
    left_high, left_low = split(left_side)
    right_high, right_low = split(right_side)
    return (
        plain_dot(left_high, right_high, left_dim, right_dim)
        + plain_dot(left_high, right_low, left_dim, right_dim)
        + plain_dot(left_low, right_high, left_dim, right_dim)
    )


def dot6(left_side, right_side, left_dim=1, right_dim=0):
    return lax.dot_general(
        left_side,
        right_side,
        (((left_dim,), (right_dim,)), ((), ())),
        precision=lax.Precision.HIGHEST,
        preferred_element_type=jnp.float32,
    )


def inverse_of(matrix):
    size = matrix.shape[0]
    count = size // TILE
    wide = 4
    shape = (TILE, size)
    lane = lax.broadcasted_iota(jnp.int32, shape, 1)
    sub = lax.broadcasted_iota(jnp.int32, shape, 0)

    def over_lanes(block, at):
        return jnp.broadcast_to(block[:, at:at + 1], shape)

    def over_subs(block, at):
        return jnp.broadcast_to(block[at:at + 1, :], shape)

    rows = [matrix[TILE * i:TILE * (i + 1), :] for i in range(count)]
    diagonal = [jnp.where(lane - TILE * i == sub, rows[i], 0.0) for i in range(count)]
    along = jnp.broadcast_to(lax.rsqrt(sum(diagonal).sum(axis=0, keepdims=True)), shape)
    down = [jnp.broadcast_to(lax.rsqrt(block.sum(axis=1, keepdims=True)), shape) for block in diagonal]
    rows = [rows[i] * down[i] * along for i in range(count)]
    for panel_at in range(0, count, wide):
        inside = range(panel_at, panel_at + wide)
        for k in inside:
            first = TILE * k
            in_block = (lane >= first) & (lane < first + TILE)
            cols = [over_lanes(rows[k], first + j) for j in range(TILE)]
            panel = jnp.where(in_block, jnp.where(lane - first == sub, 1.0, 0.0), rows[k])
            for j in range(0, TILE, 2):
                one, two = cols[j], cols[j + 1]
                a, b = over_subs(one, j), over_subs(two, j)
                c, d = over_subs(one, j + 1), over_subs(two, j + 1)
                factor = 1.0 / (a * d - b * c)

                def step(block):
                    top, bottom = over_subs(block, j), over_subs(block, j + 1)
                    new_top = d * top - b * bottom
                    new_bottom = a * bottom - c * top
                    others = one * new_top + two * new_bottom
                    kept = jnp.where((sub == j) | (sub == j + 1), 0.0, block)
                    change = jnp.where(sub == j, -new_top, jnp.where(sub == j + 1, -new_bottom, others))
                    return kept - change * factor

                panel = step(panel)
                for m in range(j + 2, TILE):
                    cols[m] = step(cols[m])
            spread_rows = [over_subs(panel, j) for j in range(TILE)]
            for i in inside:
                if i != k:
                    block = rows[i]
                    total = jnp.where(in_block, 0.0, block)
                    for j in range(TILE):
                        total = total - over_lanes(block, first + j) * spread_rows[j]
                    rows[i] = total
            rows[k] = panel
        first, last = TILE * panel_at, TILE * (panel_at + wide)
        in_panel = (lane >= first) & (lane < last)
        zero = jnp.zeros(shape, jnp.float32)
        solved = jnp.concatenate([rows[i] if i in inside else zero for i in range(count)], axis=0)
        ahead = [(panel_at + wide + i) % count for i in range(wide)]
        later = [i for i in range(count) if i not in inside and i not in ahead]
        for chosen in (ahead, later):
            factors = jnp.concatenate([jnp.where(in_panel, rows[i], 0.0) for i in chosen], axis=0)
            change = dot6(factors, solved)
            for at, i in enumerate(chosen):
                rows[i] = jnp.where(in_panel, 0.0, rows[i]) - change[TILE * at:TILE * (at + 1), :]
    return jnp.concatenate([rows[i] * down[i] * along for i in range(count)], axis=0)


def invert_kernel(a_ref, o_ref):
    o_ref[...] = inverse_of(a_ref[...])


def invert(matrix):
    size = matrix.shape[0]
    return pl.pallas_call(
        invert_kernel,
        out_shape=arr(size, size),
        in_specs=[VMEM],
        out_specs=VMEM,
        cost_estimate=cost(4 * 10 ** 9, 8 * size ** 2),
    )(matrix)


def ridge(matrix):
    size = matrix.shape[0]
    row = lax.broadcasted_iota(jnp.int32, (size, size), 0)
    col = lax.broadcasted_iota(jnp.int32, (size, size), 1)
    return matrix + jnp.where(row == col, ridge_term, 0.0)


def split3(block):
    high = block.astype(jnp.bfloat16)
    rest = block - high.astype(jnp.float32)
    middle = rest.astype(jnp.bfloat16)
    return high, middle, (rest - middle.astype(jnp.float32)).astype(jnp.bfloat16)


def marks(list_ref, level, sizes, row_count):
    place = [lax.axis_index(axis) for axis in AXES]
    device = 0
    for index, size in zip(place, sizes):
        device = device * size + index
    node = 0
    for index in place[:level + 1]:
        node = node * 2 + index
    row_total = row_count * math.prod(sizes)
    shift = node * (row_total >> level + 1) - device * row_count
    listed = list_ref[pl.ds(node + (2 ** (level + 1) - 2), 1), :] + shift
    row_ids = lax.broadcasted_iota(jnp.int32, (row_count, listed.shape[1]), 0)
    return jnp.where(row_ids == listed, 1.0, 0.0).astype(jnp.bfloat16)


def taken(mark, parts):
    return sum(plain_dot(mark, part, 0, 0) for part in reversed(parts))


def pick_kernel(wanted, sizes, list_hbm, s_hbm, kept_ref, sent_ref, list_ref, s_buf, sems):
    levels = sorted({level for level, _ in wanted})
    sources = sorted({source for _, source in wanted})
    running = copies(
        [(list_hbm, list_ref)] + [(s_hbm.at[source], s_buf.at[at]) for at, source in enumerate(sources)], sems
    )
    half = kept_ref.shape[1]
    here = lax.axis_index("core") == 0
    running[0].wait()
    mark = {level: marks(list_ref, level, sizes, s_buf.shape[1]) for level in levels}
    for at, source in enumerate(sources):
        running[1 + at].wait()
        parts = split3(s_buf[at])
        for slot, (level, from_source) in enumerate(wanted):
            if from_source == source:
                rows = taken(mark[level], parts)
                kept_ref[slot] = jnp.where(here, rows[:half], rows[half:])
                sent_ref[slot] = jnp.where(here, rows[half:], rows[:half])


def pick(skeleton_rows, sample, wanted, sizes):
    _, row_count, samples = sample.shape
    skel = skeleton_rows.shape[1]
    count = len(wanted)
    sources = len({source for _, source in wanted})
    return pl.pallas_call(
        functools.partial(pick_kernel, wanted, sizes),
        out_shape=[arr(count, skel // 2, samples)] * 2,
        in_specs=[ANY, ANY],
        out_specs=[VMEM] * 2,
        scratch_shapes=[
            pltpu.VMEM(skeleton_rows.shape, jnp.int32),
            pltpu.VMEM((sources, row_count, samples), jnp.float32),
            pltpu.SemaphoreType.DMA((1 + sources,)),
        ],
        compiler_params=BIG,
        cost_estimate=cost(10 ** 9 * count, sources * row_count * samples * 4),
    )(skeleton_rows, sample)


def project(sample_block, skeleton, samples, earlier):
    high, low = split(sample_block)
    total = dot3_halves(high, low, skeleton, 1)
    for basis, tilt in earlier:
        total = total - dot3(basis, tilt)
    return total * (1.0 / samples)


def dot3_halves(high, low, skeleton, right_dim):
    width = skeleton.shape[0]
    right_high, right_low = split(skeleton)
    both = plain_dot(high, jnp.concatenate([right_high, right_low], axis=0), 1, right_dim)
    return both[:, :width] + both[:, width:] + plain_dot(low, right_high, 1, right_dim)


def store_terms(kept_ref, sent_ref, kind, term):
    here = lax.axis_index("core") == 0
    half, width = kept_ref.shape[0], term.shape[0]
    turned = term.T
    lanes = pl.ds(kind * width, width)
    kept_ref[:, lanes] = jnp.where(here, turned[:half], turned[half:])
    sent_ref[:, lanes] = jnp.where(here, turned[half:], turned[:half])


def moments(projected, tests):
    high, low = split(projected)
    test_high, test_low = split(tests)
    return plain_dot(high, test_high, 0, 0) + plain_dot(high, test_low, 0, 0) + plain_dot(low, test_high, 0, 0)


def copies(pairs, sems):
    started = []
    for at, (source, target) in enumerate(pairs):
        copy = pltpu.make_async_copy(source, target, sems.at[at])
        copy.start()
        started.append(copy)
    return started


def ordered(mine_ref, other_ref):
    here = lax.axis_index("core") == 0
    low = jnp.where(here, mine_ref[...], other_ref[...])
    high = jnp.where(here, other_ref[...], mine_ref[...])
    return low, high


def joined(low, high, kind):
    return jnp.concatenate([half[:, kind * WIDTH:(kind + 1) * WIDTH] for half in (low, high)], axis=0)


def whole(mine_ref, other_ref):
    return jnp.concatenate(ordered(mine_ref, other_ref), axis=0)


def whole_rows(low, high, slot):
    return jnp.concatenate([low[slot], high[slot]], axis=0)


def couple(skeleton, moment_t):
    spread = ridge(dot6(moment_t, moment_t, 0, 0))
    cross = dot3(skeleton, moment_t)
    return dot3(cross, inverse_of(spread))


def gram_of(skeleton, samples):
    return ridge(dot6(skeleton, skeleton, 1, 1) * (1.0 / samples))


def first_kernel(mine_ref, other_ref, s_hbm, t_hbm, skel_ref, gram_ref, p_ref, kept_ref, sent_ref, s_buf, t_buf, sems):
    samples = mine_ref.shape[1]
    levels = t_buf.shape[0]
    running = copies([(s_hbm.at[0], s_buf)] + [(t_hbm.at[l], t_buf.at[l]) for l in range(levels)], sems)
    skeleton = whole(mine_ref, other_ref)
    skel_ref[...] = skeleton
    gram_ref[...] = gram_of(skeleton, samples)
    running[0].wait()
    projected = project(s_buf[...], skeleton, samples, [])
    p_ref[...] = projected
    for level in range(levels):
        running[1 + level].wait()
        store_terms(kept_ref, sent_ref, level, moments(projected, t_buf[level]))


def second_kernel(mine_ref, other_ref, ours_ref, rows_mine, rows_other, skel0_ref, p0_ref, s_hbm, t_hbm,
                  c0_ref, e02_ref, skel_ref, tilt_ref, gram_ref, p_ref, kept_ref, sent_ref, s_buf, t_buf, sems):
    samples = skel0_ref.shape[1]
    running = copies([(s_hbm.at[1], s_buf), (t_hbm.at[1], t_buf.at[0]), (t_hbm.at[2], t_buf.at[1])], sems)
    low, high = ordered(mine_ref, other_ref)
    rows_low, rows_high = ordered(rows_mine, rows_other)
    skeleton_0 = skel0_ref[...]
    low_0 = dot3(whole_rows(rows_low, rows_high, 0), skeleton_0, 1, 1) * (1.0 / samples)
    coupling = couple(skeleton_0, joined(low, high, 0))
    c0_ref[...] = coupling
    back = dot3(ours_ref[...], coupling)
    e01 = dot3(back, joined(low, high, 1), 1, 1)
    e02_ref[...] = dot3(back, joined(low, high, 2), 1, 1)
    skeleton = whole_rows(rows_low, rows_high, 1) - dot3(low_0, e01)
    skel_ref[...] = skeleton
    gram_ref[...] = gram_of(skeleton, samples)
    tilt = dot3(e01, skeleton, 1, 1)
    tilt_ref[...] = tilt
    running[0].wait()
    projected = project(s_buf[...], skeleton, samples, [(p0_ref[...], tilt)])
    p_ref[...] = projected
    for kind in range(2):
        running[1 + kind].wait()
        store_terms(kept_ref, sent_ref, kind, moments(projected, t_buf[kind]))


def third_kernel(mine_ref, other_ref, ours_ref, rows_mine, rows_other, skel0_ref, skel1_ref, tilt_in_ref, e02_ref,
                 p0_ref, p1_ref, s_hbm, t_hbm, c1_ref, skel_ref, gram_ref, p_ref, kept_ref, sent_ref, s_buf, t_buf, sems):
    samples = skel1_ref.shape[1]
    share = 1.0 / samples
    running = copies([(s_hbm.at[2], s_buf), (t_hbm.at[2], t_buf)], sems)
    low, high = ordered(mine_ref, other_ref)
    rows_low, rows_high = ordered(rows_mine, rows_other)
    skeleton_1 = skel1_ref[...]
    e02 = e02_ref[...]
    low_0 = dot3(whole_rows(rows_low, rows_high, 0), skel0_ref[...], 1, 1) * share
    low_1 = (dot3(whole_rows(rows_low, rows_high, 1), skeleton_1, 1, 1) - dot3(low_0, tilt_in_ref[...])) * share
    rows = whole_rows(rows_low, rows_high, 2) - dot3(low_0, e02)
    coupling = couple(skeleton_1, joined(low, high, 0))
    c1_ref[...] = coupling
    e12 = dot3(dot3(ours_ref[...], coupling), joined(low, high, 1), 1, 1)
    skeleton = rows - dot3(low_1, e12)
    skel_ref[...] = skeleton
    gram_ref[...] = gram_of(skeleton, samples)
    tilt_0 = dot3(e02, skeleton, 1, 1)
    tilt_1 = dot3(e12, skeleton, 1, 1)
    running[0].wait()
    projected = project(s_buf[...], skeleton, samples, [(p0_ref[...], tilt_0), (p1_ref[...], tilt_1)])
    p_ref[...] = projected
    running[1].wait()
    store_terms(kept_ref, sent_ref, 0, moments(projected, t_buf[...]))


def bases_kernel(*refs):
    levels = len(refs) // 2
    for level in range(levels):
        refs[-1][level] = dot3(refs[level][...], refs[levels + level][...])


def last_kernel(mine_ref, other_ref, skel_ref, c0_ref, c1_ref, out_ref):
    low, high = ordered(mine_ref, other_ref)
    out_ref[0, 0] = c0_ref[...]
    out_ref[1, 0] = c1_ref[...]
    out_ref[2, 0] = couple(skel_ref[...], joined(low, high, 0))


def level_call(kernel, specs, outs, scratch, flops, operands):
    return pl.pallas_call(
        kernel,
        out_shape=outs,
        in_specs=specs,
        out_specs=[VMEM] * len(outs),
        scratch_shapes=scratch,
        compiler_params=BIG,
        cost_estimate=cost(flops, 4 * 10 ** 6),
    )(*operands)


def swap(block, axis):
    return lax.ppermute(block, axis, [(0, 1), (1, 0)])


def chips_of(axes):
    return math.prod(lax.axis_size(axis) for axis in axes)


def to_chunks(stack, count):
    rows, width = stack.shape
    return stack.reshape(count, rows // count, width)


def exchange(pieces, axes):
    return lax.all_to_all(pieces, axes, 0, 0, tiled=True)


def total_over(stack, axes):
    for axis in axes:
        count = lax.axis_size(axis)
        if count == 2:
            stack = stack + swap(stack, axis)
        elif count > 2:
            stack = lax.psum(stack, axis)
    return stack


def held(first, *others):
    return lax.optimization_barrier((first,) + others)


def combine_kernel(plan, pieces_ref, inverse_ref, out_ref):
    inverse = inverse_ref[...]
    for at, (kind, places) in enumerate(plan):
        lanes = slice(kind * WIDTH, (kind + 1) * WIDTH)
        out_ref[at] = dot3(sum(pieces_ref[place, :, lanes] for place in places), inverse)


def combine(pieces, inverse, plan):
    rows = pieces.shape[1]
    return pl.pallas_call(
        functools.partial(combine_kernel, plan),
        out_shape=arr(len(plan), rows, WIDTH),
        in_specs=[VMEM, VMEM],
        out_specs=VMEM,
        cost_estimate=cost(10 ** 8, 10 ** 6),
    )(pieces, inverse)


def fan_kernel(plan, sums_ref, out_ref):
    for place, wanted in enumerate(plan):
        for kind, at in enumerate(wanted):
            out_ref[place, :, kind * WIDTH:(kind + 1) * WIDTH] = sums_ref[at]


def fan_out(sums, plan):
    rows = sums.shape[1]
    return pl.pallas_call(
        functools.partial(fan_kernel, plan),
        out_shape=arr(len(plan), rows, WIDTH * len(plan[0])),
        in_specs=[VMEM],
        out_specs=VMEM,
        cost_estimate=cost(10 ** 6, 10 ** 6),
    )(sums)


def local(sample, probes, skeleton_rows):
    levels, row_count, samples = sample.shape
    skel = skeleton_rows.shape[1]
    sizes = [lax.axis_size(axis) for axis in AXES]
    s_buf = pltpu.VMEM((row_count, samples), jnp.float32)
    square, wide, tall = arr(skel, skel), arr(skel, samples), arr(row_count, skel)

    def t_buf(count):
        return pltpu.VMEM((count, row_count, samples), jnp.float32)

    def sems(count):
        return pltpu.SemaphoreType.DMA((count,))

    def outgoing(kinds):
        return [arr(samples // 2, kinds * skel)] * 2

    chips = [("n1", "n2", "mid", "blk"), ("n2", "mid", "blk"), ("mid", "blk")]
    kept, sent = pick(skeleton_rows, sample, ((0, 0),), sizes)
    half = kept[0] + swap(sent[0], "core")
    half, lists = held(half, skeleton_rows)
    half = total_over(half, ("mid", "blk"))
    rest_kept, rest_sent = pick(lists, sample, ((1, 0), (1, 1)), sizes)
    half = total_over(half, ("n2", "n1"))
    rest = rest_kept + swap(rest_sent, "core")
    rest = total_over(rest, ("mid", "blk"))

    skeleton_0, gram, projected_0, kept, sent = level_call(
        first_kernel,
        [VMEM] * 2 + [ANY, ANY],
        [wide, square, tall] + outgoing(levels),
        [s_buf, t_buf(levels), sems(1 + levels)],
        3 * 10 ** 9,
        (half, swap(half, "core"), sample, probes),
    )
    sent, rest = held(sent, rest)
    terms = kept + swap(sent, "core")
    inverse_0 = invert(gram)
    rows_one = total_over(rest, ("n2",))
    pieces = exchange(to_chunks(terms, chips_of(chips[0])), chips[0])
    pieces, inverse_0 = held(pieces, inverse_0)
    inner = chips_of(chips[2])
    places = [(one, two) for one in range(2) for two in range(2) for _ in range(inner)]
    every = range(len(places))
    plan = [(0, list(every))]
    plan += [(1, [at for at in every if places[at][0] == one]) for one in range(2)]
    plan += [(2, [at for at in every if places[at][1] == two]) for two in range(2)]
    sums = swap(combine(pieces, inverse_0, plan), "n0")
    sums, lists, rows_one = held(sums, skeleton_rows, rows_one)
    rest_kept, rest_sent = pick(lists, sample, ((2, 0), (2, 1), (2, 2)), sizes)
    mine = exchange(fan_out(sums, [(0, 2 - one, 4 - two) for one, two in places]), chips[0])
    mine = mine.reshape(samples // 2, levels * skel)
    mine, rest_kept, rest_sent = held(mine, rest_kept, rest_sent)
    other = swap(mine, "core")
    rest = rest_kept + swap(rest_sent, "core")

    coupling_0, e02, skeleton_1, tilt, gram, projected_1, kept, sent = level_call(
        second_kernel,
        [VMEM] * 7 + [ANY, ANY],
        [square, wide, wide, square, square, tall] + outgoing(2),
        [s_buf, t_buf(2), sems(3)],
        8 * 10 ** 9,
        (mine, other, inverse_0, rows_one, swap(rows_one, "core"), skeleton_0, projected_0, sample, probes),
    )
    sent, rest = held(sent, rest)
    terms = kept + swap(sent, "core")
    inverse_1 = invert(gram)
    pieces = exchange(to_chunks(terms, chips_of(chips[1])), chips[1])
    rows_two = total_over(rest, ("mid", "blk"))
    pieces, inverse_1, rows_two = held(pieces, inverse_1, rows_two)
    places = [two for two in range(2) for _ in range(inner)]
    every = range(len(places))
    plan = [(0, list(every))] + [(1, [at for at in every if places[at] == two]) for two in range(2)]
    sums = swap(combine(pieces, inverse_1, plan), "n1")
    mine = exchange(fan_out(sums, [(0, 2 - two) for two in places]), chips[1])
    mine = mine.reshape(samples // 2, 2 * skel)
    other = swap(mine, "core")

    coupling_1, skeleton_2, gram, projected_2, kept, sent = level_call(
        third_kernel,
        [VMEM] * 11 + [ANY, ANY],
        [square, wide, square, tall] + outgoing(1),
        [s_buf, pltpu.VMEM((row_count, samples), jnp.float32), sems(2)],
        8 * 10 ** 9,
        (mine, other, inverse_1, rows_two, swap(rows_two, "core"), skeleton_0, skeleton_1, tilt, e02,
         projected_0, projected_1, sample, probes),
    )
    terms = kept + swap(sent, "core")
    terms = total_over(terms, chips[2])
    inverse_2 = invert(gram)
    terms, inverse_2 = held(terms, inverse_2)
    mine = swap(combine(terms[None], inverse_2, [(0, [0])])[0], "n2")
    bases, = level_call(
        bases_kernel, [VMEM] * 6, [arr(levels, row_count, skel)], [], 4 * 10 ** 9,
        (projected_0, projected_1, projected_2, inverse_0, inverse_1, inverse_2),
    )
    mine, bases = held(mine, bases)
    other = swap(mine, "core")
    couplings, = level_call(
        last_kernel, [VMEM] * 5, [arr(levels, 1, skel, skel)], [], 5 * 10 ** 9,
        (mine, other, skeleton_2, coupling_0, coupling_1),
    )
    return bases, couplings


def solution(mesh):
    leaves, blocks = mesh.shape["leaf"], mesh.shape["blk"]
    fine = jax.sharding.Mesh(mesh.devices.reshape(2, 2, 2, leaves // 16, 2, blocks), AXES)
    rows = P(None, AXES, None)
    return jax.shard_map(
        local,
        mesh=fine,
        in_specs=(rows, rows, P()),
        out_specs=(rows, P(None, AXES[:-1], None, None)),
        check_vma=False,
    )
```

```python
import functools
import math

import jax
import jax.numpy as jnp
from jax import lax
from jax.experimental import pallas as pl
from jax.experimental.pallas import tpu as pltpu
from jax.sharding import PartitionSpec as P

ridge_term = 0.05
AXES = ("n0", "n1", "n2", "mid", "core", "blk")
TILE = 8
PANEL = 4
WIDTH = 128
VMEM = pl.BlockSpec(memory_space=pltpu.VMEM)
SMEM = pl.BlockSpec(memory_space=pltpu.SMEM)
ANY = pl.BlockSpec(memory_space=pltpu.HBM)
BIG = pltpu.CompilerParams(vmem_limit_bytes=49 * 1024 * 1024)
SMALL = pltpu.CompilerParams(vmem_limit_bytes=4 * 1024 * 1024)


def arr(*shape):
    return jax.ShapeDtypeStruct(shape, jnp.float32)


def cost(flops, bytes_accessed):
    return pl.CostEstimate(flops=flops, bytes_accessed=bytes_accessed, transcendentals=0)


def split(block):
    high = block.astype(jnp.bfloat16)
    low = (block - high.astype(jnp.float32)).astype(jnp.bfloat16)
    return high, low


def plain_dot(left_side, right_side, left_dim, right_dim):
    return lax.dot_general(
        left_side, right_side, (((left_dim,), (right_dim,)), ((), ())), preferred_element_type=jnp.float32
    )


def dot3(left_side, right_side, left_dim=1, right_dim=0):
    left_high, left_low = split(left_side)
    right_high, right_low = split(right_side)
    return (
        plain_dot(left_high, right_high, left_dim, right_dim)
        + plain_dot(left_high, right_low, left_dim, right_dim)
        + plain_dot(left_low, right_high, left_dim, right_dim)
    )


def dot6(left_side, right_side, left_dim=1, right_dim=0):
    return lax.dot_general(
        left_side,
        right_side,
        (((left_dim,), (right_dim,)), ((), ())),
        precision=lax.Precision.HIGHEST,
        preferred_element_type=jnp.float32,
    )


def scales_of(matrix):
    size = matrix.shape[0]
    row = lax.broadcasted_iota(jnp.int32, (size, size), 0)
    col = lax.broadcasted_iota(jnp.int32, (size, size), 1)
    diagonal = jnp.where(row == col, matrix, 0.0)
    along = lax.rsqrt(diagonal.sum(axis=0, keepdims=True))
    down = lax.rsqrt(diagonal.sum(axis=1, keepdims=True))
    return jnp.broadcast_to(down, matrix.shape) * jnp.broadcast_to(along, matrix.shape)


def inverse_of(matrix):
    scales = scales_of(matrix)
    panels = matrix.shape[0] // TILE // PANEL
    return eliminate(matrix * scales, range(panels)) * scales


def eliminate(matrix, panels):
    size = matrix.shape[0]
    count = size // TILE
    wide = PANEL
    shape = (TILE, size)
    lane = lax.broadcasted_iota(jnp.int32, shape, 1)
    sub = lax.broadcasted_iota(jnp.int32, shape, 0)

    def over_lanes(block, at):
        return jnp.broadcast_to(block[:, at:at + 1], shape)

    def over_subs(block, at):
        return jnp.broadcast_to(block[at:at + 1, :], shape)

    rows = [matrix[TILE * i:TILE * (i + 1), :] for i in range(count)]
    for panel_at in [wide * panel for panel in panels]:
        inside = range(panel_at, panel_at + wide)
        for k in inside:
            first = TILE * k
            in_block = (lane >= first) & (lane < first + TILE)
            cols = [over_lanes(rows[k], first + j) for j in range(TILE)]
            panel = jnp.where(in_block, jnp.where(lane - first == sub, 1.0, 0.0), rows[k])
            for j in range(0, TILE, 2):
                one, two = cols[j], cols[j + 1]
                a, b = over_subs(one, j), over_subs(two, j)
                c, d = over_subs(one, j + 1), over_subs(two, j + 1)
                factor = 1.0 / (a * d - b * c)

                def step(block):
                    top, bottom = over_subs(block, j), over_subs(block, j + 1)
                    new_top = d * top - b * bottom
                    new_bottom = a * bottom - c * top
                    others = one * new_top + two * new_bottom
                    kept = jnp.where((sub == j) | (sub == j + 1), 0.0, block)
                    change = jnp.where(sub == j, -new_top, jnp.where(sub == j + 1, -new_bottom, others))
                    return kept - change * factor

                panel = step(panel)
                for m in range(j + 2, TILE):
                    cols[m] = step(cols[m])
            spread_rows = [over_subs(panel, j) for j in range(TILE)]
            for i in inside:
                if i != k:
                    block = rows[i]
                    total = jnp.where(in_block, 0.0, block)
                    for j in range(TILE):
                        total = total - over_lanes(block, first + j) * spread_rows[j]
                    rows[i] = total
            rows[k] = panel
        first, last = TILE * panel_at, TILE * (panel_at + wide)
        in_panel = (lane >= first) & (lane < last)
        zero = jnp.zeros(shape, jnp.float32)
        solved = jnp.concatenate([rows[i] if i in inside else zero for i in range(count)], axis=0)
        ahead = [(panel_at + wide + i) % count for i in range(wide)]
        later = [i for i in range(count) if i not in inside and i not in ahead]
        for chosen in (ahead, later):
            factors = jnp.concatenate([jnp.where(in_panel, rows[i], 0.0) for i in chosen], axis=0)
            change = dot6(factors, solved)
            for at, i in enumerate(chosen):
                rows[i] = jnp.where(in_panel, 0.0, rows[i]) - change[TILE * at:TILE * (at + 1), :]
    return jnp.concatenate(rows, axis=0)


def first_half_kernel(a_ref, o_ref, scales_ref):
    scales = scales_of(a_ref[...])
    scales_ref[...] = scales
    o_ref[...] = eliminate(a_ref[...] * scales, (0, 1))


def second_half_kernel(a_ref, scales_ref, o_ref):
    o_ref[...] = eliminate(a_ref[...], (2, 3)) * scales_ref[...]


def invert(matrix):
    size = matrix.shape[0]
    half = cost(2 * 10 ** 9, 8 * size ** 2)
    square = arr(size, size)
    state, scales = pl.pallas_call(
        first_half_kernel, out_shape=[square] * 2, in_specs=[VMEM], out_specs=[VMEM] * 2,
        compiler_params=SMALL, cost_estimate=half,
    )(matrix)
    return pl.pallas_call(
        second_half_kernel, out_shape=square, in_specs=[VMEM] * 2, out_specs=VMEM,
        compiler_params=SMALL, cost_estimate=half,
    )(state, scales)


def ridge(matrix):
    size = matrix.shape[0]
    row = lax.broadcasted_iota(jnp.int32, (size, size), 0)
    col = lax.broadcasted_iota(jnp.int32, (size, size), 1)
    return matrix + jnp.where(row == col, ridge_term, 0.0)


def split3(block):
    high = block.astype(jnp.bfloat16)
    rest = block - high.astype(jnp.float32)
    middle = rest.astype(jnp.bfloat16)
    return high, middle, (rest - middle.astype(jnp.float32)).astype(jnp.bfloat16)


def marks(list_ref, level, sizes, row_count):
    place = [lax.axis_index(axis) for axis in AXES]
    device = 0
    for index, size in zip(place, sizes):
        device = device * size + index
    node = 0
    for index in place[:level + 1]:
        node = node * 2 + index
    row_total = row_count * math.prod(sizes)
    shift = node * (row_total >> level + 1) - device * row_count
    listed = list_ref[pl.ds(node + (2 ** (level + 1) - 2), 1), :] + shift
    row_ids = lax.broadcasted_iota(jnp.int32, (row_count, listed.shape[1]), 0)
    return jnp.where(row_ids == listed, 1.0, 0.0).astype(jnp.bfloat16)


def taken(mark, parts):
    return sum(plain_dot(mark, part, 0, 0) for part in reversed(parts))


def pick_kernel(wanted, sizes, list_hbm, s_hbm, kept_ref, sent_ref, list_ref, s_buf, sems):
    levels = sorted({level for level, _ in wanted})
    sources = sorted({source for _, source in wanted})
    running = copies(
        [(list_hbm, list_ref)] + [(s_hbm.at[source], s_buf.at[at]) for at, source in enumerate(sources)], sems
    )
    half = kept_ref.shape[1]
    here = lax.axis_index("core") == 0
    running[0].wait()
    mark = {level: marks(list_ref, level, sizes, s_buf.shape[1]) for level in levels}
    for at, source in enumerate(sources):
        running[1 + at].wait()
        parts = split3(s_buf[at])
        for slot, (level, from_source) in enumerate(wanted):
            if from_source == source:
                rows = taken(mark[level], parts)
                kept_ref[slot] = jnp.where(here, rows[:half], rows[half:])
                sent_ref[slot] = jnp.where(here, rows[half:], rows[:half])


def pick(skeleton_rows, sample, wanted, sizes):
    _, row_count, samples = sample.shape
    skel = skeleton_rows.shape[1]
    count = len(wanted)
    sources = len({source for _, source in wanted})
    return pl.pallas_call(
        functools.partial(pick_kernel, wanted, sizes),
        out_shape=[arr(count, skel // 2, samples)] * 2,
        in_specs=[ANY, ANY],
        out_specs=[VMEM] * 2,
        scratch_shapes=[
            pltpu.VMEM(skeleton_rows.shape, jnp.int32),
            pltpu.VMEM((sources, row_count, samples), jnp.float32),
            pltpu.SemaphoreType.DMA((1 + sources,)),
        ],
        compiler_params=BIG,
        cost_estimate=cost(10 ** 9 * count, sources * row_count * samples * 4),
    )(skeleton_rows, sample)


def project(sample_block, skeleton, samples, earlier):
    high, low = split(sample_block)
    total = dot3_halves(high, low, skeleton, 1)
    for basis, tilt in earlier:
        total = total - dot3(basis, tilt)
    return total * (1.0 / samples)


def dot3_halves(high, low, skeleton, right_dim):
    width = skeleton.shape[0]
    right_high, right_low = split(skeleton)
    both = plain_dot(high, jnp.concatenate([right_high, right_low], axis=0), 1, right_dim)
    return both[:, :width] + both[:, width:] + plain_dot(low, right_high, 1, right_dim)


def store_terms(kept_ref, sent_ref, kind, term):
    here = lax.axis_index("core") == 0
    half, width = kept_ref.shape[0], term.shape[0]
    turned = term.T
    lanes = pl.ds(kind * width, width)
    kept_ref[:, lanes] = jnp.where(here, turned[:half], turned[half:])
    sent_ref[:, lanes] = jnp.where(here, turned[half:], turned[:half])


def moments(projected, tests):
    high, low = split(projected)
    test_high, test_low = split(tests)
    return plain_dot(high, test_high, 0, 0) + plain_dot(high, test_low, 0, 0) + plain_dot(low, test_high, 0, 0)


def copies(pairs, sems):
    started = []
    for at, (source, target) in enumerate(pairs):
        copy = pltpu.make_async_copy(source, target, sems.at[at])
        copy.start()
        started.append(copy)
    return started


def ordered(mine_ref, other_ref):
    here = lax.axis_index("core") == 0
    low = jnp.where(here, mine_ref[...], other_ref[...])
    high = jnp.where(here, other_ref[...], mine_ref[...])
    return low, high


def joined(low, high, kind):
    return jnp.concatenate([half[:, kind * WIDTH:(kind + 1) * WIDTH] for half in (low, high)], axis=0)


def whole(mine_ref, other_ref):
    return jnp.concatenate(ordered(mine_ref, other_ref), axis=0)


def whole_rows(low, high, slot):
    return jnp.concatenate([low[slot], high[slot]], axis=0)


def couple(skeleton, moment_t):
    spread = ridge(dot6(moment_t, moment_t, 0, 0))
    cross = dot3(skeleton, moment_t)
    return dot3(cross, inverse_of(spread))


def gram_of(skeleton, samples):
    return ridge(dot6(skeleton, skeleton, 1, 1) * (1.0 / samples))


def first_kernel(mine_ref, other_ref, s_hbm, t_hbm, skel_ref, gram_ref, p_hbm, kept_ref, sent_ref,
                 s_buf, t_buf, p_ref, sems):
    samples = mine_ref.shape[1]
    levels = t_buf.shape[0]
    running = copies([(s_hbm.at[0], s_buf)] + [(t_hbm.at[l], t_buf.at[l]) for l in range(levels)], sems)
    skeleton = whole(mine_ref, other_ref)
    skel_ref[...] = skeleton
    gram_ref[...] = gram_of(skeleton, samples)
    running[0].wait()
    projected = project(s_buf[...], skeleton, samples, [])
    p_ref[...] = projected
    leaving = copies([(p_ref, p_hbm)], sems.at[pl.ds(1 + levels, 1)])
    for level in range(levels):
        running[1 + level].wait()
        store_terms(kept_ref, sent_ref, level, moments(projected, t_buf[level]))
    leaving[0].wait()


def second_kernel(mine_ref, other_ref, ours_ref, rows_mine, rows_other, skel0_ref, p0_hbm, s_hbm, t_hbm,
                  c0_ref, e02_ref, skel_ref, tilt_ref, gram_ref, p_hbm, kept_ref, sent_ref,
                  s_buf, t_buf, p_ref, p0_ref, sems):
    samples = skel0_ref.shape[1]
    running = copies([(s_hbm.at[1], s_buf), (p0_hbm, p0_ref), (t_hbm.at[1], t_buf.at[0]), (t_hbm.at[2], t_buf.at[1])], sems)
    low, high = ordered(mine_ref, other_ref)
    rows_low, rows_high = ordered(rows_mine, rows_other)
    skeleton_0 = skel0_ref[...]
    low_0 = dot3(whole_rows(rows_low, rows_high, 0), skeleton_0, 1, 1) * (1.0 / samples)
    coupling = couple(skeleton_0, joined(low, high, 0))
    c0_ref[...] = coupling
    back = dot3(ours_ref[...], coupling)
    e01 = dot3(back, joined(low, high, 1), 1, 1)
    e02_ref[...] = dot3(back, joined(low, high, 2), 1, 1)
    skeleton = whole_rows(rows_low, rows_high, 1) - dot3(low_0, e01)
    skel_ref[...] = skeleton
    gram_ref[...] = gram_of(skeleton, samples)
    tilt = dot3(e01, skeleton, 1, 1)
    tilt_ref[...] = tilt
    running[0].wait()
    running[1].wait()
    projected = project(s_buf[...], skeleton, samples, [(p0_ref[...], tilt)])
    p_ref[...] = projected
    leaving = copies([(p_ref, p_hbm)], sems.at[pl.ds(4, 1)])
    for kind in range(2):
        running[2 + kind].wait()
        store_terms(kept_ref, sent_ref, kind, moments(projected, t_buf[kind]))
    leaving[0].wait()


def third_kernel(pieces, *refs):
    parts, refs = refs[:pieces], refs[pieces:]
    (ours_ref, rows_mine, rows_other, skel0_ref, skel1_ref, tilt_in_ref, e02_ref, p0_hbm, p1_hbm, s_hbm, t_hbm,
     c1_ref, skel_ref, gram_ref, p_hbm, kept_ref, sent_ref, s_buf, t_buf, p_ref, p0_ref, p1_ref, sems) = refs
    samples = skel1_ref.shape[1]
    share = 1.0 / samples
    running = copies([(s_hbm.at[2], s_buf), (p0_hbm, p0_ref), (p1_hbm, p1_ref), (t_hbm.at[2], t_buf)], sems)
    if pieces == 2:
        low, high = ordered(*parts)
    else:
        first = lax.axis_index("blk") == 0
        both = [
            jnp.concatenate([jnp.where(first, one, two), jnp.where(first, two, one)], axis=0)
            for one, two in ((parts[0][...], parts[1][...]), (parts[2][...], parts[3][...]))
        ]
        here = lax.axis_index("core") == 0
        low = jnp.where(here, both[0], both[1])
        high = jnp.where(here, both[1], both[0])
    rows_low, rows_high = ordered(rows_mine, rows_other)
    skeleton_1 = skel1_ref[...]
    e02 = e02_ref[...]
    low_0 = dot3(whole_rows(rows_low, rows_high, 0), skel0_ref[...], 1, 1) * share
    low_1 = (dot3(whole_rows(rows_low, rows_high, 1), skeleton_1, 1, 1) - dot3(low_0, tilt_in_ref[...])) * share
    rows = whole_rows(rows_low, rows_high, 2) - dot3(low_0, e02)
    coupling = couple(skeleton_1, joined(low, high, 0))
    c1_ref[...] = coupling
    e12 = dot3(dot3(ours_ref[...], coupling), joined(low, high, 1), 1, 1)
    skeleton = rows - dot3(low_1, e12)
    skel_ref[...] = skeleton
    gram_ref[...] = gram_of(skeleton, samples)
    tilt_0 = dot3(e02, skeleton, 1, 1)
    tilt_1 = dot3(e12, skeleton, 1, 1)
    for copy in running[:3]:
        copy.wait()
    projected = project(s_buf[...], skeleton, samples, [(p0_ref[...], tilt_0), (p1_ref[...], tilt_1)])
    p_ref[...] = projected
    leaving = copies([(p_ref, p_hbm)], sems.at[pl.ds(4, 1)])
    running[3].wait()
    store_terms(kept_ref, sent_ref, 0, moments(projected, t_buf[...]))
    leaving[0].wait()


def bases_kernel(p0_hbm, p1_hbm, p2_hbm, inverse_0, inverse_1, inverse_2, out_ref, p_buf, sems):
    running = copies([(source, p_buf.at[at]) for at, source in enumerate((p0_hbm, p1_hbm, p2_hbm))], sems)
    for level, inverse in enumerate((inverse_0, inverse_1, inverse_2)):
        running[level].wait()
        out_ref[level] = dot3(p_buf[level], inverse[...])


def last_kernel(mine_ref, other_ref, skel_ref, c0_ref, c1_ref, out_ref):
    low, high = ordered(mine_ref, other_ref)
    out_ref[0, 0] = c0_ref[...]
    out_ref[1, 0] = c1_ref[...]
    out_ref[2, 0] = couple(skel_ref[...], joined(low, high, 0))


def level_call(kernel, specs, outs, scratch, flops, operands, in_hbm=None):
    return pl.pallas_call(
        kernel,
        out_shape=outs,
        in_specs=specs,
        out_specs=[ANY if at == in_hbm else VMEM for at in range(len(outs))],
        scratch_shapes=scratch,
        compiler_params=BIG,
        cost_estimate=cost(flops, 4 * 10 ** 6),
    )(*operands)


def swap(block, axis):
    return lax.ppermute(block, axis, [(0, 1), (1, 0)])


def chips_of(axes):
    return math.prod(lax.axis_size(axis) for axis in axes)


def to_chunks(stack, count):
    rows, width = stack.shape
    return stack.reshape(count, rows // count, width)


def exchange(pieces, axes):
    return lax.all_to_all(pieces, axes, 0, 0, tiled=True)


def total_over(stack, axes):
    for axis in axes:
        count = lax.axis_size(axis)
        if count == 2:
            stack = stack + swap(stack, axis)
        elif count > 2:
            stack = lax.psum(stack, axis)
    return stack


def held(first, *others):
    return lax.optimization_barrier((first,) + others)


def combine_kernel(plan, *refs):
    pieces_refs, inverse_ref, out_ref = refs[:-2], refs[-2], refs[-1]
    inverse = inverse_ref[...]
    for at, (kind, places) in enumerate(plan):
        lanes = slice(kind * WIDTH, (kind + 1) * WIDTH)
        total = sum(pieces_refs[which][place, :, lanes] for which, place in places)
        out_ref[at] = dot3(total, inverse)


def combine(pieces, inverse, plan):
    rows = pieces[0].shape[1]
    return pl.pallas_call(
        functools.partial(combine_kernel, plan),
        out_shape=arr(len(plan), rows, WIDTH),
        in_specs=[VMEM] * (len(pieces) + 1),
        out_specs=VMEM,
        compiler_params=SMALL,
        cost_estimate=cost(10 ** 8, 10 ** 6),
    )(*pieces, inverse)


def add_split_kernel(axis, one_ref, two_ref, kept_ref, sent_ref):
    total = one_ref[...] + two_ref[...]
    half = kept_ref.shape[0]
    first = lax.axis_index(axis) == 0
    kept_ref[...] = jnp.where(first, total[:half], total[half:])
    sent_ref[...] = jnp.where(first, total[half:], total[:half])


def add_split(one, two, axis):
    rows, width = one.shape
    return pl.pallas_call(
        functools.partial(add_split_kernel, axis),
        out_shape=[arr(rows // 2, width)] * 2,
        in_specs=[VMEM] * 2,
        out_specs=[VMEM] * 2,
        compiler_params=SMALL,
        cost_estimate=cost(10 ** 6, 10 ** 6),
    )(one, two)


def fan_kernel(plan, sums_ref, out_ref):
    for place, wanted in enumerate(plan):
        for kind, at in enumerate(wanted):
            out_ref[place, :, kind * WIDTH:(kind + 1) * WIDTH] = sums_ref[at]


def fan_out(sums, plan):
    rows = sums.shape[1]
    return pl.pallas_call(
        functools.partial(fan_kernel, plan),
        out_shape=arr(len(plan), rows, WIDTH * len(plan[0])),
        in_specs=[VMEM],
        out_specs=VMEM,
        compiler_params=SMALL,
        cost_estimate=cost(10 ** 6, 10 ** 6),
    )(sums)


def local(sample, probes, skeleton_rows):
    levels, row_count, samples = sample.shape
    skel = skeleton_rows.shape[1]
    sizes = [lax.axis_size(axis) for axis in AXES]
    s_buf = pltpu.VMEM((row_count, samples), jnp.float32)
    p_buf = pltpu.VMEM((row_count, skel), jnp.float32)
    square, wide, tall = arr(skel, skel), arr(skel, samples), arr(row_count, skel)

    def t_buf(count):
        return pltpu.VMEM((count, row_count, samples), jnp.float32)

    def sems(count):
        return pltpu.SemaphoreType.DMA((count,))

    def outgoing(kinds):
        return [arr(samples // 2, kinds * skel)] * 2

    chips = [("n1", "n2", "mid", "blk"), ("n2", "mid", "blk"), ("mid", "blk")]
    kept, sent = pick(skeleton_rows, sample, ((0, 0),), sizes)
    half = kept[0] + swap(sent[0], "core")
    half, lists = held(half, skeleton_rows)
    half = total_over(half, ("mid", "blk"))
    rest_kept, rest_sent = pick(lists, sample, ((1, 0), (1, 1)), sizes)
    half = total_over(half, ("n2", "n1"))
    rest = rest_kept + swap(rest_sent, "core")
    half, rest = held(half, rest)
    rest = total_over(rest, ("mid", "blk"))

    skeleton_0, gram, projected_0, kept, sent = level_call(
        first_kernel,
        [VMEM] * 2 + [ANY, ANY],
        [wide, square, tall] + outgoing(levels),
        [s_buf, t_buf(levels), p_buf, sems(2 + levels)],
        3 * 10 ** 9,
        (half, swap(half, "core"), sample, probes),
        in_hbm=2,
    )
    terms = kept + swap(sent, "core")
    terms, rest = held(terms, rest)
    inverse_0 = invert(gram)
    rows_one = total_over(rest, ("n2",))
    pieces = exchange(to_chunks(terms, chips_of(chips[0])), chips[0])
    pieces, inverse_0 = held(pieces, inverse_0)
    inner = chips_of(chips[2])
    places = [(one, two) for one in range(2) for two in range(2) for _ in range(inner)]
    every = range(len(places))
    plan = [(0, [(0, at) for at in every])]
    plan += [(1, [(0, at) for at in every if places[at][0] == one]) for one in range(2)]
    plan += [(2, [(0, at) for at in every if places[at][1] == two]) for two in range(2)]
    sums = swap(combine([pieces], inverse_0, plan), "n0")
    sums, lists, rows_one = held(sums, skeleton_rows, rows_one)
    rest_kept, rest_sent = pick(lists, sample, ((2, 0), (2, 1), (2, 2)), sizes)
    mine = exchange(fan_out(sums, [(0, 2 - one, 4 - two) for one, two in places]), chips[0])
    mine = mine.reshape(samples // 2, levels * skel)
    mine, rest_kept, rest_sent = held(mine, rest_kept, rest_sent)
    other = swap(mine, "core")
    rest = rest_kept + swap(rest_sent, "core")
    mine, other, rest = held(mine, other, rest)
    rest = total_over(rest, ("mid", "blk"))

    coupling_0, e02, skeleton_1, tilt, gram, projected_1, kept, sent = level_call(
        second_kernel,
        [VMEM] * 6 + [ANY] * 3,
        [square, wide, wide, square, square, tall] + outgoing(2),
        [s_buf, t_buf(2), p_buf, p_buf, sems(5)],
        8 * 10 ** 9,
        (mine, other, inverse_0, rows_one, swap(rows_one, "core"), skeleton_0, projected_0, sample, probes),
        in_hbm=5,
    )
    sent, rest = held(sent, rest)
    sent, rows_two = held(sent, rest)
    inverse_1 = invert(gram)
    if chips_of(chips[2]) == 2:
        kept, sent = add_split(kept, swap(sent, "core"), "blk")
        terms = kept + swap(sent, "blk")
        arrived = swap(terms, "n2")
        arrived, inverse_1 = held(arrived, inverse_1)
        plan = [(0, [(0, 0), (1, 0)]), (1, [(1, 0)])]
        sums = swap(combine([terms[None], arrived[None]], inverse_1, plan), "n1")
        mine = fan_out(sums, [(0, 1)])[0]
        beside = swap(mine, "blk")
        parts = (mine, beside, swap(mine, "core"), swap(beside, "core"))
    else:
        terms = kept + swap(sent, "core")
        pieces = exchange(to_chunks(terms, chips_of(chips[1])), chips[1])
        pieces, inverse_1 = held(pieces, inverse_1)
        places = [two for two in range(2) for _ in range(inner)]
        every = range(len(places))
        plan = [(0, [(0, at) for at in every])]
        plan += [(1, [(0, at) for at in every if places[at] == two]) for two in range(2)]
        sums = swap(combine([pieces], inverse_1, plan), "n1")
        mine = exchange(fan_out(sums, [(0, 2 - two) for two in places]), chips[1])
        mine = mine.reshape(samples // 2, 2 * skel)
        parts = (mine, swap(mine, "core"))

    coupling_1, skeleton_2, gram, projected_2, kept, sent = level_call(
        functools.partial(third_kernel, len(parts)),
        [VMEM] * (len(parts) + 7) + [ANY] * 4,
        [square, wide, square, tall] + outgoing(1),
        [s_buf, pltpu.VMEM((row_count, samples), jnp.float32), p_buf, p_buf, p_buf, sems(5)],
        8 * 10 ** 9,
        parts + (inverse_1, rows_two, swap(rows_two, "core"), skeleton_0, skeleton_1, tilt, e02,
                 projected_0, projected_1, sample, probes),
        in_hbm=3,
    )
    inverse_2 = invert(gram)
    terms = kept + swap(sent, "core")
    if chips_of(chips[2]) == 2:
        arrived = swap(terms, "blk")
        arrived, inverse_2 = held(arrived, inverse_2)
        mine = combine([terms[None], arrived[None]], inverse_2, [(0, [(0, 0), (1, 0)])])
    else:
        terms, inverse_2 = held(total_over(terms, chips[2]), inverse_2)
        mine = combine([terms[None]], inverse_2, [(0, [(0, 0)])])
    mine = swap(mine[0], "n2")
    bases, = level_call(
        bases_kernel, [ANY] * 3 + [VMEM] * 3, [arr(levels, row_count, skel)],
        [pltpu.VMEM((levels, row_count, skel), jnp.float32), sems(levels)], 4 * 10 ** 9,
        (projected_0, projected_1, projected_2, inverse_0, inverse_1, inverse_2),
    )
    mine, bases = held(mine, bases)
    other = swap(mine, "core")
    couplings, = level_call(
        last_kernel, [VMEM] * 5, [arr(levels, 1, skel, skel)], [], 5 * 10 ** 9,
        (mine, other, skeleton_2, coupling_0, coupling_1),
    )
    return bases, couplings


def solution(mesh):
    leaves, blocks = mesh.shape["leaf"], mesh.shape["blk"]
    fine = jax.sharding.Mesh(mesh.devices.reshape(2, 2, 2, leaves // 16, 2, blocks), AXES)
    rows = P(None, AXES, None)
    return jax.shard_map(
        local,
        mesh=fine,
        in_specs=(rows, rows, P()),
        out_specs=(rows, P(None, AXES[:-1], None, None)),
        check_vma=False,
    )
```

```python
import functools
import math

import jax
import jax.numpy as jnp
from jax import lax
from jax.experimental import pallas as pl
from jax.experimental.pallas import tpu as pltpu
from jax.sharding import PartitionSpec as P

ridge_term = 0.05
AXES = ("n0", "n1", "n2", "mid", "core", "blk")
TILE = 8
PANEL = 4
WIDTH = 128
VMEM = pl.BlockSpec(memory_space=pltpu.VMEM)
SMEM = pl.BlockSpec(memory_space=pltpu.SMEM)
ANY = pl.BlockSpec(memory_space=pltpu.HBM)
BIG = pltpu.CompilerParams(vmem_limit_bytes=49 * 1024 * 1024)
MIDDLE = pltpu.CompilerParams(vmem_limit_bytes=10 * 1024 * 1024)
SMALL = pltpu.CompilerParams(vmem_limit_bytes=4 * 1024 * 1024)


def arr(*shape):
    return jax.ShapeDtypeStruct(shape, jnp.float32)


def cost(flops, bytes_accessed):
    return pl.CostEstimate(flops=flops, bytes_accessed=bytes_accessed, transcendentals=0)


def split(block):
    high = block.astype(jnp.bfloat16)
    low = (block - high.astype(jnp.float32)).astype(jnp.bfloat16)
    return high, low


def plain_dot(left_side, right_side, left_dim, right_dim):
    return lax.dot_general(
        left_side, right_side, (((left_dim,), (right_dim,)), ((), ())), preferred_element_type=jnp.float32
    )


def split3(block):
    high = block.astype(jnp.bfloat16)
    rest = block - high.astype(jnp.float32)
    middle = rest.astype(jnp.bfloat16)
    return high, middle, (rest - middle.astype(jnp.float32)).astype(jnp.bfloat16)


def stacked_dot(left_parts, right_parts, left_dim, right_dim):
    count = len(left_parts)
    rows = left_parts[0].shape[1 - left_dim]
    total = None
    for at in reversed(range(count)):
        stack = jnp.concatenate(left_parts[:count - at], axis=1 - left_dim)
        block = plain_dot(stack, right_parts[at], left_dim, right_dim)
        for part in reversed(range(count - at)):
            term = block[part * rows:(part + 1) * rows]
            total = term if total is None else total + term
    return total


def dot3(left_side, right_side, left_dim=1, right_dim=0):
    return stacked_dot(split(left_side), split(right_side), left_dim, right_dim)


def dot6(left_side, right_side, left_dim=1, right_dim=0):
    return stacked_dot(split3(left_side), split3(right_side), left_dim, right_dim)


def scales_of(matrix):
    size = matrix.shape[0]
    row = lax.broadcasted_iota(jnp.int32, (size, size), 0)
    col = lax.broadcasted_iota(jnp.int32, (size, size), 1)
    diagonal = jnp.where(row == col, matrix, 0.0)
    along = lax.rsqrt(diagonal.sum(axis=0, keepdims=True))
    down = lax.rsqrt(diagonal.sum(axis=1, keepdims=True))
    return jnp.broadcast_to(down, matrix.shape) * jnp.broadcast_to(along, matrix.shape)


def inverse_of(matrix):
    scales = scales_of(matrix)
    panels = matrix.shape[0] // TILE // PANEL
    return eliminate(matrix * scales, range(panels)) * scales


def eliminate(matrix, panels):
    size = matrix.shape[0]
    count = size // TILE
    wide = PANEL
    shape = (TILE, size)
    lane = lax.broadcasted_iota(jnp.int32, shape, 1)
    sub = lax.broadcasted_iota(jnp.int32, shape, 0)

    def over_lanes(block, at):
        return jnp.broadcast_to(block[:, at:at + 1], shape)

    def over_subs(block, at):
        return jnp.broadcast_to(block[at:at + 1, :], shape)

    rows = [matrix[TILE * i:TILE * (i + 1), :] for i in range(count)]
    for panel_at in [wide * panel for panel in panels]:
        inside = range(panel_at, panel_at + wide)
        for k in inside:
            first = TILE * k
            in_block = (lane >= first) & (lane < first + TILE)
            cols = [over_lanes(rows[k], first + j) for j in range(TILE)]
            panel = jnp.where(in_block, jnp.where(lane - first == sub, 1.0, 0.0), rows[k])
            for j in range(0, TILE, 2):
                one, two = cols[j], cols[j + 1]
                a, b = over_subs(one, j), over_subs(two, j)
                c, d = over_subs(one, j + 1), over_subs(two, j + 1)
                factor = 1.0 / (a * d - b * c)

                def step(block):
                    top, bottom = over_subs(block, j), over_subs(block, j + 1)
                    new_top = d * top - b * bottom
                    new_bottom = a * bottom - c * top
                    others = one * new_top + two * new_bottom
                    kept = jnp.where((sub == j) | (sub == j + 1), 0.0, block)
                    change = jnp.where(sub == j, -new_top, jnp.where(sub == j + 1, -new_bottom, others))
                    return kept - change * factor

                panel = step(panel)
                for m in range(j + 2, TILE):
                    cols[m] = step(cols[m])
            spread_rows = [over_subs(panel, j) for j in range(TILE)]
            for i in inside:
                if i != k:
                    block = rows[i]
                    total = jnp.where(in_block, 0.0, block)
                    for j in range(TILE):
                        total = total - over_lanes(block, first + j) * spread_rows[j]
                    rows[i] = total
            rows[k] = panel
        first, last = TILE * panel_at, TILE * (panel_at + wide)
        in_panel = (lane >= first) & (lane < last)
        zero = jnp.zeros(shape, jnp.float32)
        solved = jnp.concatenate([rows[i] if i in inside else zero for i in range(count)], axis=0)
        ahead = [(panel_at + wide + i) % count for i in range(wide)]
        later = [i for i in range(count) if i not in inside and i not in ahead]
        for chosen in (ahead, later):
            factors = jnp.concatenate([jnp.where(in_panel, rows[i], 0.0) for i in chosen], axis=0)
            change = dot6(factors, solved)
            for at, i in enumerate(chosen):
                rows[i] = jnp.where(in_panel, 0.0, rows[i]) - change[TILE * at:TILE * (at + 1), :]
    return jnp.concatenate(rows, axis=0)


def first_half_kernel(skel_ref, o_ref, scales_ref):
    gram = gram_of(skel_ref[...], skel_ref.shape[1])
    scales = scales_of(gram)
    scales_ref[...] = scales
    o_ref[...] = eliminate(gram * scales, (0, 1))


def second_half_kernel(a_ref, scales_ref, o_ref):
    o_ref[...] = eliminate(a_ref[...], (2, 3)) * scales_ref[...]


def invert_first(skeleton):
    square = arr(skeleton.shape[0], skeleton.shape[0])
    return pl.pallas_call(
        first_half_kernel, out_shape=[square] * 2, in_specs=[VMEM], out_specs=[VMEM] * 2,
        compiler_params=SMALL, cost_estimate=cost(2 * 10 ** 9, 10 ** 5),
    )(skeleton)


def invert_second(state, scales):
    return pl.pallas_call(
        second_half_kernel, out_shape=arr(*state.shape), in_specs=[VMEM] * 2, out_specs=VMEM,
        compiler_params=SMALL, cost_estimate=cost(2 * 10 ** 9, 10 ** 5),
    )(state, scales)


def invert(skeleton):
    return invert_second(*invert_first(skeleton))


def ridge(matrix):
    size = matrix.shape[0]
    row = lax.broadcasted_iota(jnp.int32, (size, size), 0)
    col = lax.broadcasted_iota(jnp.int32, (size, size), 1)
    return matrix + jnp.where(row == col, ridge_term, 0.0)


def marks(list_ref, level, sizes, row_count):
    place = [lax.axis_index(axis) for axis in AXES]
    device = 0
    for index, size in zip(place, sizes):
        device = device * size + index
    node = 0
    for index in place[:level + 1]:
        node = node * 2 + index
    row_total = row_count * math.prod(sizes)
    shift = node * (row_total >> level + 1) - device * row_count
    at = node + (2 ** (level + 1) - 2)
    skel = list_ref.shape[1]
    lane = lax.broadcasted_iota(jnp.int32, (TILE, skel), 1)
    parts = []
    for first in range(0, skel, 16):
        part = jnp.zeros((TILE, skel), jnp.int32)
        for i in range(first, first + 16):
            part = jnp.where(lane == i, list_ref[at, i], part)
        parts.append(part)
    listed = sum(parts)[:1] + shift
    row_ids = lax.broadcasted_iota(jnp.int32, (row_count, listed.shape[1]), 0)
    return jnp.where(row_ids == listed, 1.0, 0.0).astype(jnp.bfloat16)


def taken(mark, parts):
    return sum(plain_dot(mark, part, 0, 0) for part in reversed(parts))


def pick_kernel(wanted, sizes, list_ref, *refs):
    sources, (kept_ref, sent_ref) = refs[:-2], refs[-2:]
    half = kept_ref.shape[1]
    here = lax.axis_index("core") == 0
    mark = marks(list_ref, wanted[0][0], sizes, sources[0].shape[0])
    for slot, source_ref in enumerate(sources):
        rows = taken(mark, split3(source_ref[...]))
        kept_ref[slot] = jnp.where(here, rows[:half], rows[half:])
        sent_ref[slot] = jnp.where(here, rows[half:], rows[:half])


def pick(skeleton_rows, sample, wanted, sizes):
    _, row_count, samples = sample.shape
    skel = skeleton_rows.shape[1]
    count = len(wanted)
    block = (None, row_count, samples)
    specs = [pl.BlockSpec(block, functools.partial(lambda source, step: (source, 0, 0), source)) for _, source in wanted]
    return pl.pallas_call(
        functools.partial(pick_kernel, wanted, sizes),
        out_shape=[arr(count, skel // 2, samples)] * 2,
        grid=(1,),
        in_specs=[SMEM] + specs,
        out_specs=[VMEM] * 2,
        compiler_params=BIG,
        cost_estimate=cost(10 ** 9 * count, count * row_count * samples * 4),
    )(skeleton_rows, *([sample] * count))


def project(sample_block, skeleton, samples, earlier):
    high, low = split(sample_block)
    total = dot3_halves(high, low, skeleton, 1)
    for basis, tilt in earlier:
        total = total - dot3(basis, tilt)
    return total * (1.0 / samples)


def dot3_halves(high, low, skeleton, right_dim):
    width = skeleton.shape[0]
    right_high, right_low = split(skeleton)
    both = plain_dot(high, jnp.concatenate([right_high, right_low], axis=0), 1, right_dim)
    return both[:, :width] + both[:, width:] + plain_dot(low, right_high, 1, right_dim)


def store_terms(kept_ref, sent_ref, kind, term):
    here = lax.axis_index("core") == 0
    half, width = kept_ref.shape[0], term.shape[0]
    turned = term.T
    lanes = pl.ds(kind * width, width)
    kept_ref[:, lanes] = jnp.where(here, turned[:half], turned[half:])
    sent_ref[:, lanes] = jnp.where(here, turned[half:], turned[:half])


def moments(projected, tests):
    return dot3(projected, tests, 0, 0)


def copies(pairs, sems):
    started = []
    for at, (source, target) in enumerate(pairs):
        copy = pltpu.make_async_copy(source, target, sems.at[at])
        copy.start()
        started.append(copy)
    return started


def ordered(mine_ref, other_ref):
    here = lax.axis_index("core") == 0
    low = jnp.where(here, mine_ref[...], other_ref[...])
    high = jnp.where(here, other_ref[...], mine_ref[...])
    return low, high


def joined(low, high, kind):
    return jnp.concatenate([half[:, kind * WIDTH:(kind + 1) * WIDTH] for half in (low, high)], axis=0)


def whole(mine_ref, other_ref):
    return jnp.concatenate(ordered(mine_ref, other_ref), axis=0)


def whole_rows(low, high, slot):
    return jnp.concatenate([low[slot], high[slot]], axis=0)


def couple(skeleton, moment_t):
    spread = ridge(dot6(moment_t, moment_t, 0, 0))
    cross = dot3(skeleton, moment_t)
    return dot3(cross, inverse_of(spread))


def gram_of(skeleton, samples):
    return ridge(dot6(skeleton, skeleton, 1, 1) * (1.0 / samples))


def first_kernel(mine_ref, other_ref, s_hbm, t_hbm, skel_ref, p_hbm, kept_ref, sent_ref,
                 s_buf, t_buf, p_ref, sems):
    samples = mine_ref.shape[1]
    levels = t_buf.shape[0]
    running = copies([(s_hbm.at[0], s_buf)] + [(t_hbm.at[l], t_buf.at[l]) for l in range(levels)], sems)
    skeleton = whole(mine_ref, other_ref)
    skel_ref[...] = skeleton
    running[0].wait()
    projected = project(s_buf[...], skeleton, samples, [])
    p_ref[...] = projected
    leaving = copies([(p_ref, p_hbm)], sems.at[pl.ds(1 + levels, 1)])
    for level in range(levels):
        running[1 + level].wait()
        store_terms(kept_ref, sent_ref, level, moments(projected, t_buf[level]))
    leaving[0].wait()


def second_rows_kernel(rows_mine, rows_other, skel0_ref, low_ref, rows_ref):
    rows_low, rows_high = ordered(rows_mine, rows_other)
    samples = skel0_ref.shape[1]
    low_ref[...] = dot3(whole_rows(rows_low, rows_high, 0), skel0_ref[...], 1, 1) * (1.0 / samples)
    rows_ref[...] = whole_rows(rows_low, rows_high, 1)


def second_kernel(mine_ref, other_ref, ours_ref, low_ref, rows_ref, skel0_ref, p0_hbm, s_hbm, t_hbm,
                  c0_ref, back_ref, skel_ref, tilt_ref, p_hbm, kept_ref, sent_ref, s_buf, t_buf, p_ref, p0_ref, sems):
    samples = skel0_ref.shape[1]
    running = copies([(s_hbm.at[1], s_buf), (p0_hbm, p0_ref), (t_hbm.at[1], t_buf.at[0]), (t_hbm.at[2], t_buf.at[1])], sems)
    low, high = ordered(mine_ref, other_ref)
    coupling = couple(skel0_ref[...], joined(low, high, 0))
    c0_ref[...] = coupling
    back = dot3(ours_ref[...], coupling)
    back_ref[...] = back
    e01 = dot3(back, joined(low, high, 1), 1, 1)
    skeleton = rows_ref[...] - dot3(low_ref[...], e01)
    skel_ref[...] = skeleton
    tilt = dot3(e01, skeleton, 1, 1)
    tilt_ref[...] = tilt
    running[0].wait()
    running[1].wait()
    projected = project(s_buf[...], skeleton, samples, [(p0_ref[...], tilt)])
    p_ref[...] = projected
    leaving = copies([(p_ref, p_hbm)], sems.at[pl.ds(4, 1)])
    for kind in range(2):
        running[2 + kind].wait()
        store_terms(kept_ref, sent_ref, kind, moments(projected, t_buf[kind]))
    leaving[0].wait()


def third_rows_kernel(mine_ref, other_ref, back_ref, rows_mine, rows_other, skel0_ref, skel1_ref, tilt_ref,
                      e02_ref, low_ref, rows_ref):
    share = 1.0 / skel0_ref.shape[1]
    low, high = ordered(mine_ref, other_ref)
    rows_low, rows_high = ordered(rows_mine, rows_other)
    e02 = dot3(back_ref[...], joined(low, high, 2), 1, 1)
    e02_ref[...] = e02
    low_0 = dot3(whole_rows(rows_low, rows_high, 0), skel0_ref[...], 1, 1) * share
    low_ref[...] = (
        dot3(whole_rows(rows_low, rows_high, 1), skel1_ref[...], 1, 1) - dot3(low_0, tilt_ref[...])
    ) * share
    rows_ref[...] = whole_rows(rows_low, rows_high, 2) - dot3(low_0, e02)


def third_kernel(pieces, *refs):
    parts, refs = refs[:pieces], refs[pieces:]
    (ours_ref, rows_ref, low_ref, e02_ref, skel1_ref, p0_hbm, p1_hbm, s_hbm, t_hbm,
     c1_ref, skel_ref, p_hbm, kept_ref, sent_ref, s_buf, t_buf, p_ref, p0_ref, p1_ref, sems) = refs
    samples = skel1_ref.shape[1]
    running = copies([(s_hbm.at[2], s_buf), (p0_hbm, p0_ref), (p1_hbm, p1_ref), (t_hbm.at[2], t_buf)], sems)
    if pieces == 2:
        low, high = ordered(*parts)
    else:
        first = lax.axis_index("blk") == 0
        both = [
            jnp.concatenate([jnp.where(first, one, two), jnp.where(first, two, one)], axis=0)
            for one, two in ((parts[0][...], parts[1][...]), (parts[2][...], parts[3][...]))
        ]
        here = lax.axis_index("core") == 0
        low = jnp.where(here, both[0], both[1])
        high = jnp.where(here, both[1], both[0])
    e02 = e02_ref[...]
    coupling = couple(skel1_ref[...], joined(low, high, 0))
    c1_ref[...] = coupling
    e12 = dot3(dot3(ours_ref[...], coupling), joined(low, high, 1), 1, 1)
    skeleton = rows_ref[...] - dot3(low_ref[...], e12)
    skel_ref[...] = skeleton
    tilt_0 = dot3(e02, skeleton, 1, 1)
    tilt_1 = dot3(e12, skeleton, 1, 1)
    for copy in running[:3]:
        copy.wait()
    projected = project(s_buf[...], skeleton, samples, [(p0_ref[...], tilt_0), (p1_ref[...], tilt_1)])
    p_ref[...] = projected
    leaving = copies([(p_ref, p_hbm)], sems.at[pl.ds(4, 1)])
    running[3].wait()
    store_terms(kept_ref, sent_ref, 0, moments(projected, t_buf[...]))
    leaving[0].wait()


def bases_kernel(p0_hbm, p1_hbm, p2_hbm, inverse_0, inverse_1, inverse_2, out_ref, p_buf, sems):
    running = copies([(source, p_buf.at[at]) for at, source in enumerate((p0_hbm, p1_hbm, p2_hbm))], sems)
    for level, inverse in enumerate((inverse_0, inverse_1, inverse_2)):
        running[level].wait()
        out_ref[level] = dot3(p_buf[level], inverse[...])


def last_kernel(mine_ref, other_ref, skel_ref, c0_ref, c1_ref, out_ref):
    low, high = ordered(mine_ref, other_ref)
    out_ref[0, 0] = c0_ref[...]
    out_ref[1, 0] = c1_ref[...]
    out_ref[2, 0] = couple(skel_ref[...], joined(low, high, 0))


def level_call(kernel, specs, outs, scratch, flops, operands, in_hbm=None):
    return pl.pallas_call(
        kernel,
        out_shape=outs,
        in_specs=specs,
        out_specs=[ANY if at == in_hbm else VMEM for at in range(len(outs))],
        scratch_shapes=scratch,
        compiler_params=BIG,
        cost_estimate=cost(flops, 4 * 10 ** 6),
    )(*operands)


def small_call(kernel, outs, operands):
    return pl.pallas_call(
        kernel,
        out_shape=outs,
        in_specs=[VMEM] * len(operands),
        out_specs=[VMEM] * len(outs),
        compiler_params=MIDDLE,
        cost_estimate=cost(10 ** 9, 10 ** 6),
    )(*operands)


def swap(block, axis):
    return lax.ppermute(block, axis, [(0, 1), (1, 0)])


def cross_swap(block):
    return lax.ppermute(block, ("n1", "n2"), [(0, 3), (1, 2), (2, 1), (3, 0)])


def chips_of(axes):
    return math.prod(lax.axis_size(axis) for axis in axes)


def to_chunks(stack, count):
    rows, width = stack.shape
    return stack.reshape(count, rows // count, width)


def exchange(pieces, axes):
    return lax.all_to_all(pieces, axes, 0, 0, tiled=True)


def total_over(stack, axes):
    for axis in axes:
        count = lax.axis_size(axis)
        if count == 2:
            stack = stack + swap(stack, axis)
        elif count > 2:
            stack = lax.psum(stack, axis)
    return stack


def held(first, *others):
    return lax.optimization_barrier((first,) + others)


def combine_kernel(plan, *refs):
    pieces_refs, inverse_ref, out_ref = refs[:-2], refs[-2], refs[-1]
    inverse = inverse_ref[...]
    for at, (kind, places) in enumerate(plan):
        lanes = slice(kind * WIDTH, (kind + 1) * WIDTH)
        total = sum(pieces_refs[which][place, :, lanes] for which, place in places)
        out_ref[at] = dot3(total, inverse)


def combine(pieces, inverse, plan):
    rows = pieces[0].shape[1]
    return pl.pallas_call(
        functools.partial(combine_kernel, plan),
        out_shape=arr(len(plan), rows, WIDTH),
        in_specs=[VMEM] * (len(pieces) + 1),
        out_specs=VMEM,
        compiler_params=SMALL,
        cost_estimate=cost(10 ** 8, 10 ** 6),
    )(*pieces, inverse)


def add_split_kernel(axis, one_ref, two_ref, kept_ref, sent_ref):
    total = one_ref[...] + two_ref[...]
    half = kept_ref.shape[0]
    first = lax.axis_index(axis) == 0
    kept_ref[...] = jnp.where(first, total[:half], total[half:])
    sent_ref[...] = jnp.where(first, total[half:], total[:half])


def add_split(one, two, axis):
    rows, width = one.shape
    return pl.pallas_call(
        functools.partial(add_split_kernel, axis),
        out_shape=[arr(rows // 2, width)] * 2,
        in_specs=[VMEM] * 2,
        out_specs=[VMEM] * 2,
        compiler_params=SMALL,
        cost_estimate=cost(10 ** 6, 10 ** 6),
    )(one, two)


def fan_kernel(plan, *refs):
    for place, wanted in enumerate(plan):
        for kind, terms in enumerate(wanted):
            total = sum(refs[which][at] for which, at in terms)
            refs[-1][place, :, kind * WIDTH:(kind + 1) * WIDTH] = total


def fan_out(sums, plan):
    rows = sums[0].shape[1]
    return pl.pallas_call(
        functools.partial(fan_kernel, plan),
        out_shape=arr(len(plan), rows, WIDTH * len(plan[0])),
        in_specs=[VMEM] * len(sums),
        out_specs=VMEM,
        compiler_params=SMALL,
        cost_estimate=cost(10 ** 6, 10 ** 6),
    )(*sums)


def local(sample, probes, skeleton_rows):
    levels, row_count, samples = sample.shape
    skel = skeleton_rows.shape[1]
    sizes = [lax.axis_size(axis) for axis in AXES]
    s_buf = pltpu.VMEM((row_count, samples), jnp.float32)
    p_buf = pltpu.VMEM((row_count, skel), jnp.float32)
    square, wide, tall = arr(skel, skel), arr(skel, samples), arr(row_count, skel)

    def t_buf(count):
        return pltpu.VMEM((count, row_count, samples), jnp.float32)

    def sems(count):
        return pltpu.SemaphoreType.DMA((count,))

    def outgoing(kinds):
        return [arr(samples // 2, kinds * skel)] * 2

    chips = [("n1", "n2", "mid", "blk"), ("n2", "mid", "blk"), ("mid", "blk")]
    kept, sent = pick(skeleton_rows, sample, ((0, 0),), sizes)
    half = kept[0] + swap(sent[0], "core")
    half, lists = held(half, skeleton_rows)
    half = total_over(half, ("mid", "blk"))
    rest_kept, rest_sent = pick(lists, sample, ((1, 0), (1, 1)), sizes)
    rest = rest_kept + swap(rest_sent, "core")
    half = half + swap(half, "n2") + swap(half, "n1") + cross_swap(half)
    half_other, rest = held(swap(half, "core"), rest)
    rest = total_over(rest, ("mid", "blk"))

    skeleton_0, projected_0, kept, sent = level_call(
        first_kernel,
        [VMEM] * 2 + [ANY, ANY],
        [wide, tall] + outgoing(levels),
        [s_buf, t_buf(levels), p_buf, sems(2 + levels)],
        3 * 10 ** 9,
        (half, half_other, sample, probes),
        in_hbm=1,
    )
    sent, rest = held(sent, rest)
    terms = kept + swap(sent, "core")
    inverse_0 = invert(skeleton_0)
    rows_one = total_over(rest, ("n2",))
    pieces = exchange(to_chunks(terms, chips_of(chips[0])), chips[0])
    pieces, inverse_0 = held(pieces, inverse_0)
    inner = chips_of(chips[2])
    places = [(one, two) for one in range(2) for two in range(2) for _ in range(inner)]
    every = range(len(places))
    plan = [(0, [(0, at) for at in every])]
    plan += [(1, [(0, at) for at in every if places[at][0] == one]) for one in range(2)]
    plan += [(2, [(0, at) for at in every if places[at][1] == two]) for two in range(2)]
    sums = swap(combine([pieces], inverse_0, plan), "n0")
    sums, lists, rows_one = held(sums, skeleton_rows, rows_one)
    rest_kept, rest_sent = pick(lists, sample, ((2, 0), (2, 1), (2, 2)), sizes)
    mine = exchange(fan_out([sums], [[[(0, at)] for at in (0, 2 - one, 4 - two)] for one, two in places]), chips[0])
    mine = mine.reshape(samples // 2, levels * skel)
    mine, rest_kept, rest_sent = held(mine, rest_kept, rest_sent)
    other = swap(mine, "core")
    rest = rest_kept + swap(rest_sent, "core")
    mine, other, rest = held(mine, other, rest)
    rest = total_over(rest, ("mid", "blk"))

    low, rows_one = small_call(second_rows_kernel, [square, wide], (rows_one, swap(rows_one, "core"), skeleton_0))
    coupling_0, back, skeleton_1, tilt, projected_1, kept, sent = level_call(
        second_kernel,
        [VMEM] * 6 + [ANY] * 3,
        [square, square, wide, square, tall] + outgoing(2),
        [s_buf, t_buf(2), p_buf, p_buf, sems(5)],
        8 * 10 ** 9,
        (mine, other, inverse_0, low, rows_one, skeleton_0, projected_0, sample, probes),
        in_hbm=4,
    )
    sent, rows_two = held(sent, rest)
    rows_two_other = swap(rows_two, "core")
    inverse_1 = invert(skeleton_1)
    before = (mine, other)
    if chips_of(chips[2]) == 2:
        kept, sent = add_split(kept, swap(sent, "core"), "blk")
        arrived = swap(sent, "blk")
        arrived, inverse_1 = held(arrived, inverse_1)
        sums = combine([kept[None], arrived[None]], inverse_1, [(0, [(0, 0), (1, 0)]), (1, [(0, 0), (1, 0)])])
        far, beside = cross_swap(sums), swap(sums[:1], "n1")
        mine = fan_out([far, beside], [[[(0, 0), (1, 0)], [(0, 1)]]])[0]
        mine, rows_two = held(mine, rows_two)
        beside = swap(mine, "blk")
        parts = (mine, beside, swap(mine, "core"), swap(beside, "core"))
    else:
        terms = kept + swap(sent, "core")
        pieces = exchange(to_chunks(terms, chips_of(chips[1])), chips[1])
        pieces, inverse_1 = held(pieces, inverse_1)
        places = [two for two in range(2) for _ in range(inner)]
        every = range(len(places))
        plan = [(0, [(0, at) for at in every])]
        plan += [(1, [(0, at) for at in every if places[at] == two]) for two in range(2)]
        sums = swap(combine([pieces], inverse_1, plan), "n1")
        mine = exchange(fan_out([sums], [[[(0, at)] for at in (0, 2 - two)] for two in places]), chips[1])
        mine = mine.reshape(samples // 2, 2 * skel)
        parts = (mine, swap(mine, "core"))

    e02, low, rows_two = small_call(
        third_rows_kernel,
        [wide, square, wide],
        before + (back, rows_two, rows_two_other, skeleton_0, skeleton_1, tilt),
    )
    coupling_1, skeleton_2, projected_2, kept, sent = level_call(
        functools.partial(third_kernel, len(parts)),
        [VMEM] * (len(parts) + 5) + [ANY] * 4,
        [square, wide, tall] + outgoing(1),
        [s_buf, pltpu.VMEM((row_count, samples), jnp.float32), p_buf, p_buf, p_buf, sems(5)],
        8 * 10 ** 9,
        parts + (inverse_1, rows_two, low, e02, skeleton_1, projected_0, projected_1, sample, probes),
        in_hbm=2,
    )
    inverse_2 = invert(skeleton_2)
    terms = kept + swap(sent, "core")
    if chips_of(chips[2]) == 2:
        arrived = swap(terms, "blk")
        arrived, inverse_2 = held(arrived, inverse_2)
        mine = combine([terms[None], arrived[None]], inverse_2, [(0, [(0, 0), (1, 0)])])
    else:
        terms, inverse_2 = held(total_over(terms, chips[2]), inverse_2)
        mine = combine([terms[None]], inverse_2, [(0, [(0, 0)])])
    mine = swap(mine[0], "n2")
    bases, = level_call(
        bases_kernel, [ANY] * 3 + [VMEM] * 3, [arr(levels, row_count, skel)],
        [pltpu.VMEM((levels, row_count, skel), jnp.float32), sems(levels)], 4 * 10 ** 9,
        (projected_0, projected_1, projected_2, inverse_0, inverse_1, inverse_2),
    )
    mine, bases = held(mine, bases)
    other = swap(mine, "core")
    couplings, = level_call(
        last_kernel, [VMEM] * 5, [arr(levels, 1, skel, skel)], [], 5 * 10 ** 9,
        (mine, other, skeleton_2, coupling_0, coupling_1),
    )
    return bases, couplings


def solution(mesh):
    leaves, blocks = mesh.shape["leaf"], mesh.shape["blk"]
    fine = jax.sharding.Mesh(mesh.devices.reshape(2, 2, 2, leaves // 16, 2, blocks), AXES)
    rows = P(None, AXES, None)
    return jax.shard_map(
        local,
        mesh=fine,
        in_specs=(rows, rows, P()),
        out_specs=(rows, P(None, AXES[:-1], None, None)),
        check_vma=False,
    )
```

```python
import functools
import math

import jax
import jax.numpy as jnp
from jax import lax
from jax.experimental import pallas as pl
from jax.experimental.pallas import tpu as pltpu
from jax.sharding import PartitionSpec as P

ridge_term = 0.05
AXES = ("n0", "n1", "n2", "mid", "core", "blk")
TILE = 8
PANEL = 4
WIDTH = 128
VMEM = pl.BlockSpec(memory_space=pltpu.VMEM)
SMEM = pl.BlockSpec(memory_space=pltpu.SMEM)
ANY = pl.BlockSpec(memory_space=pltpu.HBM)
BIG = pltpu.CompilerParams(vmem_limit_bytes=49 * 1024 * 1024)
MIDDLE = pltpu.CompilerParams(vmem_limit_bytes=10 * 1024 * 1024)
SMALL = pltpu.CompilerParams(vmem_limit_bytes=4 * 1024 * 1024)


def arr(*shape):
    return jax.ShapeDtypeStruct(shape, jnp.float32)


def cost(flops, bytes_accessed):
    return pl.CostEstimate(flops=flops, bytes_accessed=bytes_accessed, transcendentals=0)


def split(block):
    high = block.astype(jnp.bfloat16)
    low = (block - high.astype(jnp.float32)).astype(jnp.bfloat16)
    return high, low


def plain_dot(left_side, right_side, left_dim, right_dim):
    return lax.dot_general(
        left_side, right_side, (((left_dim,), (right_dim,)), ((), ())), preferred_element_type=jnp.float32
    )


def split3(block):
    high = block.astype(jnp.bfloat16)
    rest = block - high.astype(jnp.float32)
    middle = rest.astype(jnp.bfloat16)
    return high, middle, (rest - middle.astype(jnp.float32)).astype(jnp.bfloat16)


def stacked_dot(left_parts, right_parts, left_dim, right_dim):
    count = len(left_parts)
    rows = left_parts[0].shape[1 - left_dim]
    total = None
    for at in reversed(range(count)):
        stack = jnp.concatenate(left_parts[:count - at], axis=1 - left_dim)
        block = plain_dot(stack, right_parts[at], left_dim, right_dim)
        for part in reversed(range(count - at)):
            term = block[part * rows:(part + 1) * rows]
            total = term if total is None else total + term
    return total


def dot3(left_side, right_side, left_dim=1, right_dim=0):
    return stacked_dot(split(left_side), split(right_side), left_dim, right_dim)


def dot6(left_side, right_side, left_dim=1, right_dim=0):
    return stacked_dot(split3(left_side), split3(right_side), left_dim, right_dim)


def scales_of(matrix):
    size = matrix.shape[0]
    row = lax.broadcasted_iota(jnp.int32, (size, size), 0)
    col = lax.broadcasted_iota(jnp.int32, (size, size), 1)
    diagonal = jnp.where(row == col, matrix, 0.0)
    along = lax.rsqrt(diagonal.sum(axis=0, keepdims=True))
    down = lax.rsqrt(diagonal.sum(axis=1, keepdims=True))
    return jnp.broadcast_to(down, matrix.shape) * jnp.broadcast_to(along, matrix.shape)


def inverse_of(matrix):
    scales = scales_of(matrix)
    panels = matrix.shape[0] // TILE // PANEL
    return eliminate(matrix * scales, range(panels)) * scales


def eliminate(matrix, panels):
    size = matrix.shape[0]
    count = size // TILE
    wide = PANEL
    shape = (TILE, size)
    lane = lax.broadcasted_iota(jnp.int32, shape, 1)
    sub = lax.broadcasted_iota(jnp.int32, shape, 0)

    def over_lanes(block, at):
        return jnp.broadcast_to(block[:, at:at + 1], shape)

    def over_subs(block, at):
        return jnp.broadcast_to(block[at:at + 1, :], shape)

    rows = [matrix[TILE * i:TILE * (i + 1), :] for i in range(count)]
    for panel_at in [wide * panel for panel in panels]:
        inside = range(panel_at, panel_at + wide)
        for k in inside:
            first = TILE * k
            in_block = (lane >= first) & (lane < first + TILE)
            cols = [over_lanes(rows[k], first + j) for j in range(TILE)]
            panel = jnp.where(in_block, jnp.where(lane - first == sub, 1.0, 0.0), rows[k])
            for j in range(0, TILE, 2):
                one, two = cols[j], cols[j + 1]
                a, b = over_subs(one, j), over_subs(two, j)
                c, d = over_subs(one, j + 1), over_subs(two, j + 1)
                factor = 1.0 / (a * d - b * c)

                def step(block):
                    top, bottom = over_subs(block, j), over_subs(block, j + 1)
                    new_top = d * top - b * bottom
                    new_bottom = a * bottom - c * top
                    others = one * new_top + two * new_bottom
                    kept = jnp.where((sub == j) | (sub == j + 1), 0.0, block)
                    change = jnp.where(sub == j, -new_top, jnp.where(sub == j + 1, -new_bottom, others))
                    return kept - change * factor

                panel = step(panel)
                for m in range(j + 2, TILE):
                    cols[m] = step(cols[m])
            spread_rows = [over_subs(panel, j) for j in range(TILE)]
            for i in inside:
                if i != k:
                    block = rows[i]
                    total = jnp.where(in_block, 0.0, block)
                    for j in range(TILE):
                        total = total - over_lanes(block, first + j) * spread_rows[j]
                    rows[i] = total
            rows[k] = panel
        first, last = TILE * panel_at, TILE * (panel_at + wide)
        in_panel = (lane >= first) & (lane < last)
        zero = jnp.zeros(shape, jnp.float32)
        solved = jnp.concatenate([rows[i] if i in inside else zero for i in range(count)], axis=0)
        ahead = [(panel_at + wide + i) % count for i in range(wide)]
        later = [i for i in range(count) if i not in inside and i not in ahead]
        for chosen in (ahead, later):
            factors = jnp.concatenate([jnp.where(in_panel, rows[i], 0.0) for i in chosen], axis=0)
            change = dot6(factors, solved)
            for at, i in enumerate(chosen):
                rows[i] = jnp.where(in_panel, 0.0, rows[i]) - change[TILE * at:TILE * (at + 1), :]
    return jnp.concatenate(rows, axis=0)


def first_half_kernel(skel_ref, o_ref, scales_ref):
    gram = gram_of(skel_ref[...], skel_ref.shape[1])
    scales = scales_of(gram)
    scales_ref[...] = scales
    o_ref[...] = eliminate(gram * scales, (0, 1))


def second_half_kernel(a_ref, scales_ref, o_ref):
    o_ref[...] = eliminate(a_ref[...], (2, 3)) * scales_ref[...]


def invert_first(skeleton):
    square = arr(skeleton.shape[0], skeleton.shape[0])
    return pl.pallas_call(
        first_half_kernel, out_shape=[square] * 2, in_specs=[VMEM], out_specs=[VMEM] * 2,
        compiler_params=SMALL, cost_estimate=cost(10 ** 8, 10 ** 5),
    )(skeleton)


def invert_second(state, scales):
    return pl.pallas_call(
        second_half_kernel, out_shape=arr(*state.shape), in_specs=[VMEM] * 2, out_specs=VMEM,
        compiler_params=SMALL, cost_estimate=cost(10 ** 8, 10 ** 5),
    )(state, scales)


def invert(skeleton):
    return invert_second(*invert_first(skeleton))


def ridge(matrix):
    size = matrix.shape[0]
    row = lax.broadcasted_iota(jnp.int32, (size, size), 0)
    col = lax.broadcasted_iota(jnp.int32, (size, size), 1)
    return matrix + jnp.where(row == col, ridge_term, 0.0)


def marks(list_ref, level, sizes, row_count):
    place = [lax.axis_index(axis) for axis in AXES]
    device = 0
    for index, size in zip(place, sizes):
        device = device * size + index
    node = 0
    for index in place[:level + 1]:
        node = node * 2 + index
    row_total = row_count * math.prod(sizes)
    shift = node * (row_total >> level + 1) - device * row_count
    at = node + (2 ** (level + 1) - 2)
    skel = list_ref.shape[1]
    lane = lax.broadcasted_iota(jnp.int32, (TILE, skel), 1)
    parts = []
    for first in range(0, skel, 16):
        part = jnp.zeros((TILE, skel), jnp.int32)
        for i in range(first, first + 16):
            part = jnp.where(lane == i, list_ref[at, i], part)
        parts.append(part)
    listed = sum(parts)[:1] + shift
    row_ids = lax.broadcasted_iota(jnp.int32, (row_count, listed.shape[1]), 0)
    return jnp.where(row_ids == listed, 1.0, 0.0).astype(jnp.bfloat16)


def taken(mark, parts):
    return sum(plain_dot(mark, part, 0, 0) for part in reversed(parts))


def pick_kernel(wanted, sizes, list_ref, *refs):
    sources, (kept_ref, sent_ref) = refs[:-2], refs[-2:]
    half = kept_ref.shape[1]
    here = lax.axis_index("core") == 0
    mark = marks(list_ref, wanted[0][0], sizes, sources[0].shape[0])
    for slot, source_ref in enumerate(sources):
        rows = taken(mark, split3(source_ref[...]))
        kept_ref[slot] = jnp.where(here, rows[:half], rows[half:])
        sent_ref[slot] = jnp.where(here, rows[half:], rows[:half])


def pick(skeleton_rows, sample, wanted, sizes):
    _, row_count, samples = sample.shape
    skel = skeleton_rows.shape[1]
    count = len(wanted)
    block = (None, row_count, samples)
    specs = [pl.BlockSpec(block, functools.partial(lambda source, step: (source, 0, 0), source)) for _, source in wanted]
    return pl.pallas_call(
        functools.partial(pick_kernel, wanted, sizes),
        out_shape=[arr(count, skel // 2, samples)] * 2,
        grid=(1,),
        in_specs=[SMEM] + specs,
        out_specs=[VMEM] * 2,
        compiler_params=BIG,
        cost_estimate=cost(10 ** 9 * count, count * row_count * samples * 4),
    )(skeleton_rows, *([sample] * count))


def project(sample_block, skeleton, samples, earlier):
    high, low = split(sample_block)
    total = dot3_halves(high, low, skeleton, 1)
    for basis, tilt in earlier:
        total = total - dot3(basis, tilt)
    return total * (1.0 / samples)


def dot3_halves(high, low, skeleton, right_dim):
    width = skeleton.shape[0]
    right_high, right_low = split(skeleton)
    both = plain_dot(high, jnp.concatenate([right_high, right_low], axis=0), 1, right_dim)
    return both[:, :width] + both[:, width:] + plain_dot(low, right_high, 1, right_dim)


def store_terms(kept_ref, sent_ref, kind, term):
    here = lax.axis_index("core") == 0
    half, width = kept_ref.shape[0], term.shape[0]
    turned = term.T
    lanes = pl.ds(kind * width, width)
    kept_ref[:, lanes] = jnp.where(here, turned[:half], turned[half:])
    sent_ref[:, lanes] = jnp.where(here, turned[half:], turned[:half])


def moments(projected, tests):
    return dot3(projected, tests, 0, 0)


def copies(pairs, sems):
    started = []
    for at, (source, target) in enumerate(pairs):
        copy = pltpu.make_async_copy(source, target, sems.at[at])
        copy.start()
        started.append(copy)
    return started


def ordered(mine_ref, other_ref):
    here = lax.axis_index("core") == 0
    low = jnp.where(here, mine_ref[...], other_ref[...])
    high = jnp.where(here, other_ref[...], mine_ref[...])
    return low, high


def ordered_pairs(parts, axis):
    first = lax.axis_index("blk") == 0
    near, far = [
        jnp.concatenate([jnp.where(first, one, two), jnp.where(first, two, one)], axis=axis)
        for one, two in ((parts[0][...], parts[1][...]), (parts[2][...], parts[3][...]))
    ]
    here = lax.axis_index("core") == 0
    return jnp.where(here, near, far), jnp.where(here, far, near)


def joined(low, high, kind):
    return jnp.concatenate([half[:, kind * WIDTH:(kind + 1) * WIDTH] for half in (low, high)], axis=0)


def whole(mine_ref, other_ref):
    return jnp.concatenate(ordered(mine_ref, other_ref), axis=0)


def whole_rows(low, high, slot):
    return jnp.concatenate([low[slot], high[slot]], axis=0)


def couple(skeleton, moment_t):
    spread = ridge(dot6(moment_t, moment_t, 0, 0))
    cross = dot3(skeleton, moment_t)
    return dot3(cross, inverse_of(spread))


def gram_of(skeleton, samples):
    return ridge(dot6(skeleton, skeleton, 1, 1) * (1.0 / samples))


def first_kernel(mine_ref, other_ref, s_hbm, t_hbm, skel_ref, p_hbm, kept_ref, sent_ref,
                 s_buf, t_buf, p_ref, sems):
    samples = mine_ref.shape[1]
    levels = t_buf.shape[0]
    running = copies([(s_hbm.at[0], s_buf)] + [(t_hbm.at[l], t_buf.at[l]) for l in range(levels)], sems)
    skeleton = whole(mine_ref, other_ref)
    skel_ref[...] = skeleton
    running[0].wait()
    projected = project(s_buf[...], skeleton, samples, [])
    p_ref[...] = projected
    leaving = copies([(p_ref, p_hbm)], sems.at[pl.ds(1 + levels, 1)])
    for level in range(levels):
        running[1 + level].wait()
        store_terms(kept_ref, sent_ref, level, moments(projected, t_buf[level]))
    leaving[0].wait()


def second_rows_kernel(*refs):
    parts, (skel0_ref, low_ref, rows_ref) = refs[:-3], refs[-3:]
    rows_low, rows_high = ordered(*parts) if len(parts) == 2 else ordered_pairs(parts, 1)
    samples = skel0_ref.shape[1]
    low_ref[...] = dot3(whole_rows(rows_low, rows_high, 0), skel0_ref[...], 1, 1) * (1.0 / samples)
    rows_ref[...] = whole_rows(rows_low, rows_high, 1)


def second_kernel(mine_ref, other_ref, ours_ref, low_ref, rows_ref, skel0_ref, p0_hbm, s_hbm, t_hbm,
                  c0_ref, back_ref, skel_ref, tilt_ref, p_hbm, kept_ref, sent_ref, s_buf, t_buf, p_ref, p0_ref, sems):
    samples = skel0_ref.shape[1]
    running = copies([(s_hbm.at[1], s_buf), (p0_hbm, p0_ref), (t_hbm.at[1], t_buf.at[0]), (t_hbm.at[2], t_buf.at[1])], sems)
    low, high = ordered(mine_ref, other_ref)
    coupling = couple(skel0_ref[...], joined(low, high, 0))
    c0_ref[...] = coupling
    back = dot3(ours_ref[...], coupling)
    back_ref[...] = back
    e01 = dot3(back, joined(low, high, 1), 1, 1)
    skeleton = rows_ref[...] - dot3(low_ref[...], e01)
    skel_ref[...] = skeleton
    tilt = dot3(e01, skeleton, 1, 1)
    tilt_ref[...] = tilt
    running[0].wait()
    running[1].wait()
    projected = project(s_buf[...], skeleton, samples, [(p0_ref[...], tilt)])
    p_ref[...] = projected
    leaving = copies([(p_ref, p_hbm)], sems.at[pl.ds(4, 1)])
    for kind in range(2):
        running[2 + kind].wait()
        store_terms(kept_ref, sent_ref, kind, moments(projected, t_buf[kind]))
    leaving[0].wait()


def third_rows_kernel(mine_ref, other_ref, back_ref, rows_mine, rows_other, last_mine, last_other,
                      skel0_ref, skel1_ref, tilt_ref, e02_ref, low_ref, rows_ref):
    share = 1.0 / skel0_ref.shape[1]
    low, high = ordered(mine_ref, other_ref)
    rows_low, rows_high = ordered(rows_mine, rows_other)
    e02 = dot3(back_ref[...], joined(low, high, 2), 1, 1)
    e02_ref[...] = e02
    low_0 = dot3(whole_rows(rows_low, rows_high, 0), skel0_ref[...], 1, 1) * share
    low_ref[...] = (
        dot3(whole_rows(rows_low, rows_high, 1), skel1_ref[...], 1, 1) - dot3(low_0, tilt_ref[...])
    ) * share
    rows_ref[...] = whole_rows(*ordered(last_mine, last_other), 0) - dot3(low_0, e02)


def third_kernel(pieces, *refs):
    parts, refs = refs[:pieces], refs[pieces:]
    (ours_ref, rows_ref, low_ref, e02_ref, skel1_ref, p0_hbm, p1_hbm, s_hbm, t_hbm,
     c1_ref, skel_ref, p_hbm, kept_ref, sent_ref, s_buf, t_buf, p_ref, p0_ref, p1_ref, sems) = refs
    samples = skel1_ref.shape[1]
    running = copies([(s_hbm.at[2], s_buf), (p0_hbm, p0_ref), (p1_hbm, p1_ref), (t_hbm.at[2], t_buf)], sems)
    low, high = ordered(*parts) if pieces == 2 else ordered_pairs(parts, 0)
    e02 = e02_ref[...]
    coupling = couple(skel1_ref[...], joined(low, high, 0))
    c1_ref[...] = coupling
    e12 = dot3(dot3(ours_ref[...], coupling), joined(low, high, 1), 1, 1)
    skeleton = rows_ref[...] - dot3(low_ref[...], e12)
    skel_ref[...] = skeleton
    tilt_0 = dot3(e02, skeleton, 1, 1)
    tilt_1 = dot3(e12, skeleton, 1, 1)
    for copy in running[:3]:
        copy.wait()
    projected = project(s_buf[...], skeleton, samples, [(p0_ref[...], tilt_0), (p1_ref[...], tilt_1)])
    p_ref[...] = projected
    leaving = copies([(p_ref, p_hbm)], sems.at[pl.ds(4, 1)])
    running[3].wait()
    store_terms(kept_ref, sent_ref, 0, moments(projected, t_buf[...]))
    leaving[0].wait()


def bases_kernel(p0_hbm, p1_hbm, p2_hbm, inverse_0, inverse_1, inverse_2, out_ref, p_buf, sems):
    running = copies([(source, p_buf.at[at]) for at, source in enumerate((p0_hbm, p1_hbm, p2_hbm))], sems)
    for level, inverse in enumerate((inverse_0, inverse_1, inverse_2)):
        running[level].wait()
        out_ref[level] = dot3(p_buf[level], inverse[...])


def last_kernel(mine_ref, other_ref, skel_ref, c0_ref, c1_ref, out_ref):
    low, high = ordered(mine_ref, other_ref)
    out_ref[0, 0] = c0_ref[...]
    out_ref[1, 0] = c1_ref[...]
    out_ref[2, 0] = couple(skel_ref[...], joined(low, high, 0))


def level_call(kernel, specs, outs, scratch, flops, operands, in_hbm=None):
    return pl.pallas_call(
        kernel,
        out_shape=outs,
        in_specs=specs,
        out_specs=[ANY if at == in_hbm else VMEM for at in range(len(outs))],
        scratch_shapes=scratch,
        compiler_params=BIG,
        cost_estimate=cost(flops, 4 * 10 ** 6),
    )(*operands)


def small_call(kernel, outs, operands):
    return pl.pallas_call(
        kernel,
        out_shape=outs,
        in_specs=[VMEM] * len(operands),
        out_specs=[VMEM] * len(outs),
        compiler_params=MIDDLE,
        cost_estimate=cost(10 ** 9, 10 ** 6),
    )(*operands)


def swap(block, axis):
    return lax.ppermute(block, axis, [(0, 1), (1, 0)])


def cross_swap(block):
    return lax.ppermute(block, ("n1", "n2"), [(0, 3), (1, 2), (2, 1), (3, 0)])


def chips_of(axes):
    return math.prod(lax.axis_size(axis) for axis in axes)


def to_chunks(stack, count):
    rows, width = stack.shape
    return stack.reshape(count, rows // count, width)


def exchange(pieces, axes):
    return lax.all_to_all(pieces, axes, 0, 0, tiled=True)


def total_over(stack, axes):
    for axis in axes:
        count = lax.axis_size(axis)
        if count == 2:
            stack = stack + swap(stack, axis)
        elif count > 2:
            stack = lax.psum(stack, axis)
    return stack


def held(first, *others):
    return lax.optimization_barrier((first,) + others)


def combine_kernel(plan, *refs):
    pieces_refs, inverse_ref, out_ref = refs[:-2], refs[-2], refs[-1]
    inverse = inverse_ref[...]
    for at, (kind, places) in enumerate(plan):
        lanes = slice(kind * WIDTH, (kind + 1) * WIDTH)
        total = sum(pieces_refs[which][place, :, lanes] for which, place in places)
        out_ref[at] = dot3(total, inverse)


def combine(pieces, inverse, plan):
    rows = pieces[0].shape[1]
    return pl.pallas_call(
        functools.partial(combine_kernel, plan),
        out_shape=arr(len(plan), rows, WIDTH),
        in_specs=[VMEM] * (len(pieces) + 1),
        out_specs=VMEM,
        compiler_params=SMALL,
        cost_estimate=cost(10 ** 8, 10 ** 6),
    )(*pieces, inverse)


def add_split_kernel(axis, one_ref, two_ref, kept_ref, sent_ref):
    half = kept_ref.shape[-2]
    first = lax.axis_index(axis) == 0
    for at in range(kept_ref.shape[0]):
        total = one_ref[at] + two_ref[at]
        kept_ref[at] = jnp.where(first, total[:half], total[half:])
        sent_ref[at] = jnp.where(first, total[half:], total[:half])


def add_split(one, two, axis):
    count, rows, width = one.shape
    return pl.pallas_call(
        functools.partial(add_split_kernel, axis),
        out_shape=[arr(count, rows // 2, width)] * 2,
        in_specs=[VMEM] * 2,
        out_specs=[VMEM] * 2,
        compiler_params=SMALL,
        cost_estimate=cost(10 ** 6, 10 ** 6),
    )(one, two)


def fan_kernel(plan, *refs):
    for place, wanted in enumerate(plan):
        for kind, terms in enumerate(wanted):
            total = sum(refs[which][at] for which, at in terms)
            refs[-1][place, :, kind * WIDTH:(kind + 1) * WIDTH] = total


def fan_out(sums, plan):
    rows = sums[0].shape[1]
    return pl.pallas_call(
        functools.partial(fan_kernel, plan),
        out_shape=arr(len(plan), rows, WIDTH * len(plan[0])),
        in_specs=[VMEM] * len(sums),
        out_specs=VMEM,
        compiler_params=SMALL,
        cost_estimate=cost(10 ** 6, 10 ** 6),
    )(*sums)


def local(sample, probes, skeleton_rows):
    levels, row_count, samples = sample.shape
    skel = skeleton_rows.shape[1]
    sizes = [lax.axis_size(axis) for axis in AXES]
    s_buf = pltpu.VMEM((row_count, samples), jnp.float32)
    p_buf = pltpu.VMEM((row_count, skel), jnp.float32)
    square, wide, tall = arr(skel, skel), arr(skel, samples), arr(row_count, skel)

    def t_buf(count):
        return pltpu.VMEM((count, row_count, samples), jnp.float32)

    def sems(count):
        return pltpu.SemaphoreType.DMA((count,))

    def outgoing(kinds):
        return [arr(samples // 2, kinds * skel)] * 2

    chips = [("n1", "n2", "mid", "blk"), ("n2", "mid", "blk"), ("mid", "blk")]
    kept, sent = pick(skeleton_rows, sample, ((0, 0),), sizes)
    half = kept[0] + swap(sent[0], "core")
    half, lists = held(half, skeleton_rows)
    half = total_over(half, ("mid", "blk"))
    rest_kept, rest_sent = pick(lists, sample, ((1, 0), (1, 1)), sizes)
    half = half + swap(half, "n2") + swap(half, "n1") + cross_swap(half)
    pairs = chips_of(chips[2]) == 2
    if pairs:
        rest, moved = add_split(rest_kept, swap(rest_sent, "core"), "blk")
        half_other, rest, moved = held(swap(half, "core"), rest, moved)
        moved = swap(moved, "blk")
    else:
        rest = rest_kept + swap(rest_sent, "core")
        half_other, rest = held(swap(half, "core"), rest)
        moved = total_over(rest, ("mid", "blk"))

    skeleton_0, projected_0, kept, sent = level_call(
        first_kernel,
        [VMEM] * 2 + [ANY, ANY],
        [wide, tall] + outgoing(levels),
        [s_buf, t_buf(levels), p_buf, sems(2 + levels)],
        3 * 10 ** 9,
        (half, half_other, sample, probes),
        in_hbm=1,
    )
    sent, moved = held(sent, moved)
    received, skeleton_in = held(swap(sent, "core"), skeleton_0)
    inverse_0 = invert(skeleton_in)
    terms = kept + received
    rows_one = total_over(rest + moved if pairs else moved, ("n2",))
    pieces = exchange(to_chunks(terms, chips_of(chips[0])), chips[0])
    pieces, inverse_0 = held(pieces, inverse_0)
    inner = chips_of(chips[2])
    places = [(one, two) for one in range(2) for two in range(2) for _ in range(inner)]
    every = range(len(places))
    plan = [(0, [(0, at) for at in every])]
    plan += [(1, [(0, at) for at in every if places[at][0] == one]) for one in range(2)]
    plan += [(2, [(0, at) for at in every if places[at][1] == two]) for two in range(2)]
    sums = swap(combine([pieces], inverse_0, plan), "n0")
    sums, lists, rows_one = held(sums, skeleton_rows, rows_one)
    rest_kept, rest_sent = pick(lists, sample, ((2, 0), (2, 1), (2, 2)), sizes)
    mine = exchange(fan_out([sums], [[[(0, at)] for at in (0, 2 - one, 4 - two)] for one, two in places]), chips[0])
    mine = mine.reshape(samples // 2, levels * skel)
    mine, rest_kept, rest_sent = held(mine, rest_kept, rest_sent)
    other = swap(mine, "core")
    rest_sent = swap(rest_sent, "core")
    rest, last = rest_kept[:2] + rest_sent[:2], rest_kept[2:] + rest_sent[2:]
    mine, other, rest = held(mine, other, rest)
    rest = total_over(rest, ("mid", "blk"))

    row_parts = (rows_one, swap(rows_one, "blk")) if pairs else (rows_one,)
    row_parts += tuple(swap(part, "core") for part in row_parts)
    low, rows_one = small_call(second_rows_kernel, [square, wide], row_parts + (skeleton_0,))
    coupling_0, back, skeleton_1, tilt, projected_1, kept, sent = level_call(
        second_kernel,
        [VMEM] * 6 + [ANY] * 3,
        [square, square, wide, square, tall] + outgoing(2),
        [s_buf, t_buf(2), p_buf, p_buf, sems(5)],
        8 * 10 ** 9,
        (mine, other, inverse_0, low, rows_one, skeleton_0, projected_0, sample, probes),
        in_hbm=4,
    )
    sent, rows_two = held(sent, rest)
    rows_two_other = swap(rows_two, "core")
    before = (mine, other)
    received, skeleton_in = held(swap(sent, "core"), skeleton_1)
    inverse_1 = invert(skeleton_in)
    if pairs:
        kept, sent = [part[0] for part in add_split(kept[None], received[None], "blk")]
        arrived = swap(sent, "blk")
        arrived, inverse_1, last = held(arrived, inverse_1, last)
        sums = combine([kept[None], arrived[None]], inverse_1, [(0, [(0, 0), (1, 0)]), (1, [(0, 0), (1, 0)])])
        far, beside = cross_swap(sums), swap(sums[:1], "n1")
        mine = fan_out([far, beside], [[[(0, 0), (1, 0)], [(0, 1)]]])[0]
        last = total_over(last, ("blk",))
        mine, rows_two, last = held(mine, rows_two, last)
        beside = swap(mine, "blk")
        parts = (mine, beside, swap(mine, "core"), swap(beside, "core"))
    else:
        last = total_over(last, ("mid", "blk"))
        pieces = exchange(to_chunks(kept + received, chips_of(chips[1])), chips[1])
        pieces, inverse_1 = held(pieces, inverse_1)
        places = [two for two in range(2) for _ in range(inner)]
        every = range(len(places))
        plan = [(0, [(0, at) for at in every])]
        plan += [(1, [(0, at) for at in every if places[at] == two]) for two in range(2)]
        sums = swap(combine([pieces], inverse_1, plan), "n1")
        mine = exchange(fan_out([sums], [[[(0, at)] for at in (0, 2 - two)] for two in places]), chips[1])
        mine = mine.reshape(samples // 2, 2 * skel)
        parts = (mine, swap(mine, "core"))

    e02, low, rows_two = small_call(
        third_rows_kernel,
        [wide, square, wide],
        before + (back, rows_two, rows_two_other, last, swap(last, "core"), skeleton_0, skeleton_1, tilt),
    )
    coupling_1, skeleton_2, projected_2, kept, sent = level_call(
        functools.partial(third_kernel, len(parts)),
        [VMEM] * (len(parts) + 5) + [ANY] * 4,
        [square, wide, tall] + outgoing(1),
        [s_buf, pltpu.VMEM((row_count, samples), jnp.float32), p_buf, p_buf, p_buf, sems(5)],
        8 * 10 ** 9,
        parts + (inverse_1, rows_two, low, e02, skeleton_1, projected_0, projected_1, sample, probes),
        in_hbm=2,
    )
    received, skeleton_in = held(swap(sent, "core"), skeleton_2)
    inverse_2 = invert(skeleton_in)
    terms = kept + received
    if pairs:
        arrived = swap(terms, "blk")
        arrived, inverse_2 = held(arrived, inverse_2)
        mine = combine([terms[None], arrived[None]], inverse_2, [(0, [(0, 0), (1, 0)])])
    else:
        terms, inverse_2 = held(total_over(terms, chips[2]), inverse_2)
        mine = combine([terms[None]], inverse_2, [(0, [(0, 0)])])
    mine = swap(mine[0], "n2")
    bases, = level_call(
        bases_kernel, [ANY] * 3 + [VMEM] * 3, [arr(levels, row_count, skel)],
        [pltpu.VMEM((levels, row_count, skel), jnp.float32), sems(levels)], 4 * 10 ** 9,
        (projected_0, projected_1, projected_2, inverse_0, inverse_1, inverse_2),
    )
    mine, bases = held(mine, bases)
    other = swap(mine, "core")
    couplings, = level_call(
        last_kernel, [VMEM] * 5, [arr(levels, 1, skel, skel)], [], 5 * 10 ** 9,
        (mine, other, skeleton_2, coupling_0, coupling_1),
    )
    return bases, couplings


def solution(mesh):
    leaves, blocks = mesh.shape["leaf"], mesh.shape["blk"]
    fine = jax.sharding.Mesh(mesh.devices.reshape(2, 2, 2, leaves // 16, 2, blocks), AXES)
    rows = P(None, AXES, None)
    return jax.shard_map(
        local,
        mesh=fine,
        in_specs=(rows, rows, P()),
        out_specs=(rows, P(None, AXES[:-1], None, None)),
        check_vma=False,
    )
```

```python
import functools
import math

import jax
import jax.numpy as jnp
from jax import lax
from jax.experimental import pallas as pl
from jax.experimental.pallas import tpu as pltpu
from jax.sharding import PartitionSpec as P

ridge_term = 0.05
AXES = ("n0", "n1", "n2", "mid", "core", "blk")
TILE = 8
PANEL = 4
WIDTH = 128
VMEM = pl.BlockSpec(memory_space=pltpu.VMEM)
SMEM = pl.BlockSpec(memory_space=pltpu.SMEM)
ANY = pl.BlockSpec(memory_space=pltpu.HBM)
BIG = pltpu.CompilerParams(vmem_limit_bytes=49 * 1024 * 1024)
MIDDLE = pltpu.CompilerParams(vmem_limit_bytes=10 * 1024 * 1024)
SMALL = pltpu.CompilerParams(vmem_limit_bytes=4 * 1024 * 1024)


def arr(*shape):
    return jax.ShapeDtypeStruct(shape, jnp.float32)


def cost(flops, bytes_accessed):
    return pl.CostEstimate(flops=flops, bytes_accessed=bytes_accessed, transcendentals=0)


def split(block):
    high = block.astype(jnp.bfloat16)
    low = (block - high.astype(jnp.float32)).astype(jnp.bfloat16)
    return high, low


def plain_dot(left_side, right_side, left_dim, right_dim):
    return lax.dot_general(
        left_side, right_side, (((left_dim,), (right_dim,)), ((), ())), preferred_element_type=jnp.float32
    )


def split3(block):
    high = block.astype(jnp.bfloat16)
    rest = block - high.astype(jnp.float32)
    middle = rest.astype(jnp.bfloat16)
    return high, middle, (rest - middle.astype(jnp.float32)).astype(jnp.bfloat16)


def stacked_dot(left_parts, right_parts, left_dim, right_dim):
    count = len(left_parts)
    rows = left_parts[0].shape[1 - left_dim]
    total = None
    for at in reversed(range(count)):
        stack = jnp.concatenate(left_parts[:count - at], axis=1 - left_dim)
        block = plain_dot(stack, right_parts[at], left_dim, right_dim)
        for part in reversed(range(count - at)):
            term = block[part * rows:(part + 1) * rows]
            total = term if total is None else total + term
    return total


def dot3(left_side, right_side, left_dim=1, right_dim=0):
    return stacked_dot(split(left_side), split(right_side), left_dim, right_dim)


def dot6(left_side, right_side, left_dim=1, right_dim=0):
    return stacked_dot(split3(left_side), split3(right_side), left_dim, right_dim)


def scales_of(matrix):
    size = matrix.shape[0]
    row = lax.broadcasted_iota(jnp.int32, (size, size), 0)
    col = lax.broadcasted_iota(jnp.int32, (size, size), 1)
    diagonal = jnp.where(row == col, matrix, 0.0)
    along = lax.rsqrt(diagonal.sum(axis=0, keepdims=True))
    down = lax.rsqrt(diagonal.sum(axis=1, keepdims=True))
    return jnp.broadcast_to(down, matrix.shape) * jnp.broadcast_to(along, matrix.shape)


def inverse_of(matrix):
    scales = scales_of(matrix)
    panels = matrix.shape[0] // TILE // PANEL
    return eliminate(matrix * scales, range(panels)) * scales


def eliminate(matrix, panels):
    size = matrix.shape[0]
    count = size // TILE
    wide = PANEL
    shape = (TILE, size)
    lane = lax.broadcasted_iota(jnp.int32, shape, 1)
    sub = lax.broadcasted_iota(jnp.int32, shape, 0)

    def over_lanes(block, at):
        return jnp.broadcast_to(block[:, at:at + 1], shape)

    def over_subs(block, at):
        return jnp.broadcast_to(block[at:at + 1, :], shape)

    rows = [matrix[TILE * i:TILE * (i + 1), :] for i in range(count)]
    for panel_at in [wide * panel for panel in panels]:
        inside = range(panel_at, panel_at + wide)
        for k in inside:
            first = TILE * k
            in_block = (lane >= first) & (lane < first + TILE)
            cols = [over_lanes(rows[k], first + j) for j in range(TILE)]
            panel = jnp.where(in_block, jnp.where(lane - first == sub, 1.0, 0.0), rows[k])
            for j in range(0, TILE, 2):
                one, two = cols[j], cols[j + 1]
                a, b = over_subs(one, j), over_subs(two, j)
                c, d = over_subs(one, j + 1), over_subs(two, j + 1)
                factor = 1.0 / (a * d - b * c)

                def step(block):
                    top, bottom = over_subs(block, j), over_subs(block, j + 1)
                    new_top = d * top - b * bottom
                    new_bottom = a * bottom - c * top
                    others = one * new_top + two * new_bottom
                    kept = jnp.where((sub == j) | (sub == j + 1), 0.0, block)
                    change = jnp.where(sub == j, -new_top, jnp.where(sub == j + 1, -new_bottom, others))
                    return kept - change * factor

                panel = step(panel)
                for m in range(j + 2, TILE):
                    cols[m] = step(cols[m])
            spread_rows = [over_subs(panel, j) for j in range(TILE)]
            for i in inside:
                if i != k:
                    block = rows[i]
                    total = jnp.where(in_block, 0.0, block)
                    for j in range(TILE):
                        total = total - over_lanes(block, first + j) * spread_rows[j]
                    rows[i] = total
            rows[k] = panel
        first, last = TILE * panel_at, TILE * (panel_at + wide)
        in_panel = (lane >= first) & (lane < last)
        zero = jnp.zeros(shape, jnp.float32)
        solved = jnp.concatenate([rows[i] if i in inside else zero for i in range(count)], axis=0)
        ahead = [(panel_at + wide + i) % count for i in range(wide)]
        later = [i for i in range(count) if i not in inside and i not in ahead]
        for chosen in (ahead, later):
            factors = jnp.concatenate([jnp.where(in_panel, rows[i], 0.0) for i in chosen], axis=0)
            change = dot6(factors, solved)
            for at, i in enumerate(chosen):
                rows[i] = jnp.where(in_panel, 0.0, rows[i]) - change[TILE * at:TILE * (at + 1), :]
    return jnp.concatenate(rows, axis=0)


def first_half_kernel(skel_ref, o_ref, scales_ref):
    gram = gram_of(skel_ref[...], skel_ref.shape[1])
    scales = scales_of(gram)
    scales_ref[...] = scales
    o_ref[...] = eliminate(gram * scales, (0, 1))


def second_half_kernel(a_ref, scales_ref, o_ref):
    o_ref[...] = eliminate(a_ref[...], (2, 3)) * scales_ref[...]


def invert_first(skeleton):
    square = arr(skeleton.shape[0], skeleton.shape[0])
    return pl.pallas_call(
        first_half_kernel, out_shape=[square] * 2, in_specs=[VMEM], out_specs=[VMEM] * 2,
        compiler_params=SMALL, cost_estimate=cost(10 ** 8, 10 ** 5),
    )(skeleton)


def invert_second(state, scales):
    return pl.pallas_call(
        second_half_kernel, out_shape=arr(*state.shape), in_specs=[VMEM] * 2, out_specs=VMEM,
        compiler_params=SMALL, cost_estimate=cost(10 ** 8, 10 ** 5),
    )(state, scales)


def invert(skeleton):
    return invert_second(*invert_first(skeleton))


def ridge(matrix):
    size = matrix.shape[0]
    row = lax.broadcasted_iota(jnp.int32, (size, size), 0)
    col = lax.broadcasted_iota(jnp.int32, (size, size), 1)
    return matrix + jnp.where(row == col, ridge_term, 0.0)


def marks(list_ref, level, sizes, row_count):
    place = [lax.axis_index(axis) for axis in AXES]
    device = 0
    for index, size in zip(place, sizes):
        device = device * size + index
    node = 0
    for index in place[:level + 1]:
        node = node * 2 + index
    row_total = row_count * math.prod(sizes)
    shift = node * (row_total >> level + 1) - device * row_count
    at = node + (2 ** (level + 1) - 2)
    skel = list_ref.shape[1]
    lane = lax.broadcasted_iota(jnp.int32, (TILE, skel), 1)
    parts = []
    for first in range(0, skel, 16):
        part = jnp.zeros((TILE, skel), jnp.int32)
        for i in range(first, first + 16):
            part = jnp.where(lane == i, list_ref[at, i], part)
        parts.append(part)
    listed = sum(parts)[:1] + shift
    row_ids = lax.broadcasted_iota(jnp.int32, (row_count, listed.shape[1]), 0)
    return jnp.where(row_ids == listed, 1.0, 0.0).astype(jnp.bfloat16)


def taken(mark, parts):
    return sum(plain_dot(mark, part, 0, 0) for part in reversed(parts))


def pick_kernel(wanted, sizes, list_ref, *refs):
    sources, (kept_ref, sent_ref) = refs[:-2], refs[-2:]
    half = kept_ref.shape[1]
    here = lax.axis_index("core") == 0
    mark = marks(list_ref, wanted[0][0], sizes, sources[0].shape[0])
    for slot, source_ref in enumerate(sources):
        rows = taken(mark, split3(source_ref[...]))
        kept_ref[slot] = jnp.where(here, rows[:half], rows[half:])
        sent_ref[slot] = jnp.where(here, rows[half:], rows[:half])


def pick(skeleton_rows, sample, wanted, sizes):
    _, row_count, samples = sample.shape
    skel = skeleton_rows.shape[1]
    count = len(wanted)
    block = (None, row_count, samples)
    specs = [pl.BlockSpec(block, functools.partial(lambda source, step: (source, 0, 0), source)) for _, source in wanted]
    return pl.pallas_call(
        functools.partial(pick_kernel, wanted, sizes),
        out_shape=[arr(count, skel // 2, samples)] * 2,
        grid=(1,),
        in_specs=[SMEM] + specs,
        out_specs=[VMEM] * 2,
        compiler_params=BIG,
        cost_estimate=cost(10 ** 9 * count, count * row_count * samples * 4),
    )(skeleton_rows, *([sample] * count))


def project(sample_block, skeleton, samples, earlier):
    high, low = split(sample_block)
    total = dot3_halves(high, low, skeleton, 1)
    for basis, tilt in earlier:
        total = total - dot3(basis, tilt)
    return total * (1.0 / samples)


def dot3_halves(high, low, skeleton, right_dim):
    width = skeleton.shape[0]
    right_high, right_low = split(skeleton)
    both = plain_dot(high, jnp.concatenate([right_high, right_low], axis=0), 1, right_dim)
    return both[:, :width] + both[:, width:] + plain_dot(low, right_high, 1, right_dim)


def store_terms(kept_ref, sent_ref, kind, term):
    here = lax.axis_index("core") == 0
    half, width = kept_ref.shape[0], term.shape[0]
    turned = term.T
    lanes = pl.ds(kind * width, width)
    kept_ref[:, lanes] = jnp.where(here, turned[:half], turned[half:])
    sent_ref[:, lanes] = jnp.where(here, turned[half:], turned[:half])


def moments(projected, tests):
    return dot3(projected, tests, 0, 0)


def copies(pairs, sems):
    started = []
    for at, (source, target) in enumerate(pairs):
        copy = pltpu.make_async_copy(source, target, sems.at[at])
        copy.start()
        started.append(copy)
    return started


def ordered(mine_ref, other_ref):
    here = lax.axis_index("core") == 0
    low = jnp.where(here, mine_ref[...], other_ref[...])
    high = jnp.where(here, other_ref[...], mine_ref[...])
    return low, high


def ordered_pairs(parts, axis):
    first = lax.axis_index("blk") == 0
    near, far = [
        jnp.concatenate([jnp.where(first, one, two), jnp.where(first, two, one)], axis=axis)
        for one, two in ((parts[0][...], parts[1][...]), (parts[2][...], parts[3][...]))
    ]
    here = lax.axis_index("core") == 0
    return jnp.where(here, near, far), jnp.where(here, far, near)


def joined(low, high, kind):
    return jnp.concatenate([half[:, kind * WIDTH:(kind + 1) * WIDTH] for half in (low, high)], axis=0)


def whole(mine_ref, other_ref):
    return jnp.concatenate(ordered(mine_ref, other_ref), axis=0)


def whole_rows(low, high, slot):
    return jnp.concatenate([low[slot], high[slot]], axis=0)


def couple(skeleton, moment_t):
    spread = ridge(dot6(moment_t, moment_t, 0, 0))
    cross = dot3(skeleton, moment_t)
    return dot3(cross, inverse_of(spread))


def gram_of(skeleton, samples):
    return ridge(dot6(skeleton, skeleton, 1, 1) * (1.0 / samples))


def first_kernel(mine_ref, other_ref, s_hbm, t_hbm, skel_ref, p_hbm, kept_ref, sent_ref,
                 s_buf, t_buf, p_ref, sems):
    samples = mine_ref.shape[1]
    levels = t_buf.shape[0]
    running = copies([(s_hbm.at[0], s_buf)] + [(t_hbm.at[l], t_buf.at[l]) for l in range(levels)], sems)
    skeleton = whole(mine_ref, other_ref)
    skel_ref[...] = skeleton
    running[0].wait()
    projected = project(s_buf[...], skeleton, samples, [])
    p_ref[...] = projected
    leaving = copies([(p_ref, p_hbm)], sems.at[pl.ds(1 + levels, 1)])
    for level in range(levels):
        running[1 + level].wait()
        store_terms(kept_ref, sent_ref, level, moments(projected, t_buf[level]))
    leaving[0].wait()


def second_rows_kernel(*refs):
    parts, (skel0_ref, low_ref, rows_ref) = refs[:-3], refs[-3:]
    rows_low, rows_high = ordered(*parts) if len(parts) == 2 else ordered_pairs(parts, 1)
    samples = skel0_ref.shape[1]
    low_ref[...] = dot3(whole_rows(rows_low, rows_high, 0), skel0_ref[...], 1, 1) * (1.0 / samples)
    rows_ref[...] = whole_rows(rows_low, rows_high, 1)


def second_kernel(mine_ref, other_ref, ours_ref, low_ref, rows_ref, skel0_ref, p0_hbm, s_hbm, t_hbm,
                  c0_ref, back_ref, skel_ref, tilt_ref, p_hbm, kept_ref, sent_ref, s_buf, t_buf, p_ref, p0_ref, sems):
    samples = skel0_ref.shape[1]
    running = copies([(s_hbm.at[1], s_buf), (p0_hbm, p0_ref), (t_hbm.at[1], t_buf.at[0]), (t_hbm.at[2], t_buf.at[1])], sems)
    low, high = ordered(mine_ref, other_ref)
    coupling = couple(skel0_ref[...], joined(low, high, 0))
    c0_ref[...] = coupling
    back = dot3(ours_ref[...], coupling)
    back_ref[...] = back
    e01 = dot3(back, joined(low, high, 1), 1, 1)
    skeleton = rows_ref[...] - dot3(low_ref[...], e01)
    skel_ref[...] = skeleton
    tilt = dot3(e01, skeleton, 1, 1)
    tilt_ref[...] = tilt
    running[0].wait()
    running[1].wait()
    projected = project(s_buf[...], skeleton, samples, [(p0_ref[...], tilt)])
    p_ref[...] = projected
    leaving = copies([(p_ref, p_hbm)], sems.at[pl.ds(4, 1)])
    for kind in range(2):
        running[2 + kind].wait()
        store_terms(kept_ref, sent_ref, kind, moments(projected, t_buf[kind]))
    leaving[0].wait()


def third_rows_kernel(mine_ref, other_ref, back_ref, rows_mine, rows_other, last_mine, last_other,
                      skel0_ref, skel1_ref, tilt_ref, e02_ref, low_ref, rows_ref):
    share = 1.0 / skel0_ref.shape[1]
    low, high = ordered(mine_ref, other_ref)
    rows_low, rows_high = ordered(rows_mine, rows_other)
    e02 = dot3(back_ref[...], joined(low, high, 2), 1, 1)
    e02_ref[...] = e02
    low_0 = dot3(whole_rows(rows_low, rows_high, 0), skel0_ref[...], 1, 1) * share
    low_ref[...] = (
        dot3(whole_rows(rows_low, rows_high, 1), skel1_ref[...], 1, 1) - dot3(low_0, tilt_ref[...])
    ) * share
    rows_ref[...] = whole_rows(*ordered(last_mine, last_other), 0) - dot3(low_0, e02)


def third_kernel(pieces, *refs):
    parts, refs = refs[:pieces], refs[pieces:]
    (ours_ref, rows_ref, low_ref, e02_ref, skel1_ref, p0_hbm, p1_hbm, s_hbm, t_hbm,
     c1_ref, skel_ref, p_hbm, kept_ref, sent_ref, s_buf, t_buf, p_ref, p0_ref, p1_ref, sems) = refs
    samples = skel1_ref.shape[1]
    running = copies([(s_hbm.at[2], s_buf), (p0_hbm, p0_ref), (p1_hbm, p1_ref), (t_hbm.at[2], t_buf)], sems)
    low, high = ordered(*parts) if pieces == 2 else ordered_pairs(parts, 0)
    e02 = e02_ref[...]
    coupling = couple(skel1_ref[...], joined(low, high, 0))
    c1_ref[...] = coupling
    e12 = dot3(dot3(ours_ref[...], coupling), joined(low, high, 1), 1, 1)
    skeleton = rows_ref[...] - dot3(low_ref[...], e12)
    skel_ref[...] = skeleton
    tilt_0 = dot3(e02, skeleton, 1, 1)
    tilt_1 = dot3(e12, skeleton, 1, 1)
    for copy in running[:3]:
        copy.wait()
    projected = project(s_buf[...], skeleton, samples, [(p0_ref[...], tilt_0), (p1_ref[...], tilt_1)])
    p_ref[...] = projected
    leaving = copies([(p_ref, p_hbm)], sems.at[pl.ds(4, 1)])
    running[3].wait()
    store_terms(kept_ref, sent_ref, 0, moments(projected, t_buf[...]))
    leaving[0].wait()


def bases_kernel(p0_hbm, p1_hbm, p2_hbm, inverse_0, inverse_1, inverse_2, out_ref, p_buf, sems):
    running = copies([(source, p_buf.at[at]) for at, source in enumerate((p0_hbm, p1_hbm, p2_hbm))], sems)
    for level, inverse in enumerate((inverse_0, inverse_1, inverse_2)):
        running[level].wait()
        out_ref[level] = dot3(p_buf[level], inverse[...])


def last_kernel(mine_ref, other_ref, skel_ref, c0_ref, c1_ref, out_ref):
    low, high = ordered(mine_ref, other_ref)
    out_ref[0, 0] = c0_ref[...]
    out_ref[1, 0] = c1_ref[...]
    out_ref[2, 0] = couple(skel_ref[...], joined(low, high, 0))


def level_call(kernel, specs, outs, scratch, flops, operands, in_hbm=None):
    return pl.pallas_call(
        kernel,
        out_shape=outs,
        in_specs=specs,
        out_specs=[ANY if at == in_hbm else VMEM for at in range(len(outs))],
        scratch_shapes=scratch,
        compiler_params=BIG,
        cost_estimate=cost(flops, 4 * 10 ** 6),
    )(*operands)


def small_call(kernel, outs, operands):
    return pl.pallas_call(
        kernel,
        out_shape=outs,
        in_specs=[VMEM] * len(operands),
        out_specs=[VMEM] * len(outs),
        compiler_params=MIDDLE,
        cost_estimate=cost(10 ** 9, 10 ** 6),
    )(*operands)


def swap(block, axis):
    return lax.ppermute(block, axis, [(0, 1), (1, 0)])


def cross_swap(block):
    return lax.ppermute(block, ("n1", "n2"), [(0, 3), (1, 2), (2, 1), (3, 0)])


def chips_of(axes):
    return math.prod(lax.axis_size(axis) for axis in axes)


def to_chunks(stack, count):
    rows, width = stack.shape
    return stack.reshape(count, rows // count, width)


def exchange(pieces, axes):
    return lax.all_to_all(pieces, axes, 0, 0, tiled=True)


def total_over(stack, axes):
    for axis in axes:
        count = lax.axis_size(axis)
        if count == 2:
            stack = stack + swap(stack, axis)
        elif count > 2:
            stack = lax.psum(stack, axis)
    return stack


def held(first, *others):
    return lax.optimization_barrier((first,) + others)


def combine_kernel(plan, *refs):
    pieces_refs, inverse_ref, out_ref = refs[:-2], refs[-2], refs[-1]
    inverse = inverse_ref[...]
    for at, (kind, places) in enumerate(plan):
        lanes = slice(kind * WIDTH, (kind + 1) * WIDTH)
        total = sum(pieces_refs[which][place, :, lanes] for which, place in places)
        out_ref[at] = dot3(total, inverse)


def combine(pieces, inverse, plan):
    rows = pieces[0].shape[1]
    return pl.pallas_call(
        functools.partial(combine_kernel, plan),
        out_shape=arr(len(plan), rows, WIDTH),
        in_specs=[VMEM] * (len(pieces) + 1),
        out_specs=VMEM,
        compiler_params=SMALL,
        cost_estimate=cost(10 ** 8, 10 ** 6),
    )(*pieces, inverse)


def add_split_kernel(axis, one_ref, two_ref, kept_ref, sent_ref):
    half = kept_ref.shape[-2]
    first = lax.axis_index(axis) == 0
    for at in range(kept_ref.shape[0]):
        total = one_ref[at] + two_ref[at]
        kept_ref[at] = jnp.where(first, total[:half], total[half:])
        sent_ref[at] = jnp.where(first, total[half:], total[:half])


def add_split(one, two, axis):
    count, rows, width = one.shape
    return pl.pallas_call(
        functools.partial(add_split_kernel, axis),
        out_shape=[arr(count, rows // 2, width)] * 2,
        in_specs=[VMEM] * 2,
        out_specs=[VMEM] * 2,
        compiler_params=SMALL,
        cost_estimate=cost(10 ** 6, 10 ** 6),
    )(one, two)


def fan_kernel(plan, *refs):
    for place, wanted in enumerate(plan):
        for kind, terms in enumerate(wanted):
            total = sum(refs[which][at] for which, at in terms)
            refs[-1][place, :, kind * WIDTH:(kind + 1) * WIDTH] = total


def fan_out(sums, plan):
    rows = sums[0].shape[1]
    return pl.pallas_call(
        functools.partial(fan_kernel, plan),
        out_shape=arr(len(plan), rows, WIDTH * len(plan[0])),
        in_specs=[VMEM] * len(sums),
        out_specs=VMEM,
        compiler_params=SMALL,
        cost_estimate=cost(10 ** 6, 10 ** 6),
    )(*sums)


def local(sample, probes, skeleton_rows):
    levels, row_count, samples = sample.shape
    skel = skeleton_rows.shape[1]
    sizes = [lax.axis_size(axis) for axis in AXES]
    s_buf = pltpu.VMEM((row_count, samples), jnp.float32)
    p_buf = pltpu.VMEM((row_count, skel), jnp.float32)
    square, wide, tall = arr(skel, skel), arr(skel, samples), arr(row_count, skel)

    def t_buf(count):
        return pltpu.VMEM((count, row_count, samples), jnp.float32)

    def sems(count):
        return pltpu.SemaphoreType.DMA((count,))

    def outgoing(kinds):
        return [arr(samples // 2, kinds * skel)] * 2

    chips = [("n1", "n2", "mid", "blk"), ("n2", "mid", "blk"), ("mid", "blk")]
    kept, sent = pick(skeleton_rows, sample, ((0, 0),), sizes)
    half = kept[0] + swap(sent[0], "core")
    half, lists = held(half, skeleton_rows)
    half = total_over(half, ("mid", "blk"))
    rest_kept, rest_sent = pick(lists, sample, ((1, 0), (1, 1)), sizes)
    half = half + swap(half, "n2") + swap(half, "n1") + cross_swap(half)
    pairs = chips_of(chips[2]) == 2
    if pairs:
        rest, moved = add_split(rest_kept, swap(rest_sent, "core"), "blk")
        half_other, rest, moved = held(swap(half, "core"), rest, moved)
        moved = swap(moved, "blk")
    else:
        rest = rest_kept + swap(rest_sent, "core")
        half_other, rest = held(swap(half, "core"), rest)
        moved = total_over(rest, ("mid", "blk"))

    skeleton_0, projected_0, kept, sent = level_call(
        first_kernel,
        [VMEM] * 2 + [ANY, ANY],
        [wide, tall] + outgoing(levels),
        [s_buf, t_buf(levels), p_buf, sems(2 + levels)],
        3 * 10 ** 9,
        (half, half_other, sample, probes),
        in_hbm=1,
    )
    sent, moved = held(sent, moved)
    received, skeleton_in = held(swap(sent, "core"), skeleton_0)
    inverse_0 = invert(skeleton_in)
    terms = kept + received
    rows_one = total_over(rest + moved if pairs else moved, ("n2",))
    pieces = exchange(to_chunks(terms, chips_of(chips[0])), chips[0])
    pieces, inverse_0 = held(pieces, inverse_0)
    inner = chips_of(chips[2])
    places = [(one, two) for one in range(2) for two in range(2) for _ in range(inner)]
    every = range(len(places))
    plan = [(0, [(0, at) for at in every])]
    plan += [(1, [(0, at) for at in every if places[at][0] == one]) for one in range(2)]
    plan += [(2, [(0, at) for at in every if places[at][1] == two]) for two in range(2)]
    sums = swap(combine([pieces], inverse_0, plan), "n0")
    sums, lists, rows_one = held(sums, skeleton_rows, rows_one)
    rest_kept, rest_sent = pick(lists, sample, ((2, 0), (2, 1), (2, 2)), sizes)
    mine = exchange(fan_out([sums], [[[(0, at)] for at in (0, 2 - one, 4 - two)] for one, two in places]), chips[0])
    mine = mine.reshape(samples // 2, levels * skel)
    row_parts = (rows_one, swap(rows_one, "blk")) if pairs else (rows_one,)
    mine, rest_kept, rest_sent, *row_parts = held(mine, rest_kept, rest_sent, *row_parts)
    other = swap(mine, "core")
    rest_sent = swap(rest_sent, "core")
    rest, last = rest_kept[:2] + rest_sent[:2], rest_kept[2:] + rest_sent[2:]
    mine, other, rest = held(mine, other, rest)
    rest = total_over(rest, ("mid", "blk"))

    row_parts += [swap(part, "core") for part in row_parts]
    low, rows_one = small_call(second_rows_kernel, [square, wide], (*row_parts, skeleton_0))
    coupling_0, back, skeleton_1, tilt, projected_1, kept, sent = level_call(
        second_kernel,
        [VMEM] * 6 + [ANY] * 3,
        [square, square, wide, square, tall] + outgoing(2),
        [s_buf, t_buf(2), p_buf, p_buf, sems(5)],
        8 * 10 ** 9,
        (mine, other, inverse_0, low, rows_one, skeleton_0, projected_0, sample, probes),
        in_hbm=4,
    )
    sent, rows_two = held(sent, rest)
    rows_two_other = swap(rows_two, "core")
    before = (mine, other)
    received, skeleton_in = held(swap(sent, "core"), skeleton_1)
    inverse_1 = invert(skeleton_in)
    if pairs:
        kept, sent = [part[0] for part in add_split(kept[None], received[None], "blk")]
        arrived = swap(sent, "blk")
        arrived, inverse_1, last = held(arrived, inverse_1, last)
        sums = combine([kept[None], arrived[None]], inverse_1, [(0, [(0, 0), (1, 0)]), (1, [(0, 0), (1, 0)])])
        far, beside = cross_swap(sums), swap(sums[:1], "n1")
        mine = fan_out([far, beside], [[[(0, 0), (1, 0)], [(0, 1)]]])[0]
        last = total_over(last, ("blk",))
        mine, rows_two, last = held(mine, rows_two, last)
        beside = swap(mine, "blk")
        parts = (mine, beside, swap(mine, "core"), swap(beside, "core"))
    else:
        last = total_over(last, ("mid", "blk"))
        pieces = exchange(to_chunks(kept + received, chips_of(chips[1])), chips[1])
        pieces, inverse_1 = held(pieces, inverse_1)
        places = [two for two in range(2) for _ in range(inner)]
        every = range(len(places))
        plan = [(0, [(0, at) for at in every])]
        plan += [(1, [(0, at) for at in every if places[at] == two]) for two in range(2)]
        sums = swap(combine([pieces], inverse_1, plan), "n1")
        mine = exchange(fan_out([sums], [[[(0, at)] for at in (0, 2 - two)] for two in places]), chips[1])
        mine = mine.reshape(samples // 2, 2 * skel)
        parts = (mine, swap(mine, "core"))

    e02, low, rows_two = small_call(
        third_rows_kernel,
        [wide, square, wide],
        before + (back, rows_two, rows_two_other, last, swap(last, "core"), skeleton_0, skeleton_1, tilt),
    )
    coupling_1, skeleton_2, projected_2, kept, sent = level_call(
        functools.partial(third_kernel, len(parts)),
        [VMEM] * (len(parts) + 5) + [ANY] * 4,
        [square, wide, tall] + outgoing(1),
        [s_buf, pltpu.VMEM((row_count, samples), jnp.float32), p_buf, p_buf, p_buf, sems(5)],
        8 * 10 ** 9,
        parts + (inverse_1, rows_two, low, e02, skeleton_1, projected_0, projected_1, sample, probes),
        in_hbm=2,
    )
    received, skeleton_in = held(swap(sent, "core"), skeleton_2)
    inverse_2 = invert(skeleton_in)
    terms = kept + received
    if pairs:
        arrived = swap(terms, "blk")
        arrived, inverse_2 = held(arrived, inverse_2)
        mine = combine([terms[None], arrived[None]], inverse_2, [(0, [(0, 0), (1, 0)])])
    else:
        terms, inverse_2 = held(total_over(terms, chips[2]), inverse_2)
        mine = combine([terms[None]], inverse_2, [(0, [(0, 0)])])
    mine = swap(mine[0], "n2")
    bases, = level_call(
        bases_kernel, [ANY] * 3 + [VMEM] * 3, [arr(levels, row_count, skel)],
        [pltpu.VMEM((levels, row_count, skel), jnp.float32), sems(levels)], 4 * 10 ** 9,
        (projected_0, projected_1, projected_2, inverse_0, inverse_1, inverse_2),
    )
    mine, bases = held(mine, bases)
    other = swap(mine, "core")
    couplings, = level_call(
        last_kernel, [VMEM] * 5, [arr(levels, 1, skel, skel)], [], 5 * 10 ** 9,
        (mine, other, skeleton_2, coupling_0, coupling_1),
    )
    return bases, couplings


def solution(mesh):
    leaves, blocks = mesh.shape["leaf"], mesh.shape["blk"]
    fine = jax.sharding.Mesh(mesh.devices.reshape(2, 2, 2, leaves // 16, 2, blocks), AXES)
    rows = P(None, AXES, None)
    return jax.shard_map(
        local,
        mesh=fine,
        in_specs=(rows, rows, P()),
        out_specs=(rows, P(None, AXES[:-1], None, None)),
        check_vma=False,
    )
```

```python
import functools
import math

import jax
import jax.numpy as jnp
from jax import lax
from jax.experimental import pallas as pl
from jax.experimental.pallas import tpu as pltpu
from jax.sharding import PartitionSpec as P

ridge_term = 0.05
AXES = ("n0", "n1", "n2", "mid", "core", "blk")
TILE = 8
PANEL = 4
WIDTH = 128
VMEM = pl.BlockSpec(memory_space=pltpu.VMEM)
SMEM = pl.BlockSpec(memory_space=pltpu.SMEM)
ANY = pl.BlockSpec(memory_space=pltpu.HBM)
BIG = pltpu.CompilerParams(vmem_limit_bytes=49 * 1024 * 1024)
MIDDLE = pltpu.CompilerParams(vmem_limit_bytes=10 * 1024 * 1024)
SMALL = pltpu.CompilerParams(vmem_limit_bytes=4 * 1024 * 1024)


def arr(*shape):
    return jax.ShapeDtypeStruct(shape, jnp.float32)


def cost(flops, bytes_accessed):
    return pl.CostEstimate(flops=flops, bytes_accessed=bytes_accessed, transcendentals=0)


def split(block):
    high = block.astype(jnp.bfloat16)
    low = (block - high.astype(jnp.float32)).astype(jnp.bfloat16)
    return high, low


def plain_dot(left_side, right_side, left_dim, right_dim):
    return lax.dot_general(
        left_side, right_side, (((left_dim,), (right_dim,)), ((), ())), preferred_element_type=jnp.float32
    )


def split3(block):
    high = block.astype(jnp.bfloat16)
    rest = block - high.astype(jnp.float32)
    middle = rest.astype(jnp.bfloat16)
    return high, middle, (rest - middle.astype(jnp.float32)).astype(jnp.bfloat16)


def stacked_dot(left_parts, right_parts, left_dim, right_dim):
    count = len(left_parts)
    rows = left_parts[0].shape[1 - left_dim]
    total = None
    for at in reversed(range(count)):
        stack = jnp.concatenate(left_parts[:count - at], axis=1 - left_dim)
        block = plain_dot(stack, right_parts[at], left_dim, right_dim)
        for part in reversed(range(count - at)):
            term = block[part * rows:(part + 1) * rows]
            total = term if total is None else total + term
    return total


def dot3(left_side, right_side, left_dim=1, right_dim=0):
    return stacked_dot(split(left_side), split(right_side), left_dim, right_dim)


def dot6(left_side, right_side, left_dim=1, right_dim=0):
    return stacked_dot(split3(left_side), split3(right_side), left_dim, right_dim)


def scales_of(matrix):
    size = matrix.shape[0]
    row = lax.broadcasted_iota(jnp.int32, (size, size), 0)
    col = lax.broadcasted_iota(jnp.int32, (size, size), 1)
    diagonal = jnp.where(row == col, matrix, 0.0)
    along = lax.rsqrt(diagonal.sum(axis=0, keepdims=True))
    down = lax.rsqrt(diagonal.sum(axis=1, keepdims=True))
    return jnp.broadcast_to(down, matrix.shape) * jnp.broadcast_to(along, matrix.shape)


def inverse_of(matrix):
    scales = scales_of(matrix)
    panels = matrix.shape[0] // TILE // PANEL
    return eliminate(matrix * scales, range(panels)) * scales


def eliminate(matrix, panels):
    size = matrix.shape[0]
    count = size // TILE
    wide = PANEL
    shape = (TILE, size)
    lane = lax.broadcasted_iota(jnp.int32, shape, 1)
    sub = lax.broadcasted_iota(jnp.int32, shape, 0)

    def over_lanes(block, at):
        return jnp.broadcast_to(block[:, at:at + 1], shape)

    def over_subs(block, at):
        return jnp.broadcast_to(block[at:at + 1, :], shape)

    rows = [matrix[TILE * i:TILE * (i + 1), :] for i in range(count)]
    for panel_at in [wide * panel for panel in panels]:
        inside = range(panel_at, panel_at + wide)
        for k in inside:
            first = TILE * k
            in_block = (lane >= first) & (lane < first + TILE)
            cols = [over_lanes(rows[k], first + j) for j in range(TILE)]
            panel = jnp.where(in_block, jnp.where(lane - first == sub, 1.0, 0.0), rows[k])
            for j in range(0, TILE, 2):
                one, two = cols[j], cols[j + 1]
                a, b = over_subs(one, j), over_subs(two, j)
                c, d = over_subs(one, j + 1), over_subs(two, j + 1)
                factor = 1.0 / (a * d - b * c)

                def step(block):
                    top, bottom = over_subs(block, j), over_subs(block, j + 1)
                    new_top = d * top - b * bottom
                    new_bottom = a * bottom - c * top
                    others = one * new_top + two * new_bottom
                    kept = jnp.where((sub == j) | (sub == j + 1), 0.0, block)
                    change = jnp.where(sub == j, -new_top, jnp.where(sub == j + 1, -new_bottom, others))
                    return kept - change * factor

                panel = step(panel)
                for m in range(j + 2, TILE):
                    cols[m] = step(cols[m])
            spread_rows = [over_subs(panel, j) for j in range(TILE)]
            for i in inside:
                if i != k:
                    block = rows[i]
                    total = jnp.where(in_block, 0.0, block)
                    for j in range(TILE):
                        total = total - over_lanes(block, first + j) * spread_rows[j]
                    rows[i] = total
            rows[k] = panel
        first, last = TILE * panel_at, TILE * (panel_at + wide)
        in_panel = (lane >= first) & (lane < last)
        zero = jnp.zeros(shape, jnp.float32)
        solved = jnp.concatenate([rows[i] if i in inside else zero for i in range(count)], axis=0)
        ahead = [(panel_at + wide + i) % count for i in range(wide)]
        later = [i for i in range(count) if i not in inside and i not in ahead]
        for chosen in (ahead, later):
            factors = jnp.concatenate([jnp.where(in_panel, rows[i], 0.0) for i in chosen], axis=0)
            change = dot6(factors, solved)
            for at, i in enumerate(chosen):
                rows[i] = jnp.where(in_panel, 0.0, rows[i]) - change[TILE * at:TILE * (at + 1), :]
    return jnp.concatenate(rows, axis=0)


def first_half_kernel(skel_ref, o_ref, scales_ref):
    gram = gram_of(skel_ref[...], skel_ref.shape[1])
    scales = scales_of(gram)
    scales_ref[...] = scales
    o_ref[...] = eliminate(gram * scales, (0, 1))


def second_half_kernel(a_ref, scales_ref, o_ref):
    o_ref[...] = eliminate(a_ref[...], (2, 3)) * scales_ref[...]


def invert_first(skeleton):
    square = arr(skeleton.shape[0], skeleton.shape[0])
    return pl.pallas_call(
        first_half_kernel, out_shape=[square] * 2, in_specs=[VMEM], out_specs=[VMEM] * 2,
        compiler_params=SMALL, cost_estimate=cost(10 ** 8, 10 ** 5),
    )(skeleton)


def invert_second(state, scales):
    return pl.pallas_call(
        second_half_kernel, out_shape=arr(*state.shape), in_specs=[VMEM] * 2, out_specs=VMEM,
        compiler_params=SMALL, cost_estimate=cost(10 ** 8, 10 ** 5),
    )(state, scales)


def invert(skeleton):
    return invert_second(*invert_first(skeleton))


def ridge(matrix):
    size = matrix.shape[0]
    row = lax.broadcasted_iota(jnp.int32, (size, size), 0)
    col = lax.broadcasted_iota(jnp.int32, (size, size), 1)
    return matrix + jnp.where(row == col, ridge_term, 0.0)


def marks(list_ref, level, sizes, row_count):
    place = [lax.axis_index(axis) for axis in AXES]
    device = 0
    for index, size in zip(place, sizes):
        device = device * size + index
    node = 0
    for index in place[:level + 1]:
        node = node * 2 + index
    row_total = row_count * math.prod(sizes)
    shift = node * (row_total >> level + 1) - device * row_count
    at = node + (2 ** (level + 1) - 2)
    skel = list_ref.shape[1]
    lane = lax.broadcasted_iota(jnp.int32, (TILE, skel), 1)
    parts = []
    for first in range(0, skel, 16):
        part = jnp.zeros((TILE, skel), jnp.int32)
        for i in range(first, first + 16):
            part = jnp.where(lane == i, list_ref[at, i], part)
        parts.append(part)
    listed = sum(parts)[:1] + shift
    row_ids = lax.broadcasted_iota(jnp.int32, (row_count, listed.shape[1]), 0)
    return jnp.where(row_ids == listed, 1.0, 0.0).astype(jnp.bfloat16)


def taken(mark, parts):
    return sum(plain_dot(mark, part, 0, 0) for part in reversed(parts))


def pick_kernel(wanted, sizes, list_ref, *refs):
    sources, (kept_ref, sent_ref) = refs[:-2], refs[-2:]
    half = kept_ref.shape[1]
    here = lax.axis_index("core") == 0
    mark = marks(list_ref, wanted[0][0], sizes, sources[0].shape[0])
    for slot, source_ref in enumerate(sources):
        rows = taken(mark, split3(source_ref[...]))
        kept_ref[slot] = jnp.where(here, rows[:half], rows[half:])
        sent_ref[slot] = jnp.where(here, rows[half:], rows[:half])


def pick(skeleton_rows, sample, wanted, sizes):
    _, row_count, samples = sample.shape
    skel = skeleton_rows.shape[1]
    count = len(wanted)
    block = (None, row_count, samples)
    specs = [pl.BlockSpec(block, functools.partial(lambda source, step: (source, 0, 0), source)) for _, source in wanted]
    return pl.pallas_call(
        functools.partial(pick_kernel, wanted, sizes),
        out_shape=[arr(count, skel // 2, samples)] * 2,
        grid=(1,),
        in_specs=[SMEM] + specs,
        out_specs=[VMEM] * 2,
        compiler_params=BIG,
        cost_estimate=cost(10 ** 9 * count, count * row_count * samples * 4),
    )(skeleton_rows, *([sample] * count))


def project(sample_block, skeleton, samples, earlier):
    high, low = split(sample_block)
    total = dot3_halves(high, low, skeleton, 1)
    for basis, tilt in earlier:
        total = total - dot3(basis, tilt)
    return total * (1.0 / samples)


def dot3_halves(high, low, skeleton, right_dim):
    width = skeleton.shape[0]
    right_high, right_low = split(skeleton)
    both = plain_dot(high, jnp.concatenate([right_high, right_low], axis=0), 1, right_dim)
    return both[:, :width] + both[:, width:] + plain_dot(low, right_high, 1, right_dim)


def store_terms(kept_ref, sent_ref, kind, term):
    here = lax.axis_index("core") == 0
    half, width = kept_ref.shape[0], term.shape[0]
    turned = term.T
    lanes = pl.ds(kind * width, width)
    kept_ref[:, lanes] = jnp.where(here, turned[:half], turned[half:])
    sent_ref[:, lanes] = jnp.where(here, turned[half:], turned[:half])


def moments(projected, tests):
    return dot3(projected, tests, 0, 0)


def copies(pairs, sems):
    started = []
    for at, (source, target) in enumerate(pairs):
        copy = pltpu.make_async_copy(source, target, sems.at[at])
        copy.start()
        started.append(copy)
    return started


def ordered(mine_ref, other_ref):
    here = lax.axis_index("core") == 0
    low = jnp.where(here, mine_ref[...], other_ref[...])
    high = jnp.where(here, other_ref[...], mine_ref[...])
    return low, high


def ordered_pairs(parts, axis):
    first = lax.axis_index("blk") == 0
    near, far = [
        jnp.concatenate([jnp.where(first, one, two), jnp.where(first, two, one)], axis=axis)
        for one, two in ((parts[0][...], parts[1][...]), (parts[2][...], parts[3][...]))
    ]
    here = lax.axis_index("core") == 0
    return jnp.where(here, near, far), jnp.where(here, far, near)


def joined(low, high, kind):
    return jnp.concatenate([half[:, kind * WIDTH:(kind + 1) * WIDTH] for half in (low, high)], axis=0)


def whole(mine_ref, other_ref):
    return jnp.concatenate(ordered(mine_ref, other_ref), axis=0)


def whole_rows(low, high, slot):
    return jnp.concatenate([low[slot], high[slot]], axis=0)


def couple(skeleton, moment_t):
    spread = ridge(dot6(moment_t, moment_t, 0, 0))
    cross = dot3(skeleton, moment_t)
    return dot3(cross, inverse_of(spread))


def gram_of(skeleton, samples):
    return ridge(dot6(skeleton, skeleton, 1, 1) * (1.0 / samples))


def first_kernel(mine_ref, other_ref, s_hbm, t_hbm, skel_ref, p_hbm, kept_ref, sent_ref,
                 s_buf, t_buf, p_ref, sems):
    samples = mine_ref.shape[1]
    levels = t_buf.shape[0]
    running = copies([(s_hbm.at[0], s_buf)] + [(t_hbm.at[l], t_buf.at[l]) for l in range(levels)], sems)
    skeleton = whole(mine_ref, other_ref)
    skel_ref[...] = skeleton
    running[0].wait()
    projected = project(s_buf[...], skeleton, samples, [])
    p_ref[...] = projected
    leaving = copies([(p_ref, p_hbm)], sems.at[pl.ds(1 + levels, 1)])
    for level in range(levels):
        running[1 + level].wait()
        store_terms(kept_ref, sent_ref, level, moments(projected, t_buf[level]))
    leaving[0].wait()


def second_rows_kernel(*refs):
    parts, (skel0_ref, low_ref, rows_ref) = refs[:-3], refs[-3:]
    rows_low, rows_high = ordered(*parts) if len(parts) == 2 else ordered_pairs(parts, 1)
    samples = skel0_ref.shape[1]
    low_ref[...] = dot3(whole_rows(rows_low, rows_high, 0), skel0_ref[...], 1, 1) * (1.0 / samples)
    rows_ref[...] = whole_rows(rows_low, rows_high, 1)


def second_kernel(mine_ref, other_ref, ours_ref, low_ref, rows_ref, skel0_ref, p0_hbm, s_hbm, t_hbm,
                  c0_ref, back_ref, skel_ref, tilt_ref, p_hbm, kept_ref, sent_ref, s_buf, t_buf, p_ref, p0_ref, sems):
    samples = skel0_ref.shape[1]
    running = copies([(s_hbm.at[1], s_buf), (p0_hbm, p0_ref), (t_hbm.at[1], t_buf.at[0]), (t_hbm.at[2], t_buf.at[1])], sems)
    low, high = ordered(mine_ref, other_ref)
    coupling = couple(skel0_ref[...], joined(low, high, 0))
    c0_ref[...] = coupling
    back = dot3(ours_ref[...], coupling)
    back_ref[...] = back
    e01 = dot3(back, joined(low, high, 1), 1, 1)
    skeleton = rows_ref[...] - dot3(low_ref[...], e01)
    skel_ref[...] = skeleton
    tilt = dot3(e01, skeleton, 1, 1)
    tilt_ref[...] = tilt
    running[0].wait()
    running[1].wait()
    projected = project(s_buf[...], skeleton, samples, [(p0_ref[...], tilt)])
    p_ref[...] = projected
    leaving = copies([(p_ref, p_hbm)], sems.at[pl.ds(4, 1)])
    for kind in range(2):
        running[2 + kind].wait()
        store_terms(kept_ref, sent_ref, kind, moments(projected, t_buf[kind]))
    leaving[0].wait()


def third_rows_kernel(mine_ref, other_ref, back_ref, rows_mine, rows_other, last_mine, last_other,
                      skel0_ref, skel1_ref, tilt_ref, e02_ref, low_ref, rows_ref):
    share = 1.0 / skel0_ref.shape[1]
    low, high = ordered(mine_ref, other_ref)
    rows_low, rows_high = ordered(rows_mine, rows_other)
    e02 = dot3(back_ref[...], joined(low, high, 2), 1, 1)
    e02_ref[...] = e02
    low_0 = dot3(whole_rows(rows_low, rows_high, 0), skel0_ref[...], 1, 1) * share
    low_ref[...] = (
        dot3(whole_rows(rows_low, rows_high, 1), skel1_ref[...], 1, 1) - dot3(low_0, tilt_ref[...])
    ) * share
    rows_ref[...] = whole_rows(*ordered(last_mine, last_other), 0) - dot3(low_0, e02)


def third_kernel(pieces, *refs):
    parts, refs = refs[:pieces], refs[pieces:]
    (ours_ref, rows_ref, low_ref, e02_ref, skel1_ref, p0_hbm, p1_hbm, s_hbm, t_hbm,
     c1_ref, skel_ref, p_hbm, kept_ref, sent_ref, s_buf, t_buf, p_ref, p0_ref, p1_ref, sems) = refs
    samples = skel1_ref.shape[1]
    running = copies([(s_hbm.at[2], s_buf), (p0_hbm, p0_ref), (p1_hbm, p1_ref), (t_hbm.at[2], t_buf)], sems)
    low, high = ordered(*parts) if pieces == 2 else ordered_pairs(parts, 0)
    e02 = e02_ref[...]
    coupling = couple(skel1_ref[...], joined(low, high, 0))
    c1_ref[...] = coupling
    e12 = dot3(dot3(ours_ref[...], coupling), joined(low, high, 1), 1, 1)
    skeleton = rows_ref[...] - dot3(low_ref[...], e12)
    skel_ref[...] = skeleton
    tilt_0 = dot3(e02, skeleton, 1, 1)
    tilt_1 = dot3(e12, skeleton, 1, 1)
    for copy in running[:3]:
        copy.wait()
    projected = project(s_buf[...], skeleton, samples, [(p0_ref[...], tilt_0), (p1_ref[...], tilt_1)])
    p_ref[...] = projected
    leaving = copies([(p_ref, p_hbm)], sems.at[pl.ds(4, 1)])
    running[3].wait()
    store_terms(kept_ref, sent_ref, 0, moments(projected, t_buf[...]))
    leaving[0].wait()


def bases_kernel(p0_hbm, p1_hbm, p2_hbm, inverse_0, inverse_1, inverse_2, out_ref, p_buf, sems):
    running = copies([(source, p_buf.at[at]) for at, source in enumerate((p0_hbm, p1_hbm, p2_hbm))], sems)
    for level, inverse in enumerate((inverse_0, inverse_1, inverse_2)):
        running[level].wait()
        out_ref[level] = dot3(p_buf[level], inverse[...])


def last_kernel(mine_ref, other_ref, skel_ref, c0_ref, c1_ref, out_ref):
    low, high = ordered(mine_ref, other_ref)
    out_ref[0, 0] = c0_ref[...]
    out_ref[1, 0] = c1_ref[...]
    out_ref[2, 0] = couple(skel_ref[...], joined(low, high, 0))


def level_call(kernel, specs, outs, scratch, flops, operands, in_hbm=None):
    return pl.pallas_call(
        kernel,
        out_shape=outs,
        in_specs=specs,
        out_specs=[ANY if at == in_hbm else VMEM for at in range(len(outs))],
        scratch_shapes=scratch,
        compiler_params=BIG,
        cost_estimate=cost(flops, 4 * 10 ** 6),
    )(*operands)


def small_call(kernel, outs, operands):
    return pl.pallas_call(
        kernel,
        out_shape=outs,
        in_specs=[VMEM] * len(operands),
        out_specs=[VMEM] * len(outs),
        compiler_params=MIDDLE,
        cost_estimate=cost(10 ** 9, 10 ** 6),
    )(*operands)


def swap(block, axis):
    return lax.ppermute(block, axis, [(0, 1), (1, 0)])


def cross_swap(block):
    return lax.ppermute(block, ("n1", "n2"), [(0, 3), (1, 2), (2, 1), (3, 0)])


def chips_of(axes):
    return math.prod(lax.axis_size(axis) for axis in axes)


def to_chunks(stack, count):
    rows, width = stack.shape
    return stack.reshape(count, rows // count, width)


def exchange(pieces, axes):
    return lax.all_to_all(pieces, axes, 0, 0, tiled=True)


def total_over(stack, axes):
    for axis in axes:
        count = lax.axis_size(axis)
        if count == 2:
            stack = stack + swap(stack, axis)
        elif count > 2:
            stack = lax.psum(stack, axis)
    return stack


def held(first, *others):
    return lax.optimization_barrier((first,) + others)


def combine_kernel(plan, *refs):
    pieces_refs, inverse_ref, out_ref = refs[:-2], refs[-2], refs[-1]
    inverse = inverse_ref[...]
    for at, (kind, places) in enumerate(plan):
        lanes = slice(kind * WIDTH, (kind + 1) * WIDTH)
        total = sum(pieces_refs[which][place, :, lanes] for which, place in places)
        out_ref[at] = dot3(total, inverse)


def combine(pieces, inverse, plan):
    rows = pieces[0].shape[1]
    return pl.pallas_call(
        functools.partial(combine_kernel, plan),
        out_shape=arr(len(plan), rows, WIDTH),
        in_specs=[VMEM] * (len(pieces) + 1),
        out_specs=VMEM,
        compiler_params=SMALL,
        cost_estimate=cost(10 ** 8, 10 ** 6),
    )(*pieces, inverse)


def add_kernel(one_ref, two_ref, out_ref):
    out_ref[...] = one_ref[...] + two_ref[...]


def add_blocks(one, two):
    return pl.pallas_call(
        add_kernel,
        out_shape=arr(*one.shape),
        in_specs=[VMEM] * 2,
        out_specs=VMEM,
        compiler_params=SMALL,
        cost_estimate=cost(10 ** 6, 10 ** 6),
    )(one, two)


def add_split_kernel(axis, one_ref, two_ref, kept_ref, sent_ref):
    half = kept_ref.shape[-2]
    first = lax.axis_index(axis) == 0
    for at in range(kept_ref.shape[0]):
        total = one_ref[at] + two_ref[at]
        kept_ref[at] = jnp.where(first, total[:half], total[half:])
        sent_ref[at] = jnp.where(first, total[half:], total[:half])


def add_split(one, two, axis):
    count, rows, width = one.shape
    return pl.pallas_call(
        functools.partial(add_split_kernel, axis),
        out_shape=[arr(count, rows // 2, width)] * 2,
        in_specs=[VMEM] * 2,
        out_specs=[VMEM] * 2,
        compiler_params=SMALL,
        cost_estimate=cost(10 ** 6, 10 ** 6),
    )(one, two)


def fan_kernel(plan, *refs):
    for place, wanted in enumerate(plan):
        for kind, terms in enumerate(wanted):
            total = sum(refs[which][at] for which, at in terms)
            refs[-1][place, :, kind * WIDTH:(kind + 1) * WIDTH] = total


def fan_out(sums, plan):
    rows = sums[0].shape[1]
    return pl.pallas_call(
        functools.partial(fan_kernel, plan),
        out_shape=arr(len(plan), rows, WIDTH * len(plan[0])),
        in_specs=[VMEM] * len(sums),
        out_specs=VMEM,
        compiler_params=SMALL,
        cost_estimate=cost(10 ** 6, 10 ** 6),
    )(*sums)


def local(sample, probes, skeleton_rows):
    levels, row_count, samples = sample.shape
    skel = skeleton_rows.shape[1]
    sizes = [lax.axis_size(axis) for axis in AXES]
    s_buf = pltpu.VMEM((row_count, samples), jnp.float32)
    p_buf = pltpu.VMEM((row_count, skel), jnp.float32)
    square, wide, tall = arr(skel, skel), arr(skel, samples), arr(row_count, skel)

    def t_buf(count):
        return pltpu.VMEM((count, row_count, samples), jnp.float32)

    def sems(count):
        return pltpu.SemaphoreType.DMA((count,))

    def outgoing(kinds):
        return [arr(samples // 2, kinds * skel)] * 2

    chips = [("n1", "n2", "mid", "blk"), ("n2", "mid", "blk"), ("mid", "blk")]
    kept, sent = pick(skeleton_rows, sample, ((0, 0),), sizes)
    half = kept[0] + swap(sent[0], "core")
    half, lists = held(half, skeleton_rows)
    half = total_over(half, ("mid", "blk"))
    rest_kept, rest_sent = pick(lists, sample, ((1, 0), (1, 1)), sizes)
    half = half + swap(half, "n2") + swap(half, "n1") + cross_swap(half)
    pairs = chips_of(chips[2]) == 2
    if pairs:
        rest, moved = add_split(rest_kept, swap(rest_sent, "core"), "blk")
        half_other, rest_kept, rest = held(swap(half, "core"), rest_kept, rest)
        moved = swap(moved, "blk")
    else:
        rest = rest_kept + swap(rest_sent, "core")
        half_other, rest = held(swap(half, "core"), rest)
        moved = total_over(rest, ("mid", "blk"))

    skeleton_0, projected_0, kept, sent = level_call(
        first_kernel,
        [VMEM] * 2 + [ANY, ANY],
        [wide, tall] + outgoing(levels),
        [s_buf, t_buf(levels), p_buf, sems(2 + levels)],
        3 * 10 ** 9,
        (half, half_other, sample, probes),
        in_hbm=1,
    )
    sent, moved = held(sent, moved)
    received, skeleton_in = held(swap(sent, "core"), skeleton_0)
    inverse_0 = invert(skeleton_in)
    terms = add_blocks(kept, received)
    rows_one = total_over(rest + moved if pairs else moved, ("n2",))
    pieces = exchange(to_chunks(terms, chips_of(chips[0])), chips[0])
    pieces, inverse_0 = held(pieces, inverse_0)
    inner = chips_of(chips[2])
    places = [(one, two) for one in range(2) for two in range(2) for _ in range(inner)]
    every = range(len(places))
    plan = [(0, [(0, at) for at in every])]
    plan += [(1, [(0, at) for at in every if places[at][0] == one]) for one in range(2)]
    plan += [(2, [(0, at) for at in every if places[at][1] == two]) for two in range(2)]
    sums = swap(combine([pieces], inverse_0, plan), "n0")
    sums, lists, rows_one = held(sums, skeleton_rows, rows_one)
    rest_kept, rest_sent = pick(lists, sample, ((2, 0), (2, 1), (2, 2)), sizes)
    mine = exchange(fan_out([sums], [[[(0, at)] for at in (0, 2 - one, 4 - two)] for one, two in places]), chips[0])
    mine = mine.reshape(samples // 2, levels * skel)
    row_parts = (rows_one, swap(rows_one, "blk")) if pairs else (rows_one,)
    mine, rest_kept, rest_sent, *row_parts = held(mine, rest_kept, rest_sent, *row_parts)
    other = swap(mine, "core")
    rest_sent = swap(rest_sent, "core")
    rest, last = rest_kept[:2] + rest_sent[:2], rest_kept[2:] + rest_sent[2:]
    mine, other, rest = held(mine, other, rest)
    rest = total_over(rest, ("mid", "blk"))

    row_parts += [swap(part, "core") for part in row_parts]
    low, rows_one = small_call(second_rows_kernel, [square, wide], (*row_parts, skeleton_0))
    coupling_0, back, skeleton_1, tilt, projected_1, kept, sent = level_call(
        second_kernel,
        [VMEM] * 6 + [ANY] * 3,
        [square, square, wide, square, tall] + outgoing(2),
        [s_buf, t_buf(2), p_buf, p_buf, sems(5)],
        8 * 10 ** 9,
        (mine, other, inverse_0, low, rows_one, skeleton_0, projected_0, sample, probes),
        in_hbm=4,
    )
    sent, rows_two = held(sent, rest)
    rows_two_other = swap(rows_two, "core")
    before = (mine, other)
    received, skeleton_in = held(swap(sent, "core"), skeleton_1)
    inverse_1 = invert(skeleton_in)
    if pairs:
        kept, sent = [part[0] for part in add_split(kept[None], received[None], "blk")]
        arrived = swap(sent, "blk")
        arrived, inverse_1 = held(arrived, inverse_1)
        sums = combine([kept[None], arrived[None]], inverse_1, [(0, [(0, 0), (1, 0)]), (1, [(0, 0), (1, 0)])])
        sums, last = held(sums, last)
        far, beside = cross_swap(sums), swap(sums[:1], "n1")
        mine = fan_out([far, beside], [[[(0, 0), (1, 0)], [(0, 1)]]])[0]
        last = total_over(last, ("blk",))
        mine, rows_two, last = held(mine, rows_two, last)
        beside = swap(mine, "blk")
        parts = (mine, beside, swap(mine, "core"), swap(beside, "core"))
    else:
        last = total_over(last, ("mid", "blk"))
        pieces = exchange(to_chunks(kept + received, chips_of(chips[1])), chips[1])
        pieces, inverse_1 = held(pieces, inverse_1)
        places = [two for two in range(2) for _ in range(inner)]
        every = range(len(places))
        plan = [(0, [(0, at) for at in every])]
        plan += [(1, [(0, at) for at in every if places[at] == two]) for two in range(2)]
        sums = swap(combine([pieces], inverse_1, plan), "n1")
        mine = exchange(fan_out([sums], [[[(0, at)] for at in (0, 2 - two)] for two in places]), chips[1])
        mine = mine.reshape(samples // 2, 2 * skel)
        parts = (mine, swap(mine, "core"))

    e02, low, rows_two = small_call(
        third_rows_kernel,
        [wide, square, wide],
        before + (back, rows_two, rows_two_other, last, swap(last, "core"), skeleton_0, skeleton_1, tilt),
    )
    coupling_1, skeleton_2, projected_2, kept, sent = level_call(
        functools.partial(third_kernel, len(parts)),
        [VMEM] * (len(parts) + 5) + [ANY] * 4,
        [square, wide, tall] + outgoing(1),
        [s_buf, pltpu.VMEM((row_count, samples), jnp.float32), p_buf, p_buf, p_buf, sems(5)],
        8 * 10 ** 9,
        parts + (inverse_1, rows_two, low, e02, skeleton_1, projected_0, projected_1, sample, probes),
        in_hbm=2,
    )
    received, skeleton_in = held(swap(sent, "core"), skeleton_2)
    inverse_2 = invert(skeleton_in)
    terms = kept + received
    if pairs:
        arrived = swap(terms, "blk")
        arrived, inverse_2 = held(arrived, inverse_2)
        mine = combine([terms[None], arrived[None]], inverse_2, [(0, [(0, 0), (1, 0)])])
    else:
        terms, inverse_2 = held(total_over(terms, chips[2]), inverse_2)
        mine = combine([terms[None]], inverse_2, [(0, [(0, 0)])])
    mine = swap(mine[0], "n2")
    bases, = level_call(
        bases_kernel, [ANY] * 3 + [VMEM] * 3, [arr(levels, row_count, skel)],
        [pltpu.VMEM((levels, row_count, skel), jnp.float32), sems(levels)], 4 * 10 ** 9,
        (projected_0, projected_1, projected_2, inverse_0, inverse_1, inverse_2),
    )
    mine, bases = held(mine, bases)
    other = swap(mine, "core")
    couplings, = level_call(
        last_kernel, [VMEM] * 5, [arr(levels, 1, skel, skel)], [], 5 * 10 ** 9,
        (mine, other, skeleton_2, coupling_0, coupling_1),
    )
    return bases, couplings


def solution(mesh):
    leaves, blocks = mesh.shape["leaf"], mesh.shape["blk"]
    fine = jax.sharding.Mesh(mesh.devices.reshape(2, 2, 2, leaves // 16, 2, blocks), AXES)
    rows = P(None, AXES, None)
    return jax.shard_map(
        local,
        mesh=fine,
        in_specs=(rows, rows, P()),
        out_specs=(rows, P(None, AXES[:-1], None, None)),
        check_vma=False,
    )
```
